256 devices in a mesh: slab: 8 (over x, core), tile: 32 (over z, y).
Axes of the slice: x: 4, y: 4, z: 8, core: 2. Of those that a mesh axis runs over, the one named last changes fastest.
Arguments:
- positions: float32 [3, 16384, 128], P(None, ('slab', 'tile')), may hold values from 0 to 1.6
- velocities: float32 [3, 16384, 128], P(None, ('slab', 'tile')), may hold values from -6 to 6
- masses: float32 [16384, 128], P(('slab', 'tile')), may hold values from 0.01 to 0.1
- wall_areas: float32 [16384, 128], P(('slab', 'tile')), may hold values from 0.02 to 0.2
- normals: float32 [3, 16384, 128], P(None, ('slab', 'tile')), may hold values from -1 to 1, as said below
- wall_flags: int32 [16384], P(('slab', 'tile')), may hold values 0 or 1
- counts: int32 [16384], P(('slab', 'tile')), may hold values from 1 to 128, as said below
- send_list: int32 [256, 32, 4], P(('slab', 'tile')), may hold values from 0 to 63, as said below
- local_pairs: int32 [16384, 2], P(('slab', 'tile')), may hold values from 0 to 63, as said below
- remote_pairs: int32 [40960, 2], P(('slab', 'tile')), may hold values from 0 to 223, as said below
- remote_live: int32 [256], P(('slab', 'tile')), may hold values from 40 to 160, as said below
Outputs:
- density: float32 [16384, 128], P(('slab', 'tile'))
- acceleration: float32 [3, 16384, 128], P(None, ('slab', 'tile'))
The draws below stay inside these ranges and needn't reach their ends.
Inputs may be any that keep to these rules, and one draw needn't show every extreme that they name: `counts`: every device has one block holding 128 particles; slots at or after a block's count are empty. `normals`: every component is 0.2 or more in magnitude. `send_list`: own block numbers of the sending device, distinct within the 4 entries for one receiving device. `local_pairs`: the two blocks of a row differ. `remote_pairs`: column 0 is an own block number below 64; column 1 is below 16 only for devices not in the first slab, between 80 and 95 only for devices not in the last slab, otherwise 64 + 2 * 16 or more with p never the device's own tile. `remote_live`: some device has all 160 rows live.
All inputs are finite; a program needn't handle non-finite values. No bound on the sum of `wall_flags` on one device may be relied on, other than what follows from the above.
Results may differ from the reference program's by a relative error of at most 0.00002.
Values sent between devices are 32-bit elements; how exact they have to be, the bound alone decides.
No kernel may reach another device: no remote copies, remote signals or barrier semaphores. Data moves between devices by JAX's collectives and lax.ppermute only.
A program may use at most 64 MiB of HBM per device.

```python
import math
import jax
import jax.numpy as jnp
from jax import lax

NB = 64
SLOT = 128
SLOTS = 4
HB = 16
P_LOC = 64
P_REM = 160
DEVS = 256
BLOCKS = 16384
N_SLAB = 8
N_TILE = 32


def pick_slots(key):
    return jax.random.permutation(key, NB)[:SLOTS]


def shuffle_row(key):
    return jax.random.permutation(key, P_REM)


def draw_counts(key, part):
    key = jax.random.fold_in(key, 11)
    first_key, second_key = jax.random.split(key)
    filled = jax.random.randint(first_key, (DEVS, NB), 1, SLOT + 1)
    chosen = jax.random.randint(second_key, (DEVS, 1), 0, NB)
    filled = jnp.where(jnp.arange(NB)[None, :] == chosen, SLOT, filled)
    return filled.reshape(BLOCKS).astype(jnp.int32)


def draw_normals(key, part):
    key = jax.random.fold_in(key, 12)
    first_key, second_key = jax.random.split(key)
    shape = (3, BLOCKS, SLOT)
    length = jax.random.uniform(first_key, shape, jnp.float32, 0.2, 1.0)
    signed = (jax.random.randint(second_key, shape, 0, 2) * 2 - 1).astype(jnp.float32)
    return (length * signed).astype(jnp.float32)


def draw_send_list(key, part):
    key = jax.random.fold_in(key, 13)
    keys = jax.random.split(key, DEVS * N_TILE)
    picks = jax.vmap(pick_slots)(keys)
    return picks.reshape(DEVS, N_TILE, SLOTS).astype(jnp.int32)


def draw_local_pairs(key, part):
    key = jax.random.fold_in(key, 14)
    first_key, second_key = jax.random.split(key)
    first = jax.random.randint(first_key, (DEVS * P_LOC,), 0, NB)
    stride = jax.random.randint(second_key, (DEVS * P_LOC,), 1, NB)
    second = (first + stride) % NB
    return jnp.stack([first, second], axis=1).astype(jnp.int32)


def draw_remote_pairs(key, part):
    key = jax.random.fold_in(key, 15)
    keys = jax.random.split(key, 4)
    device = jnp.arange(DEVS)[:, None]
    slab_of = device // N_TILE
    tile_of = device % N_TILE
    place = jnp.arange(P_REM)[None, :]
    other = (tile_of + jax.random.randint(keys[0], (DEVS, P_REM), 1, N_TILE)) % N_TILE
    fallback = NB + 2 * HB + other * SLOTS + jax.random.randint(keys[1], (DEVS, P_REM), 0, SLOTS)
    rest = place - 2 * HB
    natural = jnp.where(place < 2 * HB, jnp.where(place < HB, place, NB + place), NB + 2 * HB + rest)
    valid = jnp.where(place < HB, slab_of > 0, jnp.where(place < 2 * HB, slab_of < N_SLAB - 1, rest // SLOTS != tile_of))
    target = jnp.where(valid, natural, fallback)
    order = jax.vmap(shuffle_row)(jax.random.split(keys[2], DEVS))
    target = jnp.take_along_axis(target, order, axis=1)
    first = jax.random.randint(keys[3], (DEVS, P_REM), 0, NB)
    return jnp.stack([first, target], axis=-1).reshape(DEVS * P_REM, 2).astype(jnp.int32)


def draw_remote_live(key, part):
    key = jax.random.fold_in(key, 16)
    first_key, second_key = jax.random.split(key)
    live = jax.random.randint(first_key, (DEVS,), P_REM // 4, P_REM + 1)
    busiest = jax.random.randint(second_key, (1,), 0, DEVS)
    live = jnp.where(jnp.arange(DEVS) == busiest, P_REM, live)
    return live.astype(jnp.int32)


def set_ends(drawn, rng, smallest, high):
    spot = [jax.random.randint(jax.random.fold_in(rng, axis), (), 0, length) for axis, length in enumerate(drawn.shape)]
    longest = drawn.shape.index(max(drawn.shape))
    neighbour = spot[:longest] + [(spot[longest] + 1) % drawn.shape[longest]] + spot[longest + 1:]
    return drawn.at[tuple(spot)].set(smallest).at[tuple(neighbour)].set(high)


def level_of(rng, shape, pieces, least, largest):
    gain = 1.0
    for dim, blocks in pieces:
        steps = jax.random.uniform(jax.random.fold_in(jax.random.fold_in(rng, 6), dim), (blocks,), jnp.float32, least / len(pieces), largest / len(pieces))
        gain = gain * jnp.repeat(jnp.exp(steps), shape[dim] // blocks).reshape((-1,) + (1,) * (len(shape) - 1 - dim))
    return gain


def normal_values(key, dims, scale, limit, shards=(), kind=jnp.bfloat16):
    array = scale * jax.random.normal(key, dims, jnp.float32)
    if shards:
        array = array * level_of(key, dims, shards, -0.22, 0.18)
    return jnp.clip(array, -limit, limit).astype(kind)


def setup_inputs(seed: int = 0) -> dict:
    streams_of = jax.random.split(jax.random.key(seed), 12)
    positions = jnp.clip(1.6 * jax.random.uniform(streams_of[0], (3, BLOCKS, SLOT), jnp.float32) ** level_of(streams_of[0], (3, BLOCKS, SLOT), ((1, 256),), -0.2, 0.2), 0.0, 1.6)
    velocities = normal_values(streams_of[1], (3, BLOCKS, SLOT), 1.0, 6.0, ((1, 256),), jnp.float32)
    masses = jnp.clip(jnp.exp(math.log(0.1) - 2.3025851 * jax.random.uniform(streams_of[2], (BLOCKS, SLOT), jnp.float32) ** level_of(streams_of[2], (BLOCKS, SLOT), ((0, 256),), -0.2, 0.2)), 0.01, 0.1)
    wall_areas = jnp.clip(jnp.exp(math.log(0.2) - 2.3025851 * jax.random.uniform(streams_of[3], (BLOCKS, SLOT), jnp.float32) ** level_of(streams_of[3], (BLOCKS, SLOT), ((0, 256),), -0.2, 0.2)), 0.02, 0.2)
    normals = draw_normals(jax.random.fold_in(streams_of[11], 71), 0)
    wall_flags = set_ends((jax.random.randint(streams_of[5], (BLOCKS,), 0, 4) < 1).astype(jnp.int32), jax.random.fold_in(streams_of[5], 1), 0, 1)
    counts = draw_counts(jax.random.fold_in(streams_of[11], 71), 0)
    send_list = draw_send_list(jax.random.fold_in(streams_of[11], 71), 0)
    local_pairs = draw_local_pairs(jax.random.fold_in(streams_of[11], 71), 0)
    remote_pairs = draw_remote_pairs(jax.random.fold_in(streams_of[11], 71), 0)
    remote_live = draw_remote_live(jax.random.fold_in(streams_of[11], 71), 0)
    return dict(positions=positions, velocities=velocities, masses=masses, wall_areas=wall_areas, normals=normals, wall_flags=wall_flags, counts=counts, send_list=send_list, local_pairs=local_pairs, remote_pairs=remote_pairs, remote_live=remote_live)


kernel_norm = 21.0 / (16.0 * math.pi)
rest_density = 1.0
sound_sq = 1.0
viscosity = 0.1
wall_push = 1.0
softening = 0.01
pair_group = 8

def kernel_terms(dist_sq):
    distance = jnp.sqrt(dist_sq)
    remain = jnp.maximum(1.0 - 0.5 * distance, 0.0)
    cubed = remain * remain * remain
    return (kernel_norm * cubed * remain * (2.0 * distance + 1.0), -5.0 * kernel_norm * cubed)

def separation(first_pos, second_pos):
    offset = first_pos[:, :, :, None] - second_pos[:, :, None, :]
    return (offset, lax.optimization_barrier(jnp.sum(offset * offset, axis=1)))

def density_pair(side_first, side_second):
    offset, dist_sq = separation(side_first[:, 0:3], side_second[:, 0:3])
    kernel_w, slope = kernel_terms(dist_sq)
    to_first = lax.optimization_barrier(jnp.sum(kernel_w * side_second[:, 3][:, None, :], axis=2))
    to_second = lax.optimization_barrier(jnp.sum(kernel_w * side_first[:, 3][:, :, None], axis=1))
    return (to_first[:, None], to_second[:, None])

def force_pair(side_first, side_second):
    offset, dist_sq = separation(side_first[:, 0:3], side_second[:, 0:3])
    kernel_w, slope = kernel_terms(dist_sq)
    press_sum = (side_first[:, 12][:, :, None] + side_second[:, 12][:, None, :]) * slope
    damping = 2.0 * viscosity * slope * dist_sq / (dist_sq + softening)
    damping = damping / (side_first[:, 11][:, :, None] * side_second[:, 11][:, None, :])
    vel_diff = side_first[:, 3:6][:, :, :, None] - side_second[:, 3:6][:, :, None, :]
    pulling = damping[:, None] * vel_diff - press_sum[:, None] * offset
    wall_second = side_second[:, 7][:, None, :] * side_second[:, 8:11]
    wall_first = side_first[:, 7][:, None, :] * side_first[:, 8:11]
    to_first = lax.optimization_barrier(jnp.sum(pulling * side_second[:, 6][:, None, None, :], axis=3))
    to_first = to_first + wall_push * lax.optimization_barrier(jnp.sum(kernel_w[:, None] * wall_second[:, :, None, :], axis=3))
    to_second = -lax.optimization_barrier(jnp.sum(pulling * side_first[:, 6][:, None, :, None], axis=2))
    to_second = to_second + wall_push * lax.optimization_barrier(jnp.sum(kernel_w[:, None] * wall_first[:, :, :, None], axis=2))
    return (to_first, to_second)

def unit_normals(normals):
    as_float = normals.astype(jnp.float32)
    return as_float / jnp.sqrt(lax.optimization_barrier(jnp.sum(as_float * as_float, axis=0, keepdims=True)))

def particle_masks(counts, wall_flags, slot_count):
    alive = (jnp.arange(slot_count, dtype=jnp.int32)[None, :] < counts[:, None]).astype(jnp.float32)
    walled = alive * wall_flags.astype(jnp.float32)[:, None]
    return (alive - walled, walled)

def self_terms(fields, summed, pair_fn):
    steps = fields.shape[1] // pair_group
    starts = jnp.arange(steps * pair_group, dtype=jnp.int32).reshape(steps, pair_group)

    def advance(carry, first_idx):
        side = jnp.moveaxis(jnp.take(fields, first_idx, axis=1), 1, 0)
        to_first, unused = pair_fn(side, side)
        return (carry.at[:, first_idx].add(jnp.moveaxis(to_first, 0, 1)), None)
    summed, unused = lax.scan(advance, summed, starts)
    return summed

def pair_terms(fields, summed, first, second, weights, pair_fn):
    steps = first.shape[0] // pair_group

    def advance(carry, items):
        first_idx, second_idx, weight = items
        side_first = jnp.moveaxis(jnp.take(fields, first_idx, axis=1), 1, 0)
        side_second = jnp.moveaxis(jnp.take(fields, second_idx, axis=1), 1, 0)
        to_first, to_second = pair_fn(side_first, side_second)
        carry = carry.at[:, first_idx].add(jnp.moveaxis(to_first * weight[:, None, None], 0, 1))
        carry = carry.at[:, second_idx].add(jnp.moveaxis(to_second * weight[:, None, None], 0, 1))
        return (carry, None)
    summed, unused = lax.scan(advance, summed, (first.reshape(steps, pair_group), second.reshape(steps, pair_group), weights.reshape(steps, pair_group)))
    return summed

def global_pairs(send_list, local_pairs, remote_pairs, remote_live):
    local_owner = jnp.repeat(jnp.arange(DEVS, dtype=jnp.int32), P_LOC)
    remote_owner = jnp.repeat(jnp.arange(DEVS, dtype=jnp.int32), P_REM)
    place = jnp.tile(jnp.arange(P_REM, dtype=jnp.int32), DEVS)
    target = remote_pairs[:, 1]
    slab_of = remote_owner // N_TILE
    tile_of = remote_owner % N_TILE
    lower = (remote_owner - N_TILE) * NB + NB - HB + target
    upper = (remote_owner + N_TILE) * NB + target - HB - NB
    slot_no = jnp.clip(target - NB - 2 * HB, 0, N_TILE * SLOTS - 1)
    source = slab_of * N_TILE + slot_no // SLOTS
    picked = send_list[source, tile_of, slot_no % SLOTS]
    across = source * NB + picked
    remote_second = jnp.where(target < HB, lower, jnp.where(target < NB + 2 * HB, upper, across))
    first = jnp.concatenate([local_owner * NB + local_pairs[:, 0], remote_owner * NB + remote_pairs[:, 0]])
    second = jnp.concatenate([local_owner * NB + local_pairs[:, 1], remote_second])
    live = (place < remote_live[remote_owner]).astype(jnp.float32)
    weights = jnp.concatenate([jnp.ones((DEVS * P_LOC,), jnp.float32), live])
    return (first.astype(jnp.int32), second.astype(jnp.int32), weights)

def reference(positions, velocities, masses, wall_areas, normals, wall_flags, counts, send_list, local_pairs, remote_pairs, remote_live):
    fluid, walled = particle_masks(counts, wall_flags, SLOT)
    fluid_mass = fluid * masses
    wall_weight = walled * wall_areas
    dens_weight = fluid_mass + rest_density * wall_weight
    first, second, weights = global_pairs(send_list, local_pairs, remote_pairs, remote_live)
    dens_fields = jnp.concatenate([positions, dens_weight[None]], axis=0)
    summed = self_terms(dens_fields, jnp.zeros((1, BLOCKS, SLOT), jnp.float32), density_pair)
    summed = pair_terms(dens_fields, summed, first, second, weights, density_pair)
    density = fluid * summed[0]
    rho = density + (1.0 - fluid) * rest_density
    pressure = fluid * sound_sq * (rho - rest_density) / (rho * rho)
    force_fields = jnp.concatenate([positions, velocities, fluid_mass[None], wall_weight[None], unit_normals(normals), rho[None], pressure[None]], axis=0)
    pushed = self_terms(force_fields, jnp.zeros((3, BLOCKS, SLOT), jnp.float32), force_pair)
    pushed = pair_terms(force_fields, pushed, first, second, weights, force_pair)
    return (density, fluid[None] * pushed)
```

```python
import functools
import math

import jax
import jax.numpy as jnp
from jax import lax
from jax.experimental import pallas as pl
from jax.experimental.pallas import tpu as pltpu
from jax.sharding import PartitionSpec as P

kernel_norm = 21.0 / (16.0 * math.pi)
softening = 0.01
tiny = 1e-30
rows_item = 32
groups = rows_item // 8
batch = 4
lanes = 128
vmem = pltpu.VMEM
smem = pltpu.SMEM


def spec(space):
    return pl.BlockSpec(memory_space=space)


def params(mib):
    return pltpu.CompilerParams(vmem_limit_bytes=mib * 1024 * 1024)


def reciprocal(x):
    return 1.0 / x


def pack_kernel(
    blocks, faces, counts, send, pos, vel, mass, area, normal, flags_col, counts_col, table, picked, head, tail
):
    slot = lax.broadcasted_iota(jnp.int32, (blocks, lanes), 1)
    alive = slot < counts_col[...]
    wall = flags_col[...] > 0
    nx, ny, nz = normal[0], normal[1], normal[2]
    length = jnp.sqrt(nx * nx + ny * ny + nz * nz)
    weight = jnp.where(alive, jnp.where(wall, area[...], mass[...]), 0.0)
    wall_scale = weight / length
    parts = (nx, ny, nz)
    for c in range(3):
        table[pl.ds(c, blocks, stride=8), :] = 0.5 * pos[c]
        table[pl.ds(3 + c, blocks, stride=8), :] = jnp.where(wall, wall_scale * parts[c], vel[c])
    table[pl.ds(6, blocks, stride=8), :] = weight
    table[pl.ds(7, blocks, stride=8), :] = jnp.where(wall, 1.0, 0.0) + jnp.zeros((blocks, lanes), jnp.float32)
    head[...] = table[0 : faces * 8, :]
    tail[...] = table[(blocks - faces) * 8 : blocks * 8, :]

    def pick(k, carry):
        source = pl.multiple_of(send[k] * 8, 8)
        picked[pl.ds(pl.multiple_of(k * 8, 8), 8), :] = table[pl.ds(source, 8), :]
        return carry

    lax.fori_loop(0, send.shape[0], pick, 0, unroll=8)


def make_columns(blocks, table, columns):
    def some(g, carry):
        turned = table[pl.ds(pl.multiple_of(g * lanes, lanes), lanes), :].T
        for k in range(16):
            moved = turned if k == 0 else pltpu.roll(turned, lanes - 8 * k, 1)
            columns[g * 16 + k] = moved
        return carry

    lax.fori_loop(0, blocks // 16, some, 0)
    columns[blocks] = jnp.zeros((lanes, lanes), jnp.float32)


def put_items(items, at, first, second):
    code = first | (second << 8)
    for k in range(lanes // rows_item):
        items[at + k] = code | (k << 16)


def close_items(items, count, blocks):
    for k in range(batch):
        items[count + k] = jnp.int32(blocks)


def decode(code):
    first = code & 255
    second = (code >> 8) & 255
    row = pl.multiple_of((code >> 16) * rows_item, rows_item)
    return first, second, row


def wide(row):
    return jnp.broadcast_to(row, (8, lanes))


def close_u(cols, rows):
    dx = cols[:, 0:1] - rows[0]
    dy = cols[:, 1:2] - rows[1]
    dz = cols[:, 2:3] - rows[2]
    square = dx * dx + dy * dy + dz * dz
    safe = jnp.maximum(square, tiny)
    q = safe * lax.rsqrt(safe)
    u = jnp.maximum(1.0 - q, 0.0)
    return dx, dy, dz, square, u


def kernel_shape(u):
    u2 = u * u
    return (u2 * u2) * (5.0 - 4.0 * u)


def run_items(items, count, body):
    def step(it, carry):
        body([decode(items[it * batch + k]) for k in range(batch)])
        return carry

    lax.fori_loop(0, (count + batch - 1) // batch, step, 0)


def lane_numbers():
    return lax.broadcasted_iota(jnp.int32, (8, lanes), 1)


def merge_lanes(values, first, lane):
    base = (first & 31) * 4
    total = jnp.zeros((8, lanes), jnp.float32)
    for c, value in enumerate(values):
        total = jnp.where(lane == base + c, value, total)
    return total


def add_first(acc_first, first, row, merged):
    slab = first >> 5
    for g in range(groups):
        acc_first[slab, pl.ds(row + 8 * g, 8), :] += merged[g]


def add_second(acc_second, second, values):
    for c, value in enumerate(values):
        at = pl.multiple_of(second * 32 + 8 * c, 8)
        acc_second[pl.ds(at, 8), :] += value


def density_body(columns, source, acc_first, acc_second, to_first, to_second, decoded):
    lane = lane_numbers()
    outs = []
    for first, second, row in decoded:
        base = pl.multiple_of(second * 8, 8)
        rows = [wide(source[pl.ds(base + c, 1), :]) for c in range(3)]
        given = []
        if to_first:
            given = [wide(source[pl.ds(base + 6, 1), :])]
            if to_first == 4:
                given += [wide(source[pl.ds(base + 3 + c, 1), :]) for c in range(3)]
        merged = []
        sums = None
        for g in range(groups):
            cols = columns[first, pl.ds(row + 8 * g, 8), :]
            w = kernel_shape(close_u(cols, rows)[4])
            if to_first:
                values = [jnp.sum(w * other, axis=1, keepdims=True) for other in given]
                merged.append(merge_lanes(values, first, lane))
            if to_second:
                back = [w * cols[:, 6:7]]
                if to_second == 4:
                    back += [w * cols[:, 3 + c : 4 + c] for c in range(3)]
                sums = back if sums is None else [s + b for s, b in zip(sums, back)]
        outs.append((merged, sums))
    for (first, second, row), (merged, sums) in zip(decoded, outs):
        if to_first:
            add_first(acc_first, first, row, merged)
        if to_second:
            add_second(acc_second, second, sums)


def clear(ref, pieces):
    size = ref.shape[0] // pieces

    def some(k, carry):
        at = pl.multiple_of(k * size, size)
        ref[pl.ds(at, size)] = jnp.zeros((size,) + tuple(ref.shape[1:]), jnp.float32)
        return carry

    lax.fori_loop(0, pieces, some, 0)


def sublane_sums(acc_second, number, c):
    total = acc_second[pl.ds(8 * c, number, stride=32), :]
    for k in range(1, 8):
        total = total + acc_second[pl.ds(8 * c + k, number, stride=32), :]
    return total


def first_rows(acc_first, turned, blocks):
    for s in range(blocks // 32):
        turned[s * lanes : (s + 1) * lanes, :] = acc_first[s].T


def own_density_kernel(
    blocks, counts, flags, pairs, table, own, both_items, self_items, columns, acc_first, acc_second, turned, wall_items
):
    make_columns(blocks, table, columns)
    clear(acc_first, 1)
    clear(acc_second, 16)

    def self_step(b, n):
        put_items(self_items, n, b, b)
        return n + jnp.where(flags[b] > 0, 0, (counts[b] + rows_item - 1) // rows_item)

    n_self = lax.fori_loop(0, blocks, self_step, jnp.int32(0), unroll=4)
    close_items(self_items, n_self, blocks)

    def pair_step(p, carry):
        n_both, n_wall = carry
        a = pairs[2 * p]
        b = pairs[2 * p + 1]
        kinds = flags[a] + flags[b]
        swap = jnp.where(kinds == 1, flags[b] > 0, counts[b] < counts[a])
        first = jnp.where(swap, b, a)
        second = jnp.where(swap, a, b)
        number = (counts[first] + rows_item - 1) // rows_item
        put_items(both_items, n_both, first, second)
        put_items(wall_items, n_wall, first, second)
        return (n_both + jnp.where(kinds == 0, number, 0), n_wall + jnp.where(kinds == 1, number, 0))

    n_both, n_wall = lax.fori_loop(
        0, pairs.shape[0] // 2, pair_step, (jnp.int32(0), jnp.int32(0)), unroll=4
    )
    close_items(both_items, n_both, blocks)
    close_items(wall_items, n_wall, blocks)
    both_items[both_items.shape[0] - 1] = n_both
    self_items[self_items.shape[0] - 1] = n_self
    density = functools.partial(density_body, columns, table, acc_first, acc_second)
    run_items(self_items, n_self, functools.partial(density, 0, 1))
    run_items(both_items, n_both, functools.partial(density, 1, 1))
    run_items(wall_items, n_wall, functools.partial(density, 0, 4))
    first_rows(acc_first, turned, blocks)
    for c in range(4):
        own[c] = turned[pl.ds(c, blocks, stride=4), :] + sublane_sums(acc_second, blocks, c)


def far_density_kernel(
    blocks,
    faces,
    counts,
    flags,
    live,
    pairs,
    table,
    low,
    high,
    far,
    own,
    back,
    push,
    both_items,
    columns,
    acc_first,
    acc_second,
    turned,
    source,
    wall_rows,
    wall_flag,
    first_items,
    second_items,
    sem,
):
    others = source.shape[0] // 8
    source[0 : faces * 8, :] = low[...]
    source[faces * 8 : 2 * faces * 8, :] = high[...]
    source[2 * faces * 8 :, :] = far[...]
    wall_rows[...] = source[pl.ds(7, others, stride=8), :]
    copy = pltpu.make_async_copy(wall_rows, wall_flag, sem)
    copy.start()
    make_columns(blocks, table, columns)
    clear(acc_first, 1)
    clear(acc_second, 16)
    copy.wait()

    def pair_step(p, carry):
        n_both, n_first, n_second = carry
        a = pairs[2 * p]
        j = pairs[2 * p + 1]
        b = jnp.where(j < blocks, j, j - blocks)
        wall_a = flags[a]
        wall_b = jnp.where(wall_flag[b, 0] > 0.5, 1, 0)
        number = jnp.where(p < live[0], (counts[a] + rows_item - 1) // rows_item, 0)
        put_items(both_items, n_both, a, b)
        put_items(first_items, n_first, a, b)
        put_items(second_items, n_second, a, b)
        return (
            n_both + number * (1 - wall_a) * (1 - wall_b),
            n_first + number * (1 - wall_a) * wall_b,
            n_second + number * wall_a * (1 - wall_b),
        )

    zero = jnp.int32(0)
    n_both, n_first, n_second = lax.fori_loop(
        0, pairs.shape[0] // 2, pair_step, (zero, zero, zero), unroll=4
    )
    close_items(both_items, n_both, blocks)
    close_items(first_items, n_first, blocks)
    close_items(second_items, n_second, blocks)
    both_items[both_items.shape[0] - 1] = n_both
    density = functools.partial(density_body, columns, source, acc_first, acc_second)
    run_items(both_items, n_both, functools.partial(density, 1, 1))
    run_items(first_items, n_first, functools.partial(density, 4, 0))
    run_items(second_items, n_second, functools.partial(density, 0, 4))
    first_rows(acc_first, turned, blocks)
    for c in range(4):
        own[c] = turned[pl.ds(c, blocks, stride=4), :]
    back[...] = sublane_sums(acc_second, others, 0)
    for c in range(3):
        push[c] = sublane_sums(acc_second, others, 1 + c)


def add_returned(send, total, returned, stride, offset):
    def one(k, carry):
        total[pl.ds(send[k], 1), :] += returned[pl.ds(k * stride + offset, 1), :]
        return carry

    lax.fori_loop(0, send.shape[0], one, 0, unroll=4)


def density_kernel(
    blocks, faces, send, table, near_sum, far_sum, from_above, from_below, returned, density, picked, head, tail
):
    density[...] = near_sum[0] + far_sum[0]
    density[blocks - faces :, :] += from_above[...]
    density[0:faces, :] += from_below[...]
    add_returned(send, density, returned, 1, 0)
    weight = table[pl.ds(6, blocks, stride=8), :]
    wall = table[pl.ds(7, blocks, stride=8), :]
    fluid = jnp.logical_and(weight > 0.0, wall < 0.5)
    density[...] = jnp.where(fluid, kernel_norm * density[...], 0.0)
    head[...] = density[0:faces, :]
    tail[...] = density[blocks - faces :, :]

    def pick(k, carry):
        picked[pl.ds(k, 1), :] = density[pl.ds(send[k], 1), :]
        return carry

    lax.fori_loop(0, send.shape[0], pick, 0, unroll=8)


def force_fields(source, density, number, extra):
    mass = source[pl.ds(6, number, stride=8), :]
    rho = jnp.where(mass > 0.0, density, 1.0)
    inverse = reciprocal(jnp.where(rho > 0.0, rho, 1.0))
    scaled = mass * inverse
    extra[pl.ds(0, number, stride=8), :] = scaled
    extra[pl.ds(1, number, stride=8), :] = 10.0 * (rho - 1.0) * inverse * scaled


def force_columns(blocks, extra, table, columns, more):
    make_columns(blocks, table, columns)

    def some(g, carry):
        turned = extra[pl.ds(pl.multiple_of(g * lanes, lanes), lanes), :].T
        for k in range(16):
            more[g * 16 + k] = turned if k == 0 else pltpu.roll(turned, lanes - 8 * k, 1)
        return carry

    lax.fori_loop(0, blocks // 16, some, 0)
    more[blocks] = jnp.zeros((lanes, lanes), jnp.float32)


def force_body(columns, more, source, extra, acc_first, acc_second, two_sided, decoded):
    lane = lane_numbers()
    outs = []
    for first, second, row in decoded:
        base = pl.multiple_of(second * 8, 8)
        rows = [wide(source[pl.ds(base + c, 1), :]) for c in range(7)]
        scaled = wide(extra[pl.ds(base, 1), :])
        press = wide(extra[pl.ds(base + 1, 1), :])
        merged = []
        sums = None
        for g in range(groups):
            cols = columns[first, pl.ds(row + 8 * g, 8), :]
            cols2 = more[first, pl.ds(row + 8 * g, 8), :]
            dx, dy, dz, square, u = close_u(cols, rows)
            u3 = (u * u) * u
            damp = u3 * (square * reciprocal(square + 0.25 * softening)) * (cols2[:, 0:1] * scaled)
            pull = u3 * (cols2[:, 1:2] * rows[6] + cols[:, 6:7] * press)
            values = [
                pull * d - damp * (cols[:, 3 + c : 4 + c] - rows[3 + c])
                for c, d in enumerate((dx, dy, dz))
            ]
            if two_sided:
                merged.append(
                    merge_lanes([jnp.sum(v, axis=1, keepdims=True) for v in values], first, lane)
                )
            sums = values if sums is None else [s + v for s, v in zip(sums, values)]
        outs.append((merged, sums))
    for (first, second, row), (merged, sums) in zip(decoded, outs):
        if two_sided:
            add_first(acc_first, first, row, merged)
        add_second(acc_second, second, sums)


def own_force_kernel(
    blocks,
    both_items,
    self_items,
    table,
    density,
    own,
    columns,
    more,
    extra,
    acc_first,
    acc_second,
    turned,
):
    force_fields(table, density[...], blocks, extra)
    force_columns(blocks, extra, table, columns, more)
    clear(acc_first, 1)
    clear(acc_second, 16)
    force = functools.partial(force_body, columns, more, table, extra, acc_first, acc_second)
    run_items(self_items, self_items[self_items.shape[0] - 1], functools.partial(force, False))
    run_items(both_items, both_items[both_items.shape[0] - 1], functools.partial(force, True))
    first_rows(acc_first, turned, blocks)
    for c in range(3):
        own[c] = turned[pl.ds(c, blocks, stride=4), :] - sublane_sums(acc_second, blocks, c)


def far_force_kernel(
    blocks,
    faces,
    both_items,
    table,
    density,
    low,
    high,
    far,
    low_density,
    high_density,
    far_density,
    push,
    own,
    back,
    columns,
    more,
    extra,
    source,
    source_density,
    source_extra,
    acc_first,
    acc_second,
    turned,
):
    others = source.shape[0] // 8
    source[0 : faces * 8, :] = low[...]
    source[faces * 8 : 2 * faces * 8, :] = high[...]
    source[2 * faces * 8 :, :] = far[...]
    source_density[0:faces, :] = low_density[...]
    source_density[faces : 2 * faces, :] = high_density[...]
    source_density[2 * faces :, :] = far_density[...]
    force_fields(table, density[...], blocks, extra)
    force_fields(source, source_density[...], others, source_extra)
    force_columns(blocks, extra, table, columns, more)
    clear(acc_first, 1)
    clear(acc_second, 16)
    force = functools.partial(force_body, columns, more, source, source_extra, acc_first, acc_second)
    run_items(both_items, both_items[both_items.shape[0] - 1], functools.partial(force, True))
    first_rows(acc_first, turned, blocks)
    for c in range(3):
        own[c] = turned[pl.ds(c, blocks, stride=4), :]
    mass = source[pl.ds(6, others, stride=8), :]
    inverse = reciprocal(jnp.where(mass > 0.0, mass, 1.0))
    for c in range(3):
        back[pl.ds(c, others, stride=4), :] = push[c] - sublane_sums(acc_second, others, c) * inverse
    back[pl.ds(3, others, stride=4), :] = jnp.zeros((others, lanes), jnp.float32)


def final_kernel(
    blocks,
    faces,
    send,
    table,
    near_sum,
    far_sum,
    near_force,
    far_force,
    from_above,
    from_below,
    returned,
    out,
    total,
):
    mass = table[pl.ds(6, blocks, stride=8), :]
    wall = table[pl.ds(7, blocks, stride=8), :]
    fluid = jnp.logical_and(mass > 0.0, wall < 0.5)
    inverse = reciprocal(jnp.where(mass > 0.0, mass, 1.0))
    for c in range(3):
        total[...] = near_sum[1 + c] + far_sum[1 + c] + (near_force[c] + far_force[c]) * inverse
        total[blocks - faces :, :] += from_above[pl.ds(c, faces, stride=4), :]
        total[0:faces, :] += from_below[pl.ds(c, faces, stride=4), :]
        add_returned(send, total, returned, 4, c)
        out[c] = jnp.where(fluid, kernel_norm * total[...], 0.0)


def f32(*shape):
    return jax.ShapeDtypeStruct(shape, jnp.float32)


def i32(*shape):
    return jax.ShapeDtypeStruct(shape, jnp.int32)


def to_above(shard):
    count = lax.axis_size("slab")
    return lax.ppermute(shard, "slab", [(i, i + 1) for i in range(count - 1)])


def to_below(shard):
    count = lax.axis_size("slab")
    return lax.ppermute(shard, "slab", [(i + 1, i) for i in range(count - 1)])


def swap_tiles(rows, tiles):
    parts = rows.reshape(tiles, rows.shape[0] // tiles, lanes)
    return lax.all_to_all(parts, "tile", split_axis=0, concat_axis=0, tiled=True).reshape(rows.shape)


def on_device(
    positions,
    velocities,
    masses,
    wall_areas,
    normals,
    wall_flags,
    counts,
    send_list,
    local_pairs,
    remote_pairs,
    remote_live,
):
    blocks = positions.shape[1]
    faces = blocks // 4
    tiles = lax.axis_size("tile")
    send = send_list.reshape(-1)
    offered = send.shape[0]
    others = 2 * faces + offered
    n_local = local_pairs.shape[0]
    n_remote = remote_pairs.shape[0]
    per = lanes // rows_item
    local_flat = local_pairs.reshape(-1)
    remote_flat = remote_pairs.reshape(-1)
    own_cap = per * max(n_local, blocks) + 8
    far_cap = per * n_remote + 8
    columns = vmem((blocks + 1, lanes, lanes), jnp.float32)
    acc_first = vmem((blocks // 32 + 1, lanes, lanes), jnp.float32)
    turned = vmem((blocks * 4, lanes), jnp.float32)

    table, picked, head, tail = pl.pallas_call(
        functools.partial(pack_kernel, blocks, faces),
        out_shape=(f32(blocks * 8, lanes), f32(offered * 8, lanes), f32(faces * 8, lanes), f32(faces * 8, lanes)),
        in_specs=[spec(smem)] * 2 + [spec(vmem)] * 7,
        out_specs=[spec(vmem)] * 4,
        name="pack",
    )(
        counts,
        send,
        positions,
        velocities,
        masses,
        wall_areas,
        normals,
        wall_flags[:, None],
        counts[:, None],
    )
    low = to_above(tail)
    high = to_below(head)
    far = swap_tiles(picked, tiles)

    near_sum, own_items, self_items = pl.pallas_call(
        functools.partial(own_density_kernel, blocks),
        out_shape=(f32(4, blocks, lanes), i32(own_cap), i32(own_cap)),
        in_specs=[spec(smem)] * 3 + [spec(vmem)],
        out_specs=[spec(vmem), spec(smem), spec(smem)],
        scratch_shapes=[
            columns,
            acc_first,
            vmem((blocks * 32, lanes), jnp.float32),
            turned,
            smem((own_cap,), jnp.int32),
        ],
        compiler_params=params(24),
        cost_estimate=pl.CostEstimate(flops=40_000_000, bytes_accessed=400_000, transcendentals=1_000_000),
        name="own_density",
    )(counts, wall_flags, local_flat, table)

    far_sum, back, push, far_items = pl.pallas_call(
        functools.partial(far_density_kernel, blocks, faces),
        out_shape=(f32(4, blocks, lanes), f32(others, lanes), f32(3, others, lanes), i32(far_cap)),
        in_specs=[spec(smem)] * 4 + [spec(vmem)] * 4,
        out_specs=[spec(vmem)] * 3 + [spec(smem)],
        scratch_shapes=[
            columns,
            acc_first,
            vmem((others * 32, lanes), jnp.float32),
            turned,
            vmem((others * 8, lanes), jnp.float32),
            vmem((others, lanes), jnp.float32),
            smem((others, lanes), jnp.float32),
            smem((far_cap,), jnp.int32),
            smem((far_cap,), jnp.int32),
            pltpu.SemaphoreType.DMA,
        ],
        compiler_params=params(24),
        cost_estimate=pl.CostEstimate(flops=80_000_000, bytes_accessed=1_000_000, transcendentals=2_000_000),
        name="far_density",
    )(counts, wall_flags, remote_live, remote_flat, table, low, high, far)

    from_above = to_below(back[0:faces])
    from_below = to_above(back[faces : 2 * faces])
    returned = swap_tiles(back[2 * faces :], tiles)

    density, picked_density, head_density, tail_density = pl.pallas_call(
        functools.partial(density_kernel, blocks, faces),
        out_shape=(f32(blocks, lanes), f32(offered, lanes), f32(faces, lanes), f32(faces, lanes)),
        in_specs=[spec(smem)] + [spec(vmem)] * 6,
        out_specs=[spec(vmem)] * 4,
        name="density",
    )(send, table, near_sum, far_sum, from_above, from_below, returned)

    low_density = to_above(tail_density)
    high_density = to_below(head_density)
    far_density = swap_tiles(picked_density, tiles)

    near_force = pl.pallas_call(
        functools.partial(own_force_kernel, blocks),
        out_shape=f32(3, blocks, lanes),
        in_specs=[spec(smem)] * 2 + [spec(vmem)] * 2,
        out_specs=spec(vmem),
        scratch_shapes=[
            columns,
            columns,
            vmem((blocks * 8, lanes), jnp.float32),
            acc_first,
            vmem((blocks * 32, lanes), jnp.float32),
            turned,
        ],
        compiler_params=params(24),
        cost_estimate=pl.CostEstimate(flops=80_000_000, bytes_accessed=400_000, transcendentals=2_000_000),
        name="own_force",
    )(own_items, self_items, table, density)

    far_force, force_back = pl.pallas_call(
        functools.partial(far_force_kernel, blocks, faces),
        out_shape=(f32(3, blocks, lanes), f32(others * 4, lanes)),
        in_specs=[spec(smem)] + [spec(vmem)] * 9,
        out_specs=[spec(vmem)] * 2,
        scratch_shapes=[
            columns,
            columns,
            vmem((blocks * 8, lanes), jnp.float32),
            vmem((others * 8, lanes), jnp.float32),
            vmem((others, lanes), jnp.float32),
            vmem((others * 8, lanes), jnp.float32),
            acc_first,
            vmem((others * 32, lanes), jnp.float32),
            turned,
        ],
        compiler_params=params(32),
        cost_estimate=pl.CostEstimate(flops=160_000_000, bytes_accessed=1_000_000, transcendentals=4_000_000),
        name="far_force",
    )(
        far_items,
        table,
        density,
        low,
        high,
        far,
        low_density,
        high_density,
        far_density,
        push,
    )

    force_above = to_below(force_back[0 : faces * 4])
    force_below = to_above(force_back[faces * 4 : 2 * faces * 4])
    force_returned = swap_tiles(force_back[2 * faces * 4 :], tiles)

    acceleration = pl.pallas_call(
        functools.partial(final_kernel, blocks, faces),
        out_shape=f32(3, blocks, lanes),
        in_specs=[spec(smem)] + [spec(vmem)] * 8,
        out_specs=spec(vmem),
        scratch_shapes=[vmem((blocks, lanes), jnp.float32)],
        name="total",
    )(send, table, near_sum, far_sum, near_force, far_force, force_above, force_below, force_returned)
    return (density, acceleration)


def solution(mesh):
    placed = (
        P(None, ("slab", "tile"), None),
        P(None, ("slab", "tile"), None),
        P(("slab", "tile"), None),
        P(("slab", "tile"), None),
        P(None, ("slab", "tile"), None),
        P(("slab", "tile")),
        P(("slab", "tile")),
        P(("slab", "tile"), None, None),
        P(("slab", "tile"), None),
        P(("slab", "tile"), None),
        P(("slab", "tile")),
    )
    return jax.shard_map(
        on_device,
        mesh=mesh,
        in_specs=placed,
        out_specs=(P(("slab", "tile"), None), P(None, ("slab", "tile"), None)),
        check_vma=False,
    )
```

```python
import functools
import math

import jax
import jax.numpy as jnp
from jax import lax
from jax.experimental import pallas as pl
from jax.experimental.pallas import tpu as pltpu
from jax.sharding import PartitionSpec as P

kernel_norm = 21.0 / (16.0 * math.pi)
softening = 0.01
tiny = 1e-30
lanes = 128
rows_item = 32
groups = rows_item // 8
batch = lanes // rows_item
halves = 2
field_order = (0, 1, 2, 6, 3, 4, 5, 7)
bf16 = jnp.bfloat16
vmem = pltpu.VMEM
smem = pltpu.SMEM


def spec(space):
    return pl.BlockSpec(memory_space=space)


def params(mib):
    return pltpu.CompilerParams(vmem_limit_bytes=mib * 1024 * 1024)


def column_of(row):
    number = row.shape[1]
    same = lax.broadcasted_iota(jnp.int32, (number, number), 0) == lax.broadcasted_iota(
        jnp.int32, (number, number), 1
    )
    return jnp.sum(jnp.where(same, row, 0.0), axis=1, keepdims=True)


def pack_kernel(
    blocks, faces, per_peer, send, pos, vel, mass, area, normal, flags_row, counts_row, table, picked, head, tail
):
    slot = lax.broadcasted_iota(jnp.int32, (blocks, lanes), 1).astype(jnp.float32)
    alive = slot < column_of(counts_row[...].astype(jnp.float32))
    wall_value = column_of(flags_row[...].astype(jnp.float32)) + jnp.zeros((blocks, lanes), jnp.float32)
    wall = wall_value > 0.5
    nx, ny, nz = normal[0], normal[1], normal[2]
    length = jnp.sqrt(nx * nx + ny * ny + nz * nz)
    weight = jnp.where(alive, jnp.where(wall, area[...], mass[...]), 0.0)
    wall_scale = weight / length
    parts = (nx, ny, nz)
    for c in range(3):
        table[pl.ds(c, blocks, stride=8), :] = 0.5 * pos[c]
        table[pl.ds(3 + c, blocks, stride=8), :] = jnp.where(wall, wall_scale * parts[c], vel[c])
    table[pl.ds(6, blocks, stride=8), :] = weight
    table[pl.ds(7, blocks, stride=8), :] = wall_value
    head[...] = table[0 : faces * 8, :]
    tail[...] = table[(blocks - faces) * 8 : blocks * 8, :]

    def pick(t, carry):
        for k in range(per_peer):
            source = pl.multiple_of(send[0, t, k] * 8, 8)
            at = pl.multiple_of((t * per_peer + k) * 8, 8)
            picked[pl.ds(at, 8), :] = table[pl.ds(source, 8), :]
        return carry

    lax.fori_loop(0, picked.shape[0] // (8 * per_peer), pick, 0, unroll=2)


def rounded(x):
    return x.astype(bf16).astype(jnp.float32)


def split3(x):
    high = rounded(x)
    rest = x - high
    middle = rounded(rest)
    return high, middle, rest - middle


def make_spread(spread):
    shape = spread.shape
    k = lax.broadcasted_iota(jnp.int32, shape, 0) & 31
    tile = lax.broadcasted_iota(jnp.int32, shape, 1) >> 7
    want = jnp.where(tile == 3, 6, jnp.where(tile > 3, tile - 1, tile))
    want = jnp.where(tile == 7, 7, want)
    hit = jnp.logical_and(jnp.logical_and(k < 24, (k & 7) == want), tile < 8)
    hit = jnp.logical_or(hit, jnp.logical_and(jnp.logical_and(k >= 24, k < 27), tile == 8))
    spread[...] = jnp.where(hit, 1.0, 0.0).astype(bf16)


def make_columns(blocks, table, last, columns, stage):
    lane = lax.broadcasted_iota(jnp.int32, (lanes, lanes), 1) >> 5
    for g in range(blocks // 4):
        for j in range(4):
            b = 4 * g + j
            for p, piece in enumerate(split3(table[8 * b : 8 * b + 8, :])):
                stage[32 * b + 8 * p : 32 * b + 8 * p + 8, :] = piece
            if last is None:
                stage[32 * b + 24 : 32 * b + 32, :] = jnp.zeros((8, lanes), jnp.float32)
            else:
                stage[32 * b + 24 : 32 * b + 32, :] = last[8 * b : 8 * b + 8, :]

    def some(g, carry):
        turned = stage[pl.ds(pl.multiple_of(g * lanes, lanes), lanes), :].T
        for j in range(4):
            columns[g * 4 + j] = jnp.where(lane == j, turned, 0.0).astype(bf16)
        return carry

    lax.fori_loop(0, blocks // 4, some, 0)
    columns[blocks] = jnp.zeros((lanes, lanes), bf16)


def put_items(items, at, first, second):
    code = first | (second << 8)
    for k in range(lanes // rows_item):
        items[at + k] = code | (k << 16)


def close_items(items, count, blocks):
    for k in range(batch * halves):
        items[count + k] = jnp.int32(blocks)


def decode(code):
    first = code & 255
    second = (code >> 8) & 255
    row = pl.multiple_of((code >> 16) * rows_item, rows_item)
    return first, second, row


def wide(row):
    return jnp.broadcast_to(row, (8, lanes))


def spread_fields(columns, spread, wide_fields, tiles, decoded):
    left = jnp.concatenate([columns[first, pl.ds(row, rows_item), :] for first, second, row in decoded], axis=0)
    for t in range((tiles + 1) // 2):
        both = jnp.dot(left, spread[:, 256 * t : 256 * t + 256], preferred_element_type=jnp.float32)
        wide_fields[2 * t] = both[:, 0:lanes]
        wide_fields[2 * t + 1] = both[:, lanes : 2 * lanes]


def close_u(fields, rows):
    dx = fields[0] - rows[0]
    dy = fields[1] - rows[1]
    dz = fields[2] - rows[2]
    square = dx * dx + dy * dy + dz * dz
    safe = jnp.maximum(square, tiny)
    q = safe * lax.rsqrt(safe)
    u = jnp.maximum(1.0 - q, 0.0)
    return dx, dy, dz, square, u


def kernel_shape(u):
    u2 = u * u
    return (u2 * u2) * (5.0 - 4.0 * u)


def run_items(columns, spread, wide_fields, tiles, items, count, body, finish):
    def step(it, carry):
        done = []
        for h in range(halves):
            decoded = [decode(items[(it * halves + h) * batch + k]) for k in range(batch)]
            spread_fields(columns, spread, wide_fields[h], tiles, decoded)
            done.append((decoded, body(wide_fields[h], decoded)))
        for decoded, outs in done:
            finish(decoded, outs)
        return carry

    size = batch * halves
    lax.fori_loop(0, (count + size - 1) // size, step, 0)


def merge_lanes(values, first, lane):
    base = (first & 15) * 8
    total = jnp.zeros((8, lanes), jnp.float32)
    for c, value in enumerate(values):
        total = jnp.where(lane == base + c, value, total)
    return total


def merge_rows(values, sub):
    total = jnp.zeros((8, lanes), jnp.float32)
    for c, value in enumerate(values):
        total = jnp.where(sub == c, jnp.sum(value, axis=0, keepdims=True), total)
    return total


def add_sums(acc_first, acc_second, decoded, outs):
    for (first, second, row), (merged, tile) in zip(decoded, outs):
        if merged:
            slab = first >> 4
            for g in range(groups):
                acc_first[slab, pl.ds(row + 8 * g, 8), :] += merged[g]
        if tile is not None:
            at = pl.multiple_of(second * 8, 8)
            acc_second[pl.ds(at, 8), :] += tile


def density_body(source, to_first, to_second, wide_fields, decoded):
    lane = lax.broadcasted_iota(jnp.int32, (8, lanes), 1)
    sub = lax.broadcasted_iota(jnp.int32, (8, lanes), 0)
    outs = []
    for k, (first, second, row) in enumerate(decoded):
        base = pl.multiple_of(second * 8, 8)
        rows = [wide(source[pl.ds(base + c, 1), :]) for c in range(3)]
        given = []
        if to_first:
            given = [wide(source[pl.ds(base + 6, 1), :])]
            if to_first == 4:
                given += [wide(source[pl.ds(base + 3 + c, 1), :]) for c in range(3)]
        merged = []
        sums = None
        for g in range(groups):
            at = rows_item * k + 8 * g
            fields = [wide_fields[f, at : at + 8, :] for f in range(3 + to_second)]
            w = kernel_shape(close_u(fields, rows)[4])
            if to_first:
                values = [jnp.sum(w * other, axis=1, keepdims=True) for other in given]
                merged.append(merge_lanes(values, first, lane))
            if to_second:
                back = [w * field for field in fields[3:]]
                sums = back if sums is None else [s + b for s, b in zip(sums, back)]
        outs.append((merged, merge_rows(sums, sub) if to_second else None))
    return outs


def clear(ref, pieces):
    size = ref.shape[0] // pieces

    def some(k, carry):
        at = pl.multiple_of(k * size, size)
        ref[pl.ds(at, size)] = jnp.zeros((size,) + tuple(ref.shape[1:]), jnp.float32)
        return carry

    lax.fori_loop(0, pieces, some, 0)


def plane(ref, number, c):
    return ref[pl.ds(c, number, stride=8), :]


def first_rows(acc_first, turned, blocks):
    for s in range(blocks // 16):
        turned[s * lanes : (s + 1) * lanes, :] = acc_first[s].T


def run_density(columns, spread, fields, source, acc_first, acc_second, to_first, to_second, items, count):
    run_items(
        columns,
        spread,
        fields,
        3 + to_second,
        items,
        count,
        functools.partial(density_body, source, to_first, to_second),
        functools.partial(add_sums, acc_first, acc_second),
    )


def self_density_kernel(
    blocks, counts, flags, table, columns, own, items, stage, spread, wide_a, wide_b, acc_second
):
    make_columns(blocks, table, None, columns, stage)
    make_spread(spread)
    clear(acc_second, 4)

    def self_step(b, n):
        put_items(items, n, b, b)
        return n + jnp.where(flags[b] > 0, 0, (counts[b] + rows_item - 1) // rows_item)

    count = lax.fori_loop(0, blocks, self_step, jnp.int32(0), unroll=4)
    close_items(items, count, blocks)
    items[items.shape[0] - 1] = count
    run_density(columns, spread, (wide_a, wide_b), table, None, acc_second, 0, 1, items, count)
    own[...] = plane(acc_second, blocks, 0)


def local_density_kernel(
    blocks,
    counts,
    flags,
    pairs,
    table,
    columns,
    own,
    both_items,
    spread,
    wide_a,
    wide_b,
    acc_first,
    acc_second,
    turned,
    wall_items,
):
    make_spread(spread)
    clear(acc_first, 1)
    clear(acc_second, 4)

    def pair_step(p, carry):
        n_both, n_wall = carry
        a = pairs[0, p]
        b = pairs[1, p]
        kinds = flags[a] + flags[b]
        swap = jnp.where(kinds == 1, flags[b] > 0, counts[b] < counts[a])
        first = jnp.where(swap, b, a)
        second = jnp.where(swap, a, b)
        number = (counts[first] + rows_item - 1) // rows_item
        put_items(both_items, n_both, first, second)
        put_items(wall_items, n_wall, first, second)
        return (n_both + jnp.where(kinds == 0, number, 0), n_wall + jnp.where(kinds == 1, number, 0))

    n_both, n_wall = lax.fori_loop(
        0, pairs.shape[1], pair_step, (jnp.int32(0), jnp.int32(0)), unroll=4
    )
    close_items(both_items, n_both, blocks)
    close_items(wall_items, n_wall, blocks)
    both_items[both_items.shape[0] - 1] = n_both
    density = functools.partial(
        run_density, columns, spread, (wide_a, wide_b), table, acc_first, acc_second
    )
    density(1, 1, both_items, n_both)
    density(0, 4, wall_items, n_wall)
    first_rows(acc_first, turned, blocks)
    for c in range(4):
        own[c] = plane(turned, blocks, c) + plane(acc_second, blocks, c)


def far_density_kernel(
    blocks,
    faces,
    counts,
    flags,
    live,
    pairs,
    columns,
    low,
    high,
    far,
    own,
    back_low,
    back_high,
    back_far,
    push,
    both_items,
    spread,
    wide_a,
    wide_b,
    acc_first,
    acc_second,
    turned,
    source,
    wall_rows,
    wall_flag,
    first_items,
    second_items,
    sem,
):
    others = source.shape[0] // 8
    source[0 : faces * 8, :] = low[...]
    source[faces * 8 : 2 * faces * 8, :] = high[...]
    source[2 * faces * 8 :, :] = far[...]
    wall_rows[...] = plane(source, others, 7)
    copy = pltpu.make_async_copy(wall_rows, wall_flag, sem)
    copy.start()
    make_spread(spread)
    clear(acc_first, 1)
    clear(acc_second, 4)
    copy.wait()

    def pair_step(p, carry):
        n_both, n_first, n_second = carry
        a = pairs[0, p]
        j = pairs[1, p]
        b = jnp.where(j < blocks, j, j - blocks)
        wall_a = flags[a]
        wall_b = jnp.where(wall_flag[b, 0] > 0.5, 1, 0)
        number = jnp.where(p < live[0], (counts[a] + rows_item - 1) // rows_item, 0)
        put_items(both_items, n_both, a, b)
        put_items(first_items, n_first, a, b)
        put_items(second_items, n_second, a, b)
        return (
            n_both + number * (1 - wall_a) * (1 - wall_b),
            n_first + number * (1 - wall_a) * wall_b,
            n_second + number * wall_a * (1 - wall_b),
        )

    zero = jnp.int32(0)
    n_both, n_first, n_second = lax.fori_loop(
        0, pairs.shape[1], pair_step, (zero, zero, zero), unroll=4
    )
    close_items(both_items, n_both, blocks)
    close_items(first_items, n_first, blocks)
    close_items(second_items, n_second, blocks)
    both_items[both_items.shape[0] - 1] = n_both
    density = functools.partial(
        run_density, columns, spread, (wide_a, wide_b), source, acc_first, acc_second
    )
    density(1, 1, both_items, n_both)
    density(4, 0, first_items, n_first)
    density(0, 4, second_items, n_second)
    first_rows(acc_first, turned, blocks)
    for c in range(4):
        own[c] = plane(turned, blocks, c)
    back_low[...] = acc_second[pl.ds(0, faces, stride=8), :]
    back_high[...] = acc_second[pl.ds(faces * 8, faces, stride=8), :]
    back_far[...] = acc_second[pl.ds(2 * faces * 8, others - 2 * faces, stride=8), :]
    for c in range(3):
        push[c] = plane(acc_second, others, 1 + c)


def fluid_mask(blocks, table):
    return jnp.logical_and(plane(table, blocks, 6) > 0.0, plane(table, blocks, 7) < 0.5)


def density_kernel(
    blocks,
    faces,
    per_peer,
    send,
    table,
    self_sum,
    local_sum,
    far_sum,
    from_above,
    from_below,
    returned,
    density,
    picked,
    head,
    tail,
):
    density[...] = self_sum[...] + local_sum[0] + far_sum[0]
    density[blocks - faces :, :] += from_above[...]
    density[0:faces, :] += from_below[...]
    peers = picked.shape[0] // per_peer

    def give(t, carry):
        for k in range(per_peer):
            density[pl.ds(send[0, t, k], 1), :] += returned[pl.ds(t * per_peer + k, 1), :]
        return carry

    lax.fori_loop(0, peers, give, 0, unroll=2)
    density[...] = jnp.where(fluid_mask(blocks, table), kernel_norm * density[...], 0.0)
    head[...] = density[0:faces, :]
    tail[...] = density[blocks - faces :, :]

    def pick(t, carry):
        for k in range(per_peer):
            picked[pl.ds(t * per_peer + k, 1), :] = density[pl.ds(send[0, t, k], 1), :]
        return carry

    lax.fori_loop(0, peers, pick, 0, unroll=4)


def force_fields(source, density, number, pressed):
    mass = plane(source, number, 6)
    rho = jnp.where(mass > 0.0, density, 1.0)
    inverse = 1.0 / jnp.where(rho > 0.0, rho, 1.0)
    scaled = mass * inverse
    source[pl.ds(7, number, stride=8), :] = scaled
    press = 10.0 * (rho - 1.0) * inverse * scaled
    pressed[...] = press
    return press


def force_body(source, pressed, to_first, wide_fields, decoded):
    lane = lax.broadcasted_iota(jnp.int32, (8, lanes), 1)
    sub = lax.broadcasted_iota(jnp.int32, (8, lanes), 0)
    outs = []
    for k, (first, second, row) in enumerate(decoded):
        base = pl.multiple_of(second * 8, 8)
        rows = [wide(source[pl.ds(base + c, 1), :]) for c in range(8)]
        press = wide(pressed[pl.ds(second, 1), :])
        merged = []
        sums = None
        for g in range(groups):
            at = rows_item * k + 8 * g
            fields = [wide_fields[f, at : at + 8, :] for f in range(9)]
            dx, dy, dz, square, u = close_u(fields, rows)
            u3 = (u * u) * u
            damp = u3 * (square * (1.0 / (square + 0.25 * softening))) * (fields[7] * rows[7])
            pull = u3 * (fields[8] * rows[6] + fields[3] * press)
            values = [
                pull * d - damp * (fields[4 + c] - rows[3 + c]) for c, d in enumerate((dx, dy, dz))
            ]
            if to_first:
                merged.append(
                    merge_lanes([jnp.sum(v, axis=1, keepdims=True) for v in values], first, lane)
                )
            sums = values if sums is None else [s + v for s, v in zip(sums, values)]
        outs.append((merged, merge_rows(sums, sub)))
    return outs


def run_force(columns, spread, fields, source, pressed, acc_first, acc_second, to_first, items):
    run_items(
        columns,
        spread,
        fields,
        9,
        items,
        items[items.shape[0] - 1],
        functools.partial(force_body, source, pressed, to_first),
        functools.partial(add_sums, acc_first, acc_second),
    )


def self_force_kernel(
    blocks,
    items,
    table,
    density,
    columns,
    source,
    pressed,
    own,
    stage,
    last,
    spread,
    wide_a,
    wide_b,
    acc_second,
):
    source[...] = table[...]
    press = force_fields(source, density[...], blocks, pressed)
    last[...] = jnp.zeros(last.shape, jnp.float32)
    for p, piece in enumerate(split3(press)):
        last[pl.ds(p, blocks, stride=8), :] = piece
    make_columns(blocks, source, last, columns, stage)
    make_spread(spread)
    clear(acc_second, 4)
    run_force(columns, spread, (wide_a, wide_b), source, pressed, None, acc_second, False, items)
    for c in range(3):
        own[c] = -plane(acc_second, blocks, c)


def local_force_kernel(
    blocks,
    items,
    columns,
    source,
    pressed,
    own,
    spread,
    wide_a,
    wide_b,
    acc_first,
    acc_second,
    turned,
):
    make_spread(spread)
    clear(acc_first, 1)
    clear(acc_second, 4)
    run_force(columns, spread, (wide_a, wide_b), source, pressed, acc_first, acc_second, True, items)
    first_rows(acc_first, turned, blocks)
    for c in range(3):
        own[c] = plane(turned, blocks, c) - plane(acc_second, blocks, c)


def far_force_kernel(
    blocks,
    faces,
    items,
    columns,
    low,
    high,
    far,
    low_density,
    high_density,
    far_density,
    push,
    own,
    back_low,
    back_high,
    back_far,
    source,
    source_density,
    pressed,
    spread,
    wide_a,
    wide_b,
    acc_first,
    acc_second,
    turned,
):
    others = source.shape[0] // 8
    source[0 : faces * 8, :] = low[...]
    source[faces * 8 : 2 * faces * 8, :] = high[...]
    source[2 * faces * 8 :, :] = far[...]
    source_density[0:faces, :] = low_density[...]
    source_density[faces : 2 * faces, :] = high_density[...]
    source_density[2 * faces :, :] = far_density[...]
    mass = plane(source, others, 6)
    inverse = 1.0 / jnp.where(mass > 0.0, mass, 1.0)
    force_fields(source, source_density[...], others, pressed)
    make_spread(spread)
    clear(acc_first, 1)
    clear(acc_second, 4)
    run_force(columns, spread, (wide_a, wide_b), source, pressed, acc_first, acc_second, True, items)
    first_rows(acc_first, turned, blocks)
    for c in range(3):
        own[c] = plane(turned, blocks, c)
        acc_second[pl.ds(c, others, stride=8), :] = push[c] - plane(acc_second, others, c) * inverse
    for at, (out, number) in zip(
        (0, faces, 2 * faces), ((back_low, faces), (back_high, faces), (back_far, others - 2 * faces))
    ):
        for k in range(number):
            out[4 * k : 4 * k + 4, :] = acc_second[8 * (at + k) : 8 * (at + k) + 4, :]


def final_kernel(
    blocks,
    faces,
    per_peer,
    send,
    table,
    local_sum,
    far_sum,
    self_force,
    local_force,
    far_force,
    from_above,
    from_below,
    returned,
    out,
    total,
):
    mass = plane(table, blocks, 6)
    inverse = 1.0 / jnp.where(mass > 0.0, mass, 1.0)
    for c in range(3):
        force = (self_force[c] + local_force[c] + far_force[c]) * inverse
        total[pl.ds(c, blocks, stride=8), :] = local_sum[1 + c] + far_sum[1 + c] + force
    for k in range(faces):
        at = 8 * (blocks - faces + k)
        total[at : at + 4, :] += from_above[4 * k : 4 * k + 4, :]
        total[8 * k : 8 * k + 4, :] += from_below[4 * k : 4 * k + 4, :]

    def give(t, carry):
        for k in range(per_peer):
            at = pl.multiple_of(send[0, t, k] * 8, 8)
            source = pl.multiple_of((t * per_peer + k) * 4, 4)
            total[pl.ds(at, 4), :] += returned[pl.ds(source, 4), :]
        return carry

    lax.fori_loop(0, send.shape[1], give, 0, unroll=2)
    fluid = fluid_mask(blocks, table)
    for c in range(3):
        out[c] = jnp.where(fluid, kernel_norm * plane(total, blocks, c), 0.0)


def f32(*shape):
    return jax.ShapeDtypeStruct(shape, jnp.float32)


def i32(*shape):
    return jax.ShapeDtypeStruct(shape, jnp.int32)


def to_above(shard):
    count = lax.axis_size("slab")
    return lax.ppermute(shard, "slab", [(i, i + 1) for i in range(count - 1)])


def to_below(shard):
    count = lax.axis_size("slab")
    return lax.ppermute(shard, "slab", [(i + 1, i) for i in range(count - 1)])


def swap_tiles(rows, tiles):
    parts = rows.reshape(tiles, rows.shape[0] // tiles, lanes)
    return lax.all_to_all(parts, "tile", split_axis=0, concat_axis=0, tiled=True).reshape(rows.shape)


def on_device(
    positions,
    velocities,
    masses,
    wall_areas,
    normals,
    wall_flags,
    counts,
    send_list,
    local_pairs,
    remote_pairs,
    remote_live,
):
    blocks = positions.shape[1]
    faces = blocks // 4
    tiles = lax.axis_size("tile")
    per_peer = send_list.shape[2]
    offered = send_list.shape[1] * per_peer
    others = 2 * faces + offered
    n_local = local_pairs.shape[0]
    n_remote = remote_pairs.shape[0]
    per = lanes // rows_item
    spare = 2 * batch * halves
    self_cap = per * blocks + spare
    own_cap = per * n_local + spare
    far_cap = per * n_remote + spare
    columns_shape = jax.ShapeDtypeStruct((blocks + 1, lanes, lanes), bf16)
    stage = vmem((blocks * 32, lanes), jnp.float32)

    def fields(number):
        return [vmem((lanes, 128 * number), bf16)] + [vmem((number, lanes, lanes), jnp.float32)] * 2

    def sums(number):
        return [
            vmem((blocks // 16 + 1, lanes, lanes), jnp.float32),
            vmem((number * 8, lanes), jnp.float32),
            vmem((blocks * 8, lanes), jnp.float32),
        ]

    def cost(flops):
        return pl.CostEstimate(flops=flops, bytes_accessed=400_000, transcendentals=0)

    table, picked, head, tail = pl.pallas_call(
        functools.partial(pack_kernel, blocks, faces, per_peer),
        out_shape=(f32(blocks * 8, lanes), f32(offered * 8, lanes), f32(faces * 8, lanes), f32(faces * 8, lanes)),
        in_specs=[spec(smem)] + [spec(vmem)] * 7,
        out_specs=[spec(vmem)] * 4,
        name="pack",
    )(
        send_list,
        positions,
        velocities,
        masses,
        wall_areas,
        normals,
        wall_flags[None, :],
        counts[None, :],
    )
    low = to_above(tail)
    high = to_below(head)
    far = swap_tiles(picked, tiles)

    columns, self_sum, self_items = pl.pallas_call(
        functools.partial(self_density_kernel, blocks),
        out_shape=(columns_shape, f32(blocks, lanes), i32(self_cap)),
        in_specs=[spec(smem)] * 2 + [spec(vmem)],
        out_specs=[spec(vmem), spec(vmem), spec(smem)],
        scratch_shapes=[stage] + fields(8) + [vmem((blocks * 8, lanes), jnp.float32)],
        compiler_params=params(20),
        cost_estimate=cost(40_000_000),
        name="self_density",
    )(counts, wall_flags, table)

    far_sum, back_low, back_high, back_far, push, far_items = pl.pallas_call(
        functools.partial(far_density_kernel, blocks, faces),
        out_shape=(
            f32(4, blocks, lanes),
            f32(faces, lanes),
            f32(faces, lanes),
            f32(offered, lanes),
            f32(3, others, lanes),
            i32(far_cap),
        ),
        in_specs=[spec(smem)] * 4 + [spec(vmem)] * 4,
        out_specs=[spec(vmem)] * 5 + [spec(smem)],
        scratch_shapes=fields(8)
        + sums(others)
        + [
            vmem((others * 8, lanes), jnp.float32),
            vmem((others, lanes), jnp.float32),
            smem((others, lanes), jnp.float32),
            smem((far_cap,), jnp.int32),
            smem((far_cap,), jnp.int32),
            pltpu.SemaphoreType.DMA,
        ],
        compiler_params=params(20),
        cost_estimate=cost(100_000_000),
        name="far_density",
    )(counts, wall_flags, remote_live, remote_pairs.T, columns, low, high, far)

    from_above = to_below(back_low)
    from_below = to_above(back_high)
    returned = swap_tiles(back_far, tiles)

    local_sum, own_items = pl.pallas_call(
        functools.partial(local_density_kernel, blocks),
        out_shape=(f32(4, blocks, lanes), i32(own_cap)),
        in_specs=[spec(smem)] * 3 + [spec(vmem)] * 2,
        out_specs=[spec(vmem), spec(smem)],
        scratch_shapes=fields(8) + sums(blocks) + [smem((own_cap,), jnp.int32)],
        compiler_params=params(20),
        cost_estimate=cost(40_000_000),
        name="local_density",
    )(counts, wall_flags, local_pairs.T, table, columns)

    density, picked_density, head_density, tail_density = pl.pallas_call(
        functools.partial(density_kernel, blocks, faces, per_peer),
        out_shape=(f32(blocks, lanes), f32(offered, lanes), f32(faces, lanes), f32(faces, lanes)),
        in_specs=[spec(smem)] + [spec(vmem)] * 7,
        out_specs=[spec(vmem)] * 4,
        name="density",
    )(send_list, table, self_sum, local_sum, far_sum, from_above, from_below, returned)

    low_density = to_above(tail_density)
    high_density = to_below(head_density)
    far_density = swap_tiles(picked_density, tiles)

    force_columns, force_table, pressed, self_force = pl.pallas_call(
        functools.partial(self_force_kernel, blocks),
        out_shape=(columns_shape, f32(blocks * 8, lanes), f32(blocks, lanes), f32(3, blocks, lanes)),
        in_specs=[spec(smem)] + [spec(vmem)] * 2,
        out_specs=[spec(vmem)] * 4,
        scratch_shapes=[stage, vmem((blocks * 8, lanes), jnp.float32)]
        + fields(10)
        + [vmem((blocks * 8, lanes), jnp.float32)],
        compiler_params=params(20),
        cost_estimate=cost(80_000_000),
        name="self_force",
    )(self_items, table, density)

    far_force, force_low, force_high, force_far = pl.pallas_call(
        functools.partial(far_force_kernel, blocks, faces),
        out_shape=(
            f32(3, blocks, lanes),
            f32(faces * 4, lanes),
            f32(faces * 4, lanes),
            f32(offered * 4, lanes),
        ),
        in_specs=[spec(smem)] + [spec(vmem)] * 8,
        out_specs=[spec(vmem)] * 4,
        scratch_shapes=[
            vmem((others * 8, lanes), jnp.float32),
            vmem((others, lanes), jnp.float32),
            vmem((others, lanes), jnp.float32),
        ]
        + fields(10)
        + sums(others),
        compiler_params=params(20),
        cost_estimate=cost(200_000_000),
        name="far_force",
    )(far_items, force_columns, low, high, far, low_density, high_density, far_density, push)

    force_above = to_below(force_low)
    force_below = to_above(force_high)
    force_returned = swap_tiles(force_far, tiles)

    local_force = pl.pallas_call(
        functools.partial(local_force_kernel, blocks),
        out_shape=f32(3, blocks, lanes),
        in_specs=[spec(smem)] + [spec(vmem)] * 3,
        out_specs=spec(vmem),
        scratch_shapes=fields(10) + sums(blocks),
        compiler_params=params(20),
        cost_estimate=cost(80_000_000),
        name="local_force",
    )(own_items, force_columns, force_table, pressed)

    acceleration = pl.pallas_call(
        functools.partial(final_kernel, blocks, faces, per_peer),
        out_shape=f32(3, blocks, lanes),
        in_specs=[spec(smem)] + [spec(vmem)] * 9,
        out_specs=spec(vmem),
        scratch_shapes=[vmem((blocks * 8, lanes), jnp.float32)],
        name="total",
    )(
        send_list,
        table,
        local_sum,
        far_sum,
        self_force,
        local_force,
        far_force,
        force_above,
        force_below,
        force_returned,
    )
    return (density, acceleration)


def solution(mesh):
    placed = (
        P(None, ("slab", "tile"), None),
        P(None, ("slab", "tile"), None),
        P(("slab", "tile"), None),
        P(("slab", "tile"), None),
        P(None, ("slab", "tile"), None),
        P(("slab", "tile")),
        P(("slab", "tile")),
        P(("slab", "tile"), None, None),
        P(("slab", "tile"), None),
        P(("slab", "tile"), None),
        P(("slab", "tile")),
    )
    return jax.shard_map(
        on_device,
        mesh=mesh,
        in_specs=placed,
        out_specs=(P(("slab", "tile"), None), P(None, ("slab", "tile"), None)),
        check_vma=False,
    )
```

```python
import functools
import math

import jax
import jax.numpy as jnp
from jax import lax
from jax.experimental import pallas as pl
from jax.experimental.pallas import tpu as pltpu
from jax.sharding import PartitionSpec as P

kernel_norm = 21.0 / (16.0 * math.pi)
softening = 0.01
tiny = 1e-30
lanes = 128
rows_item = 32
groups = rows_item // 8
batch = lanes // rows_item
halves = 2
pair_pad = 8
bf16 = jnp.bfloat16
vmem = pltpu.VMEM
smem = pltpu.SMEM


def spec(space):
    return pl.BlockSpec(memory_space=space)


def params(mib):
    return pltpu.CompilerParams(vmem_limit_bytes=mib * 1024 * 1024)


def column_of(row):
    number = row.shape[1]
    same = lax.broadcasted_iota(jnp.int32, (number, number), 0) == lax.broadcasted_iota(
        jnp.int32, (number, number), 1
    )
    return jnp.sum(jnp.where(same, row, 0.0), axis=1, keepdims=True)


def pack_kernel(
    blocks, faces, per_peer, send, pos, vel, mass, area, normal, flags_row, counts_row, table, picked, head, tail
):
    slot = lax.broadcasted_iota(jnp.int32, (blocks, lanes), 1).astype(jnp.float32)
    alive = slot < column_of(counts_row[...].astype(jnp.float32))
    wall_value = column_of(flags_row[...].astype(jnp.float32)) + jnp.zeros((blocks, lanes), jnp.float32)
    wall = wall_value > 0.5
    nx, ny, nz = normal[0], normal[1], normal[2]
    length = jnp.sqrt(nx * nx + ny * ny + nz * nz)
    weight = jnp.where(alive, jnp.where(wall, area[...], mass[...]), 0.0)
    wall_scale = weight / length
    parts = (nx, ny, nz)
    for c in range(3):
        table[pl.ds(c, blocks, stride=8), :] = 0.5 * pos[c]
        table[pl.ds(3 + c, blocks, stride=8), :] = jnp.where(wall, wall_scale * parts[c], vel[c])
    table[pl.ds(6, blocks, stride=8), :] = weight
    table[pl.ds(7, blocks, stride=8), :] = wall_value
    head[...] = table[0 : faces * 8, :]
    tail[...] = table[(blocks - faces) * 8 : blocks * 8, :]

    def pick(t, carry):
        for k in range(per_peer):
            source = pl.multiple_of(send[0, t, k] * 8, 8)
            at = pl.multiple_of((t * per_peer + k) * 8, 8)
            picked[pl.ds(at, 8), :] = table[pl.ds(source, 8), :]
        return carry

    lax.fori_loop(0, picked.shape[0] // (8 * per_peer), pick, 0, unroll=2)


def rounded(x):
    return x.astype(bf16).astype(jnp.float32)


def split3(x):
    high = rounded(x)
    rest = x - high
    middle = rounded(rest)
    return high, middle, rest - middle


def make_spread(spread):
    shape = spread.shape
    k = lax.broadcasted_iota(jnp.int32, shape, 0) & 31
    tile = lax.broadcasted_iota(jnp.int32, shape, 1) >> 7
    want = jnp.where(tile == 3, 6, jnp.where(tile > 3, tile - 1, tile))
    want = jnp.where(tile == 7, 7, want)
    hit = jnp.logical_and(jnp.logical_and(k < 24, (k & 7) == want), tile < 8)
    hit = jnp.logical_or(hit, jnp.logical_and(jnp.logical_and(k >= 24, k < 27), tile == 8))
    spread[...] = jnp.where(hit, 1.0, 0.0).astype(bf16)


def make_columns(blocks, table, last, columns, stage):
    lane = lax.broadcasted_iota(jnp.int32, (lanes, lanes), 1) >> 5
    for g in range(blocks // 4):
        for j in range(4):
            b = 4 * g + j
            for p, piece in enumerate(split3(table[8 * b : 8 * b + 8, :])):
                stage[32 * b + 8 * p : 32 * b + 8 * p + 8, :] = piece
            if last is None:
                stage[32 * b + 24 : 32 * b + 32, :] = jnp.zeros((8, lanes), jnp.float32)
            else:
                stage[32 * b + 24 : 32 * b + 32, :] = last[8 * b : 8 * b + 8, :]

    def some(g, carry):
        turned = stage[pl.ds(pl.multiple_of(g * lanes, lanes), lanes), :].T
        for j in range(4):
            columns[g * 4 + j] = jnp.where(lane == j, turned, 0.0).astype(bf16)
        return carry

    lax.fori_loop(0, blocks // 4, some, 0)
    columns[blocks] = jnp.zeros((lanes, lanes), bf16)


def put_items(items, at, code):
    for k in range(lanes // rows_item):
        items[at + k] = code | (k << 16)


def close_items(items, count, blocks):
    for k in range(2 * batch * halves):
        items[count + k] = jnp.int32(blocks)


def chunks(count):
    return (count + (rows_item - 1)) >> 5


def decode(code):
    first = code & 255
    second = (code >> 8) & 255
    row = pl.multiple_of((code >> 16) * rows_item, rows_item)
    return first, second, row


def wide(row):
    return jnp.broadcast_to(row, (8, lanes))


def spread_fields(columns, spread, wide_fields, tiles, decoded):
    left = jnp.concatenate([columns[first, pl.ds(row, rows_item), :] for first, second, row in decoded], axis=0)
    for t in range((tiles + 1) // 2):
        both = jnp.dot(left, spread[:, 256 * t : 256 * t + 256], preferred_element_type=jnp.float32)
        wide_fields[2 * t] = both[:, 0:lanes]
        wide_fields[2 * t + 1] = both[:, lanes : 2 * lanes]


def close_u(fields, rows):
    dx = fields[0] - rows[0]
    dy = fields[1] - rows[1]
    dz = fields[2] - rows[2]
    square = dx * dx + dy * dy + dz * dz
    safe = jnp.maximum(square, tiny)
    q = safe * lax.rsqrt(safe)
    u = jnp.maximum(1.0 - q, 0.0)
    return dx, dy, dz, square, u


def kernel_shape(u):
    u2 = u * u
    return (u2 * u2) * (5.0 - 4.0 * u)


def run_items(columns, spread, wide_fields, tiles, items, start, count, body, finish):
    def parts(it):
        for h in range(halves):
            yield h, [decode(items[start + (it * halves + h) * batch + k]) for k in range(batch)]

    def prepare(it):
        for h, decoded in parts(it):
            spread_fields(columns, spread, wide_fields[h], tiles, decoded)

    def step(it, carry):
        done = [(decoded, body(wide_fields[h], decoded)) for h, decoded in parts(it)]
        prepare(it + 1)
        for decoded, outs in done:
            finish(decoded, outs)
        return carry

    prepare(0)
    size = batch * halves
    lax.fori_loop(0, (count + size - 1) >> 3, step, 0)


def merge_lanes(values, first, lane):
    base = (first & 15) * 8
    total = jnp.zeros((8, lanes), jnp.float32)
    for c, value in enumerate(values):
        total = jnp.where(lane == base + c, value, total)
    return total


def merge_rows(values, sub, places):
    total = jnp.zeros((8, lanes), jnp.float32)
    for c, value in zip(places, values):
        total = jnp.where(sub == c, jnp.sum(value, axis=0, keepdims=True), total)
    return total


def add_sums(acc_first, acc_second, decoded, outs):
    for (first, second, row), (merged, tile) in zip(decoded, outs):
        if merged:
            slab = first >> 4
            for g in range(groups):
                acc_first[slab, pl.ds(row + 8 * g, 8), :] += merged[g]
        if tile is not None:
            at = pl.multiple_of(second * 8, 8)
            acc_second[pl.ds(at, 8), :] += tile


def density_body(source, kind, wide_fields, decoded):
    lane = lax.broadcasted_iota(jnp.int32, (8, lanes), 1)
    sub = lax.broadcasted_iota(jnp.int32, (8, lanes), 0)
    places = {"self": (0,), "local": (0,), "both": (0, 1, 2, 3), "second": (0, 4, 5, 6)}
    outs = []
    for k, (first, second, row) in enumerate(decoded):
        base = pl.multiple_of(second * 8, 8)
        rows = [wide(source[pl.ds(base + c, 1), :]) for c in range(3)]
        given = []
        if kind in ("both", "local", "first"):
            given = [wide(source[pl.ds(base + 6, 1), :])]
            if kind == "first":
                given += [wide(source[pl.ds(base + 3 + c, 1), :]) for c in range(3)]
        merged = []
        sums = None
        for g in range(groups):
            at = rows_item * k + 8 * g
            number = {"first": 3, "second": 7}.get(kind, 4)
            fields = [wide_fields[f, at : at + 8, :] for f in range(number)]
            dx, dy, dz, square, u = close_u(fields, rows)
            w = kernel_shape(u)
            if given:
                values = [jnp.sum(w * other, axis=1, keepdims=True) for other in given]
                merged.append(merge_lanes(values, first, lane))
            if kind != "first":
                back = [w * field for field in fields[3:]]
                if kind == "both":
                    slope = ((u * u) * u) * fields[3]
                    back += [slope * d for d in (dx, dy, dz)]
                sums = back if sums is None else [s + b for s, b in zip(sums, back)]
        outs.append((merged, merge_rows(sums, sub, places[kind]) if sums else None))
    return outs


def clear(ref, pieces):
    size = ref.shape[0] // pieces

    def some(k, carry):
        at = pl.multiple_of(k * size, size)
        ref[pl.ds(at, size)] = jnp.zeros((size,) + tuple(ref.shape[1:]), jnp.float32)
        return carry

    lax.fori_loop(0, pieces, some, 0)


def plane(ref, number, c):
    return ref[pl.ds(c, number, stride=8), :]


def first_rows(acc_first, turned, blocks):
    for s in range(blocks // 16):
        turned[s * lanes : (s + 1) * lanes, :] = acc_first[s].T


def run_density(columns, spread, fields, source, acc_first, acc_second, kind, items, start, count):
    run_items(
        columns,
        spread,
        fields,
        7 if kind == "second" else 4,
        items,
        start,
        count,
        functools.partial(density_body, source, kind),
        functools.partial(add_sums, acc_first, acc_second),
    )


def self_density_kernel(
    blocks,
    counts,
    flags,
    live,
    local_pairs,
    remote_pairs,
    table,
    columns,
    own,
    items,
    local_items,
    far_pairs,
    stage,
    spread,
    wide_a,
    wide_b,
    acc_second,
):
    make_columns(blocks, table, None, columns, stage)
    make_spread(spread)
    clear(acc_second, 4)
    zero = jnp.int32(0)

    def self_step(b, n):
        put_items(items, n, b | (b << 8))
        return n + chunks(counts[b]) * (1 - flags[b])

    count = lax.fori_loop(0, blocks, self_step, zero, unroll=8)
    close_items(items, count, blocks)
    items[items.shape[0] - 1] = count
    run_density(columns, spread, (wide_a, wide_b), table, None, acc_second, "self", items, 0, count)
    own[...] = plane(acc_second, blocks, 0)
    cap = local_items.shape[0] // 2

    def local_step(p, state):
        n_both, n_wall = state
        a = local_pairs[0, p]
        b = local_pairs[1, p]
        wall_b = flags[b]
        kinds = flags[a] + wall_b
        swap = jnp.where(kinds == 1, wall_b, (counts[b] < counts[a]).astype(jnp.int32)) > 0
        first = jnp.where(swap, b, a)
        second = jnp.where(swap, a, b)
        number = chunks(counts[first])
        put_items(local_items, jnp.where(kinds == 0, n_both, n_wall), first | (second << 8))
        return n_both + jnp.where(kinds == 0, number, 0), n_wall + jnp.where(kinds == 1, number, 0)

    n_both, n_wall = lax.fori_loop(0, local_pairs.shape[1], local_step, (zero, zero + cap), unroll=8)
    close_items(local_items, n_both, blocks)
    close_items(local_items, n_wall, blocks)
    local_items[cap - 1] = n_both
    local_items[2 * cap - 1] = n_wall - cap
    half = far_pairs.shape[0] // 2

    def remote_step(p, state):
        n_fluid, n_wall = state
        a = remote_pairs[0, p]
        j = remote_pairs[1, p]
        b = jnp.where(j < blocks, j, j - blocks)
        wall = flags[a]
        code = a | (b << 8) | (chunks(counts[a]) << 16)
        far_pairs[jnp.where(wall > 0, n_wall, n_fluid)] = code
        return n_fluid + 1 - wall, n_wall + wall

    n_fluid, n_wall = lax.fori_loop(0, live[0], remote_step, (zero, zero + half))
    far_pairs[half - 1] = n_fluid
    far_pairs[2 * half - 1] = n_wall - half
    for k in range(pair_pad):
        far_pairs[n_fluid + k] = zero
        far_pairs[n_wall + k] = zero


def local_density_kernel(
    blocks,
    items,
    table,
    columns,
    own,
    spread,
    wide_a,
    wide_b,
    acc_first,
    acc_second,
    turned,
):
    make_spread(spread)
    clear(acc_first, 1)
    clear(acc_second, 4)
    density = functools.partial(run_density, columns, spread, (wide_a, wide_b), table, acc_first, acc_second)
    cap = items.shape[0] // 2
    density("local", items, 0, items[cap - 1])
    density("second", items, cap, items[2 * cap - 1])
    first_rows(acc_first, turned, blocks)
    own[0] = plane(turned, blocks, 0) + plane(acc_second, blocks, 0)
    for c in range(1, 4):
        own[c] = plane(acc_second, blocks, 3 + c)


def rows_out(tiles, out, start, number):
    for k in range(number):
        out[4 * k : 4 * k + 4, :] = tiles[8 * (start + k) : 8 * (start + k) + 4, :]


def far_density_kernel(
    blocks,
    faces,
    far_pairs,
    columns,
    low,
    high,
    far,
    own,
    back_low,
    back_high,
    back_far,
    push,
    items,
    spread,
    wide_a,
    wide_b,
    acc_first,
    acc_second,
    turned,
    source,
    wall_rows,
    wall_flag,
    wall_items,
    sem,
):
    others = source.shape[0] // 8
    source[0 : faces * 8, :] = low[...]
    source[faces * 8 : 2 * faces * 8, :] = high[...]
    source[2 * faces * 8 :, :] = far[...]
    wall_rows[...] = plane(source, others, 7)
    copy = pltpu.make_async_copy(wall_rows, wall_flag, sem)
    copy.start()
    make_spread(spread)
    clear(acc_first, 1)
    clear(acc_second, 4)
    copy.wait()
    zero = jnp.int32(0)
    half = far_pairs.shape[0] // 2
    cap = items.shape[0] // 2

    def fluid_second(code):
        return wall_flag[(code >> 8) & 255, 0] < 0.5

    def wall_step(q, n):
        for k in range(pair_pad):
            code = far_pairs[half + q * pair_pad + k]
            put_items(wall_items, n, code & 65535)
            n = n + jnp.where(fluid_second(code), code >> 16, 0)
        return n

    def fluid_step(q, state):
        n_both, n_first = state
        for k in range(pair_pad):
            code = far_pairs[q * pair_pad + k]
            number = code >> 16
            fluid = fluid_second(code)
            put_items(items, jnp.where(fluid, n_both, n_first), code & 65535)
            n_both = n_both + jnp.where(fluid, number, 0)
            n_first = n_first + jnp.where(fluid, 0, number)
        return n_both, n_first

    def passes(pairs):
        return (pairs + (pair_pad - 1)) >> 3

    n_both, n_first = lax.fori_loop(0, passes(far_pairs[half - 1]), fluid_step, (zero, zero + cap))
    close_items(items, n_both, blocks)
    close_items(items, n_first, blocks)
    items[cap - 1] = n_both
    n_second = lax.fori_loop(0, passes(far_pairs[2 * half - 1]), wall_step, zero)
    close_items(wall_items, n_second, blocks)
    density = functools.partial(run_density, columns, spread, (wide_a, wide_b), source, acc_first, acc_second)
    density("second", wall_items, 0, n_second)
    density("both", items, 0, n_both)
    density("first", items, cap, n_first - cap)
    first_rows(acc_first, turned, blocks)
    for c in range(4):
        own[c] = plane(turned, blocks, c)
    rows_out(acc_second, back_low, 0, faces)
    rows_out(acc_second, back_high, faces, faces)
    rows_out(acc_second, back_far, 2 * faces, others - 2 * faces)
    for c in range(3):
        push[c] = plane(acc_second, others, 4 + c)


def fluid_mask(blocks, table):
    return jnp.logical_and(plane(table, blocks, 6) > 0.0, plane(table, blocks, 7) < 0.5)


def density_kernel(
    blocks,
    faces,
    per_peer,
    send,
    table,
    self_sum,
    local_sum,
    far_sum,
    from_above,
    from_below,
    returned,
    density,
    slopes,
    total,
):
    total[pl.ds(0, blocks, stride=8), :] = self_sum[...] + local_sum[0] + far_sum[0]
    for c in range(1, 8):
        total[pl.ds(c, blocks, stride=8), :] = jnp.zeros((blocks, lanes), jnp.float32)
    for k in range(faces):
        at = 8 * (blocks - faces + k)
        total[at : at + 4, :] += from_above[4 * k : 4 * k + 4, :]
        total[8 * k : 8 * k + 4, :] += from_below[4 * k : 4 * k + 4, :]

    def give(t, carry):
        for k in range(per_peer):
            at = pl.multiple_of(send[0, t, k] * 8, 8)
            source = pl.multiple_of((t * per_peer + k) * 4, 4)
            total[pl.ds(at, 4), :] += returned[pl.ds(source, 4), :]
        return carry

    lax.fori_loop(0, send.shape[1], give, 0, unroll=2)
    density[...] = jnp.where(fluid_mask(blocks, table), kernel_norm * plane(total, blocks, 0), 0.0)
    for c in range(3):
        slopes[c] = plane(total, blocks, 1 + c)


def force_fields(source, density, number, pressed):
    mass = plane(source, number, 6)
    rho = jnp.where(mass > 0.0, density, 1.0)
    inverse = 1.0 / jnp.where(rho > 0.0, rho, 1.0)
    scaled = mass * inverse
    source[pl.ds(7, number, stride=8), :] = scaled
    press = 10.0 * (rho - 1.0) * inverse * scaled
    pressed[...] = press
    return press


def force_body(source, pressed, kind, wide_fields, decoded):
    lane = lax.broadcasted_iota(jnp.int32, (8, lanes), 1)
    sub = lax.broadcasted_iota(jnp.int32, (8, lanes), 0)
    outs = []
    for k, (first, second, row) in enumerate(decoded):
        base = pl.multiple_of(second * 8, 8)
        rows = [wide(source[pl.ds(base + c, 1), :]) for c in range(6 if kind == "second" else 8)]
        if kind != "second":
            press = wide(pressed[pl.ds(second, 1), :])
        merged = []
        sums = None
        for g in range(groups):
            at = rows_item * k + 8 * g
            fields = [wide_fields[f, at : at + 8, :] for f in range(9)]
            dx, dy, dz, square, u = close_u(fields, rows)
            u3 = (u * u) * u
            damp = u3 * (square * (1.0 / (square + 0.25 * softening)))
            if kind == "second":
                damp = damp * fields[7]
                pull = u3 * fields[8]
                values = [damp * (fields[4 + c] - rows[3 + c]) for c in range(3)]
                values += [pull * d for d in (dx, dy, dz)]
            else:
                damp = damp * (fields[7] * rows[7])
                pull = u3 * (fields[8] * rows[6] + fields[3] * press)
                values = [
                    pull * d - damp * (fields[4 + c] - rows[3 + c]) for c, d in enumerate((dx, dy, dz))
                ]
            if kind in ("local", "first"):
                merged.append(
                    merge_lanes([jnp.sum(v, axis=1, keepdims=True) for v in values], first, lane)
                )
            if kind != "first":
                sums = values if sums is None else [s + v for s, v in zip(sums, values)]
        outs.append((merged, merge_rows(sums, sub, range(1, 7)) if sums else None))
    return outs


def run_force(columns, spread, fields, source, pressed, acc_first, acc_second, kind, items, cap):
    run_items(
        columns,
        spread,
        fields,
        9,
        items,
        0,
        items[cap - 1],
        functools.partial(force_body, source, pressed, kind),
        functools.partial(add_sums, acc_first, acc_second),
    )


def far_send_kernel(
    blocks,
    faces,
    per_peer,
    send,
    items,
    table,
    density,
    low,
    high,
    far,
    push,
    columns,
    own_source,
    pressed,
    out_low,
    out_high,
    out_far,
    stage,
    last,
    source,
    spread,
    wide_a,
    wide_b,
    acc_second,
):
    others = source.shape[0] // 8
    source[0 : faces * 8, :] = low[...]
    source[faces * 8 : 2 * faces * 8, :] = high[...]
    source[2 * faces * 8 :, :] = far[...]
    own_source[...] = table[...]
    press = force_fields(own_source, density[...], blocks, pressed)
    last[...] = jnp.zeros(last.shape, jnp.float32)
    for p, piece in enumerate(split3(press)):
        last[pl.ds(p, blocks, stride=8), :] = piece
    make_columns(blocks, own_source, last, columns, stage)
    make_spread(spread)
    clear(acc_second, 4)
    run_force(columns, spread, (wide_a, wide_b), source, None, None, acc_second, "second", items, items.shape[0] // 2)
    for c in range(3):
        acc_second[pl.ds(4 + c, others, stride=8), :] = push[c] - plane(acc_second, others, 4 + c)
    acc_second[pl.ds(0, faces, stride=8), :] = density[0:faces, :]
    acc_second[pl.ds(8 * faces, faces, stride=8), :] = density[blocks - faces :, :]

    def pick(t, carry):
        for k in range(per_peer):
            at = 8 * (2 * faces + t * per_peer + k)
            acc_second[pl.ds(at, 1), :] = density[pl.ds(send[0, t, k], 1), :]
        return carry

    lax.fori_loop(0, send.shape[1], pick, 0, unroll=4)
    out_low[...] = acc_second[0 : 8 * faces, :]
    out_high[...] = acc_second[8 * faces : 16 * faces, :]
    out_far[...] = acc_second[16 * faces :, :]


def own_force_kernel(
    blocks,
    self_items,
    both_items,
    columns,
    source,
    pressed,
    own,
    spread,
    wide_a,
    wide_b,
    acc_first,
    acc_second,
    turned,
):
    make_spread(spread)
    clear(acc_first, 1)
    clear(acc_second, 4)
    force = functools.partial(
        run_force, columns, spread, (wide_a, wide_b), source, pressed, acc_first, acc_second
    )
    force("self", self_items, self_items.shape[0])
    force("local", both_items, both_items.shape[0] // 2)
    first_rows(acc_first, turned, blocks)
    for c in range(3):
        own[c] = plane(turned, blocks, c) - plane(acc_second, blocks, 1 + c)


def far_force_kernel(
    blocks,
    faces,
    items,
    columns,
    low,
    high,
    far,
    from_below,
    from_above,
    returned,
    own,
    source,
    source_density,
    pressed,
    spread,
    wide_a,
    wide_b,
    acc_first,
    turned,
):
    others = source.shape[0] // 8
    source[0 : faces * 8, :] = low[...]
    source[faces * 8 : 2 * faces * 8, :] = high[...]
    source[2 * faces * 8 :, :] = far[...]
    source_density[0:faces, :] = plane(from_below, faces, 0)
    source_density[faces : 2 * faces, :] = plane(from_above, faces, 0)
    source_density[2 * faces :, :] = plane(returned, others - 2 * faces, 0)
    force_fields(source, source_density[...], others, pressed)
    make_spread(spread)
    clear(acc_first, 1)
    run_force(columns, spread, (wide_a, wide_b), source, pressed, acc_first, None, "first", items, items.shape[0] // 2)
    first_rows(acc_first, turned, blocks)
    for c in range(3):
        own[c] = plane(turned, blocks, c)


def final_kernel(
    blocks,
    faces,
    per_peer,
    send,
    table,
    density,
    slopes,
    local_sum,
    far_sum,
    own_force,
    far_force,
    from_above,
    from_below,
    returned,
    out,
    total,
):
    total[...] = jnp.zeros(total.shape, jnp.float32)
    total[8 * (blocks - faces) :, :] += from_above[...]
    total[0 : 8 * faces, :] += from_below[...]

    def give(t, carry):
        for k in range(per_peer):
            at = pl.multiple_of(send[0, t, k] * 8, 8)
            source = pl.multiple_of((t * per_peer + k) * 8, 8)
            total[pl.ds(at, 8), :] += returned[pl.ds(source, 8), :]
        return carry

    lax.fori_loop(0, send.shape[1], give, 0, unroll=2)
    fluid = fluid_mask(blocks, table)
    mass = plane(table, blocks, 6)
    over_mass = 1.0 / jnp.where(mass > 0.0, mass, 1.0)
    over_rho = 1.0 / jnp.where(fluid, density[...], 1.0)
    press = jnp.where(fluid, 10.0 * (density[...] - 1.0) * over_rho * over_rho, 0.0)
    for c in range(3):
        force = (own_force[c] + far_force[c]) * over_mass
        force = force + local_sum[1 + c] + far_sum[1 + c]
        force = force + plane(total, blocks, 1 + c) * over_rho + plane(total, blocks, 4 + c)
        out[c] = jnp.where(fluid, kernel_norm * (force - press * slopes[c]), 0.0)


def f32(*shape):
    return jax.ShapeDtypeStruct(shape, jnp.float32)


def i32(*shape):
    return jax.ShapeDtypeStruct(shape, jnp.int32)


def to_above(shard):
    count = lax.axis_size("slab")
    return lax.ppermute(shard, "slab", [(i, i + 1) for i in range(count - 1)])


def to_below(shard):
    count = lax.axis_size("slab")
    return lax.ppermute(shard, "slab", [(i + 1, i) for i in range(count - 1)])


def swap_tiles(rows, tiles):
    parts = rows.reshape(tiles, rows.shape[0] // tiles, lanes)
    return lax.all_to_all(parts, "tile", split_axis=0, concat_axis=0, tiled=True).reshape(rows.shape)


def on_device(
    positions,
    velocities,
    masses,
    wall_areas,
    normals,
    wall_flags,
    counts,
    send_list,
    local_pairs,
    remote_pairs,
    remote_live,
):
    blocks = positions.shape[1]
    faces = blocks // 4
    tiles = lax.axis_size("tile")
    per_peer = send_list.shape[2]
    offered = send_list.shape[1] * per_peer
    others = 2 * faces + offered
    n_local = local_pairs.shape[0]
    n_remote = remote_pairs.shape[0]
    per = lanes // rows_item
    spare = 3 * batch * halves
    self_cap = per * blocks + spare
    own_cap = per * n_local + spare
    far_cap = per * n_remote + spare
    pair_cap = n_remote + 2 * pair_pad
    columns_shape = jax.ShapeDtypeStruct((blocks + 1, lanes, lanes), bf16)
    stage = vmem((blocks * 32, lanes), jnp.float32)

    def fields(number):
        return [vmem((lanes, 128 * number), bf16)] + [vmem((number, lanes, lanes), jnp.float32)] * 2

    acc_first = vmem((blocks // 16 + 1, lanes, lanes), jnp.float32)
    turned = vmem((blocks * 8, lanes), jnp.float32)

    def tiles_of(number):
        return vmem((number * 8, lanes), jnp.float32)

    def cost(flops):
        return pl.CostEstimate(flops=flops, bytes_accessed=400_000, transcendentals=0)

    table, picked, head, tail = pl.pallas_call(
        functools.partial(pack_kernel, blocks, faces, per_peer),
        out_shape=(f32(blocks * 8, lanes), f32(offered * 8, lanes), f32(faces * 8, lanes), f32(faces * 8, lanes)),
        in_specs=[spec(smem)] + [spec(vmem)] * 7,
        out_specs=[spec(vmem)] * 4,
        compiler_params=params(8),
        name="pack",
    )(
        send_list,
        positions,
        velocities,
        masses,
        wall_areas,
        normals,
        wall_flags[None, :],
        counts[None, :],
    )
    low = to_above(tail)
    high = to_below(head)
    far = swap_tiles(picked, tiles)

    columns, self_sum, self_items, own_items, far_pairs = pl.pallas_call(
        functools.partial(self_density_kernel, blocks),
        out_shape=(
            columns_shape,
            f32(blocks, lanes),
            i32(self_cap),
            i32(2 * own_cap),
            i32(2 * pair_cap),
        ),
        in_specs=[spec(smem)] * 5 + [spec(vmem)],
        out_specs=[spec(vmem)] * 2 + [spec(smem)] * 3,
        scratch_shapes=[stage] + fields(8) + [tiles_of(blocks)],
        compiler_params=params(12),
        cost_estimate=cost(40_000_000),
        name="self_density",
    )(counts, wall_flags, remote_live, local_pairs.T, remote_pairs.T, table)

    far_sum, back_low, back_high, back_far, push, far_items = pl.pallas_call(
        functools.partial(far_density_kernel, blocks, faces),
        out_shape=(
            f32(4, blocks, lanes),
            f32(faces * 4, lanes),
            f32(faces * 4, lanes),
            f32(offered * 4, lanes),
            f32(3, others, lanes),
            i32(2 * far_cap),
        ),
        in_specs=[spec(smem)] + [spec(vmem)] * 4,
        out_specs=[spec(vmem)] * 5 + [spec(smem)],
        scratch_shapes=fields(8)
        + [acc_first, tiles_of(others), turned]
        + [
            tiles_of(others),
            vmem((others, lanes), jnp.float32),
            smem((others, lanes), jnp.float32),
            smem((far_cap,), jnp.int32),
            pltpu.SemaphoreType.DMA,
        ],
        compiler_params=params(12),
        cost_estimate=cost(100_000_000),
        name="far_density",
    )(far_pairs, columns, low, high, far)

    from_above = to_below(back_low)
    from_below = to_above(back_high)
    returned = swap_tiles(back_far, tiles)

    local_sum = pl.pallas_call(
        functools.partial(local_density_kernel, blocks),
        out_shape=f32(4, blocks, lanes),
        in_specs=[spec(smem)] + [spec(vmem)] * 2,
        out_specs=spec(vmem),
        scratch_shapes=fields(8) + [acc_first, tiles_of(blocks), turned],
        compiler_params=params(12),
        cost_estimate=cost(40_000_000),
        name="local_density",
    )(own_items, table, columns)

    density, slopes = pl.pallas_call(
        functools.partial(density_kernel, blocks, faces, per_peer),
        out_shape=(f32(blocks, lanes), f32(3, blocks, lanes)),
        in_specs=[spec(smem)] + [spec(vmem)] * 7,
        out_specs=[spec(vmem)] * 2,
        scratch_shapes=[tiles_of(blocks)],
        compiler_params=params(8),
        name="density",
    )(send_list, table, self_sum, local_sum, far_sum, from_above, from_below, returned)

    force_columns, force_table, pressed, out_low, out_high, out_far = pl.pallas_call(
        functools.partial(far_send_kernel, blocks, faces, per_peer),
        out_shape=(
            columns_shape,
            f32(blocks * 8, lanes),
            f32(blocks, lanes),
            f32(faces * 8, lanes),
            f32(faces * 8, lanes),
            f32(offered * 8, lanes),
        ),
        in_specs=[spec(smem)] * 2 + [spec(vmem)] * 6,
        out_specs=[spec(vmem)] * 6,
        scratch_shapes=[stage, tiles_of(blocks), tiles_of(others)] + fields(10) + [tiles_of(others)],
        compiler_params=params(12),
        cost_estimate=cost(100_000_000),
        name="far_send",
    )(send_list, far_items, table, density, low, high, far, push)

    force_above = to_below(out_low)
    force_below = to_above(out_high)
    force_far = swap_tiles(out_far, tiles)

    own_force = pl.pallas_call(
        functools.partial(own_force_kernel, blocks),
        out_shape=f32(3, blocks, lanes),
        in_specs=[spec(smem)] * 2 + [spec(vmem)] * 3,
        out_specs=spec(vmem),
        scratch_shapes=fields(10) + [acc_first, tiles_of(blocks), turned],
        compiler_params=params(12),
        cost_estimate=cost(80_000_000),
        name="own_force",
    )(self_items, own_items, force_columns, force_table, pressed)

    far_force = pl.pallas_call(
        functools.partial(far_force_kernel, blocks, faces),
        out_shape=f32(3, blocks, lanes),
        in_specs=[spec(smem)] + [spec(vmem)] * 7,
        out_specs=spec(vmem),
        scratch_shapes=[
            tiles_of(others),
            vmem((others, lanes), jnp.float32),
            vmem((others, lanes), jnp.float32),
        ]
        + fields(10)
        + [acc_first, turned],
        compiler_params=params(12),
        cost_estimate=cost(100_000_000),
        name="far_force",
    )(far_items, force_columns, low, high, far, force_below, force_above, force_far)

    acceleration = pl.pallas_call(
        functools.partial(final_kernel, blocks, faces, per_peer),
        out_shape=f32(3, blocks, lanes),
        in_specs=[spec(smem)] + [spec(vmem)] * 10,
        out_specs=spec(vmem),
        scratch_shapes=[tiles_of(blocks)],
        compiler_params=params(8),
        name="total",
    )(
        send_list,
        table,
        density,
        slopes,
        local_sum,
        far_sum,
        own_force,
        far_force,
        force_above,
        force_below,
        force_far,
    )
    return (density, acceleration)


def solution(mesh):
    placed = (
        P(None, ("slab", "tile"), None),
        P(None, ("slab", "tile"), None),
        P(("slab", "tile"), None),
        P(("slab", "tile"), None),
        P(None, ("slab", "tile"), None),
        P(("slab", "tile")),
        P(("slab", "tile")),
        P(("slab", "tile"), None, None),
        P(("slab", "tile"), None),
        P(("slab", "tile"), None),
        P(("slab", "tile")),
    )
    return jax.shard_map(
        on_device,
        mesh=mesh,
        in_specs=placed,
        out_specs=(P(("slab", "tile"), None), P(None, ("slab", "tile"), None)),
        check_vma=False,
    )
```

```python
import functools
import math

import jax
import jax.numpy as jnp
from jax import lax
from jax.experimental import pallas as pl
from jax.experimental.pallas import tpu as pltpu
from jax.sharding import PartitionSpec as P

kernel_norm = 21.0 / (16.0 * math.pi)
softening = 0.01
tiny = 1e-30
lanes = 128
rows_item = 32
groups = rows_item // 8
batch = lanes // rows_item
density_halves = 4
force_halves = 2
pair_pad = 8
grant_mib = 64
bf16 = jnp.bfloat16
vmem = pltpu.VMEM
smem = pltpu.SMEM


def spec(space):
    return pl.BlockSpec(memory_space=space)


def params(mib):
    return pltpu.CompilerParams(vmem_limit_bytes=mib * 1024 * 1024)


def column_of(row):
    number = row.shape[1]
    same = lax.broadcasted_iota(jnp.int32, (number, number), 0) == lax.broadcasted_iota(
        jnp.int32, (number, number), 1
    )
    return jnp.sum(jnp.where(same, row, 0.0), axis=1, keepdims=True)


def pack_kernel(
    blocks, faces, per_peer, send, pos, vel, mass, area, normal, flags_row, counts_row, table, picked, head, tail
):
    slot = lax.broadcasted_iota(jnp.int32, (blocks, lanes), 1).astype(jnp.float32)
    alive = slot < column_of(counts_row[...].astype(jnp.float32))
    wall_value = column_of(flags_row[...].astype(jnp.float32)) + jnp.zeros((blocks, lanes), jnp.float32)
    wall = wall_value > 0.5
    nx, ny, nz = normal[0], normal[1], normal[2]
    length = jnp.sqrt(nx * nx + ny * ny + nz * nz)
    weight = jnp.where(alive, jnp.where(wall, area[...], mass[...]), 0.0)
    wall_scale = weight / length
    parts = (nx, ny, nz)
    for c in range(3):
        table[pl.ds(c, blocks, stride=8), :] = 0.5 * pos[c]
        table[pl.ds(3 + c, blocks, stride=8), :] = jnp.where(wall, wall_scale * parts[c], vel[c])
    table[pl.ds(6, blocks, stride=8), :] = weight
    table[pl.ds(7, blocks, stride=8), :] = wall_value
    head[...] = table[0 : faces * 8, :]
    tail[...] = table[(blocks - faces) * 8 : blocks * 8, :]

    def pick(t, carry):
        for k in range(per_peer):
            source = pl.multiple_of(send[0, t, k] * 8, 8)
            at = pl.multiple_of((t * per_peer + k) * 8, 8)
            picked[pl.ds(at, 8), :] = table[pl.ds(source, 8), :]
        return carry

    lax.fori_loop(0, picked.shape[0] // (8 * per_peer), pick, 0, unroll=2)


def rounded(x):
    return x.astype(bf16).astype(jnp.float32)


def split3(x):
    high = rounded(x)
    rest = x - high
    middle = rounded(rest)
    return high, middle, rest - middle


def make_spread(spread):
    shape = spread.shape
    k = lax.broadcasted_iota(jnp.int32, shape, 0) & 31
    tile = lax.broadcasted_iota(jnp.int32, shape, 1) >> 7
    want = jnp.where(tile == 3, 6, jnp.where(tile > 3, tile - 1, tile))
    want = jnp.where(tile == 7, 7, want)
    hit = jnp.logical_and(jnp.logical_and(k < 24, (k & 7) == want), tile < 8)
    hit = jnp.logical_or(hit, jnp.logical_and(jnp.logical_and(k >= 24, k < 27), tile == 8))
    spread[...] = jnp.where(hit, 1.0, 0.0).astype(bf16)


def make_columns(blocks, table, last, columns, stage):
    lane = lax.broadcasted_iota(jnp.int32, (lanes, lanes), 1) >> 5
    for g in range(blocks // 4):
        for j in range(4):
            b = 4 * g + j
            for p, piece in enumerate(split3(table[8 * b : 8 * b + 8, :])):
                stage[32 * b + 8 * p : 32 * b + 8 * p + 8, :] = piece
            if last is None:
                stage[32 * b + 24 : 32 * b + 32, :] = jnp.zeros((8, lanes), jnp.float32)
            else:
                stage[32 * b + 24 : 32 * b + 32, :] = last[8 * b : 8 * b + 8, :]

    def some(g, carry):
        turned = stage[pl.ds(pl.multiple_of(g * lanes, lanes), lanes), :].T
        for j in range(4):
            columns[g * 4 + j] = jnp.where(lane == j, turned, 0.0).astype(bf16)
        return carry

    lax.fori_loop(0, blocks // 4, some, 0)
    columns[blocks] = jnp.zeros((lanes, lanes), bf16)


def put_items(items, at, code):
    for k in range(lanes // rows_item):
        items[at + k] = code | (k << 16)


def close_items(items, count, blocks):
    for k in range(2 * batch * density_halves):
        items[count + k] = jnp.int32(blocks)


def chunks(count):
    return (count + (rows_item - 1)) >> 5


def decode(code):
    first = code & 255
    second = (code >> 8) & 255
    row = pl.multiple_of((code >> 16) * rows_item, rows_item)
    return first, second, row


def wide(row):
    return jnp.broadcast_to(row, (8, lanes))


def spread_fields(columns, spread, wide_fields, tiles, decoded):
    left = jnp.concatenate([columns[first, pl.ds(row, rows_item), :] for first, second, row in decoded], axis=0)
    for t in range((tiles + 1) // 2):
        both = jnp.dot(left, spread[:, 256 * t : 256 * t + 256], preferred_element_type=jnp.float32)
        wide_fields[2 * t] = both[:, 0:lanes]
        wide_fields[2 * t + 1] = both[:, lanes : 2 * lanes]


def close_u(fields, rows):
    dx = fields[0] - rows[0]
    dy = fields[1] - rows[1]
    dz = fields[2] - rows[2]
    square = dx * dx + dy * dy + dz * dz
    safe = jnp.maximum(square, tiny)
    q = safe * lax.rsqrt(safe)
    u = jnp.maximum(1.0 - q, 0.0)
    return dx, dy, dz, square, u


def kernel_shape(u):
    u2 = u * u
    return (u2 * u2) * (5.0 - 4.0 * u)


def run_items(columns, spread, wide_fields, tiles, items, start, count, body, finish):
    halves = wide_fields.shape[0]
    size = batch * halves

    def parts(it):
        for h in range(halves):
            yield h, [decode(items[start + (it * halves + h) * batch + k]) for k in range(batch)]

    def prepare(it):
        for h, decoded in parts(it):
            spread_fields(columns, spread, wide_fields.at[h], tiles, decoded)

    def step(it, carry):
        done = [(decoded, body(wide_fields.at[h], decoded)) for h, decoded in parts(it)]
        prepare(it + 1)
        for decoded, outs in done:
            finish(decoded, outs)
        return carry

    prepare(0)
    lax.fori_loop(0, (count + size - 1) >> (size.bit_length() - 1), step, 0)


def merge_lanes(values, first, lane):
    base = (first & 15) * 8
    total = jnp.zeros((8, lanes), jnp.float32)
    for c, value in enumerate(values):
        total = jnp.where(lane == base + c, value, total)
    return total


def merge_rows(values, sub, places):
    total = jnp.zeros((8, lanes), jnp.float32)
    for c, value in zip(places, values):
        total = jnp.where(sub == c, jnp.sum(value, axis=0, keepdims=True), total)
    return total


def add_sums(acc_first, acc_second, decoded, outs):
    for (first, second, row), (merged, tile) in zip(decoded, outs):
        if merged:
            slab = first >> 4
            for g in range(groups):
                acc_first[slab, pl.ds(row + 8 * g, 8), :] += merged[g]
        if tile is not None:
            at = pl.multiple_of(second * 8, 8)
            acc_second[pl.ds(at, 8), :] += tile


def density_body(source, kind, wide_fields, decoded):
    lane = lax.broadcasted_iota(jnp.int32, (8, lanes), 1)
    sub = lax.broadcasted_iota(jnp.int32, (8, lanes), 0)
    places = {"self": (0,), "local": (0,), "both": (0, 1, 2, 3), "second": (0, 4, 5, 6)}
    outs = []
    for k, (first, second, row) in enumerate(decoded):
        base = pl.multiple_of(second * 8, 8)
        rows = [wide(source[pl.ds(base + c, 1), :]) for c in range(3)]
        given = []
        if kind in ("both", "local", "first"):
            given = [wide(source[pl.ds(base + 6, 1), :])]
            if kind == "first":
                given += [wide(source[pl.ds(base + 3 + c, 1), :]) for c in range(3)]
        merged = []
        sums = None
        for g in range(groups):
            at = rows_item * k + 8 * g
            number = {"first": 3, "second": 7}.get(kind, 4)
            fields = [wide_fields[f, at : at + 8, :] for f in range(number)]
            dx, dy, dz, square, u = close_u(fields, rows)
            w = kernel_shape(u)
            if given:
                values = [jnp.sum(w * other, axis=1, keepdims=True) for other in given]
                merged.append(merge_lanes(values, first, lane))
            if kind != "first":
                back = [w * field for field in fields[3:]]
                if kind == "both":
                    slope = ((u * u) * u) * fields[3]
                    back += [slope * d for d in (dx, dy, dz)]
                sums = back if sums is None else [s + b for s, b in zip(sums, back)]
        outs.append((merged, merge_rows(sums, sub, places[kind]) if sums else None))
    return outs


def clear(ref, pieces):
    size = ref.shape[0] // pieces

    def some(k, carry):
        at = pl.multiple_of(k * size, size)
        ref[pl.ds(at, size)] = jnp.zeros((size,) + tuple(ref.shape[1:]), jnp.float32)
        return carry

    lax.fori_loop(0, pieces, some, 0)


def plane(ref, number, c):
    return ref[pl.ds(c, number, stride=8), :]


def first_rows(acc_first, turned, blocks):
    for s in range(blocks // 16):
        turned[s * lanes : (s + 1) * lanes, :] = acc_first[s].T


def run_density(columns, spread, fields, source, acc_first, acc_second, kind, items, start, count):
    run_items(
        columns,
        spread,
        fields,
        7 if kind == "second" else 4,
        items,
        start,
        count,
        functools.partial(density_body, source, kind),
        functools.partial(add_sums, acc_first, acc_second),
    )


def self_density_kernel(
    blocks,
    counts,
    flags,
    live,
    local_pairs,
    remote_pairs,
    table,
    columns,
    own,
    items,
    local_items,
    far_pairs,
    stage,
    spread,
    wide_fields,
    acc_second,
):
    make_columns(blocks, table, None, columns, stage)
    make_spread(spread)
    clear(acc_second, 4)
    zero = jnp.int32(0)

    def self_step(b, n):
        put_items(items, n, b | (b << 8))
        return n + chunks(counts[b]) * (1 - flags[b])

    count = lax.fori_loop(0, blocks, self_step, zero, unroll=8)
    close_items(items, count, blocks)
    items[items.shape[0] - 1] = count
    run_density(columns, spread, wide_fields, table, None, acc_second, "self", items, 0, count)
    own[...] = plane(acc_second, blocks, 0)
    cap = local_items.shape[0] // 2

    def local_step(p, state):
        n_both, n_wall = state
        a = local_pairs[0, p]
        b = local_pairs[1, p]
        wall_b = flags[b]
        kinds = flags[a] + wall_b
        swap = jnp.where(kinds == 1, wall_b, (counts[b] < counts[a]).astype(jnp.int32)) > 0
        first = jnp.where(swap, b, a)
        second = jnp.where(swap, a, b)
        number = chunks(counts[first])
        put_items(local_items, jnp.where(kinds == 0, n_both, n_wall), first | (second << 8))
        return n_both + jnp.where(kinds == 0, number, 0), n_wall + jnp.where(kinds == 1, number, 0)

    n_both, n_wall = lax.fori_loop(0, local_pairs.shape[1], local_step, (zero, zero + cap), unroll=8)
    close_items(local_items, n_both, blocks)
    close_items(local_items, n_wall, blocks)
    local_items[cap - 1] = n_both
    local_items[2 * cap - 1] = n_wall - cap
    half = far_pairs.shape[0] // 2

    def remote_step(p, state):
        n_fluid, n_wall = state
        a = remote_pairs[0, p]
        j = remote_pairs[1, p]
        b = jnp.where(j < blocks, j, j - blocks)
        wall = flags[a]
        code = a | (b << 8) | (chunks(counts[a]) << 16)
        far_pairs[jnp.where(wall > 0, n_wall, n_fluid)] = code
        return n_fluid + 1 - wall, n_wall + wall

    n_fluid, n_wall = lax.fori_loop(0, live[0], remote_step, (zero, zero + half))
    far_pairs[half - 1] = n_fluid
    far_pairs[2 * half - 1] = n_wall - half
    for k in range(pair_pad):
        far_pairs[n_fluid + k] = zero
        far_pairs[n_wall + k] = zero


def local_density_kernel(
    blocks,
    items,
    table,
    columns,
    own,
    spread,
    wide_fields,
    acc_first,
    acc_second,
    turned,
):
    make_spread(spread)
    clear(acc_first, 1)
    clear(acc_second, 4)
    density = functools.partial(run_density, columns, spread, wide_fields, table, acc_first, acc_second)
    cap = items.shape[0] // 2
    density("local", items, 0, items[cap - 1])
    density("second", items, cap, items[2 * cap - 1])
    first_rows(acc_first, turned, blocks)
    own[0] = plane(turned, blocks, 0) + plane(acc_second, blocks, 0)
    for c in range(1, 4):
        own[c] = plane(acc_second, blocks, 3 + c)


def rows_out(tiles, out, start, number):
    for k in range(number):
        out[4 * k : 4 * k + 4, :] = tiles[8 * (start + k) : 8 * (start + k) + 4, :]


def far_density_kernel(
    blocks,
    faces,
    far_pairs,
    columns,
    low,
    high,
    far,
    own,
    back_low,
    back_high,
    back_far,
    push,
    items,
    spread,
    wide_fields,
    acc_first,
    acc_second,
    turned,
    source,
    wall_rows,
    wall_flag,
    wall_items,
    sem,
):
    others = source.shape[0] // 8
    source[0 : faces * 8, :] = low[...]
    source[faces * 8 : 2 * faces * 8, :] = high[...]
    source[2 * faces * 8 :, :] = far[...]
    wall_rows[...] = plane(source, others, 7)
    copy = pltpu.make_async_copy(wall_rows, wall_flag, sem)
    copy.start()
    make_spread(spread)
    clear(acc_first, 1)
    clear(acc_second, 4)
    copy.wait()
    zero = jnp.int32(0)
    half = far_pairs.shape[0] // 2
    cap = items.shape[0] // 2

    def fluid_second(code):
        return wall_flag[(code >> 8) & 255, 0] < 0.5

    def wall_step(q, n):
        for k in range(pair_pad):
            code = far_pairs[half + q * pair_pad + k]
            put_items(wall_items, n, code & 65535)
            n = n + jnp.where(fluid_second(code), code >> 16, 0)
        return n

    def fluid_step(q, state):
        n_both, n_first = state
        for k in range(pair_pad):
            code = far_pairs[q * pair_pad + k]
            number = code >> 16
            fluid = fluid_second(code)
            put_items(items, jnp.where(fluid, n_both, n_first), code & 65535)
            n_both = n_both + jnp.where(fluid, number, 0)
            n_first = n_first + jnp.where(fluid, 0, number)
        return n_both, n_first

    def passes(pairs):
        return (pairs + (pair_pad - 1)) >> 3

    n_both, n_first = lax.fori_loop(0, passes(far_pairs[half - 1]), fluid_step, (zero, zero + cap))
    close_items(items, n_both, blocks)
    close_items(items, n_first, blocks)
    items[cap - 1] = n_both
    n_second = lax.fori_loop(0, passes(far_pairs[2 * half - 1]), wall_step, zero)
    close_items(wall_items, n_second, blocks)
    density = functools.partial(run_density, columns, spread, wide_fields, source, acc_first, acc_second)
    density("second", wall_items, 0, n_second)
    density("both", items, 0, n_both)
    density("first", items, cap, n_first - cap)
    first_rows(acc_first, turned, blocks)
    for c in range(4):
        own[c] = plane(turned, blocks, c)
    rows_out(acc_second, back_low, 0, faces)
    rows_out(acc_second, back_high, faces, faces)
    rows_out(acc_second, back_far, 2 * faces, others - 2 * faces)
    for c in range(3):
        push[c] = plane(acc_second, others, 4 + c)


def fluid_mask(blocks, table):
    return jnp.logical_and(plane(table, blocks, 6) > 0.0, plane(table, blocks, 7) < 0.5)


def density_kernel(
    blocks,
    faces,
    per_peer,
    send,
    table,
    self_sum,
    local_sum,
    far_sum,
    from_above,
    from_below,
    returned,
    density,
    slopes,
    total,
):
    total[pl.ds(0, blocks, stride=8), :] = self_sum[...] + local_sum[0] + far_sum[0]
    for c in range(1, 8):
        total[pl.ds(c, blocks, stride=8), :] = jnp.zeros((blocks, lanes), jnp.float32)
    for k in range(faces):
        at = 8 * (blocks - faces + k)
        total[at : at + 4, :] += from_above[4 * k : 4 * k + 4, :]
        total[8 * k : 8 * k + 4, :] += from_below[4 * k : 4 * k + 4, :]

    def give(t, carry):
        for k in range(per_peer):
            at = pl.multiple_of(send[0, t, k] * 8, 8)
            source = pl.multiple_of((t * per_peer + k) * 4, 4)
            total[pl.ds(at, 4), :] += returned[pl.ds(source, 4), :]
        return carry

    lax.fori_loop(0, send.shape[1], give, 0, unroll=2)
    density[...] = jnp.where(fluid_mask(blocks, table), kernel_norm * plane(total, blocks, 0), 0.0)
    for c in range(3):
        slopes[c] = plane(total, blocks, 1 + c)


def force_fields(source, density, number, pressed):
    mass = plane(source, number, 6)
    rho = jnp.where(mass > 0.0, density, 1.0)
    inverse = 1.0 / jnp.where(rho > 0.0, rho, 1.0)
    scaled = mass * inverse
    source[pl.ds(7, number, stride=8), :] = scaled
    press = 10.0 * (rho - 1.0) * inverse * scaled
    pressed[...] = press
    return press


def force_body(source, pressed, kind, wide_fields, decoded):
    lane = lax.broadcasted_iota(jnp.int32, (8, lanes), 1)
    sub = lax.broadcasted_iota(jnp.int32, (8, lanes), 0)
    outs = []
    for k, (first, second, row) in enumerate(decoded):
        base = pl.multiple_of(second * 8, 8)
        rows = [wide(source[pl.ds(base + c, 1), :]) for c in range(6 if kind == "second" else 8)]
        if kind != "second":
            press = wide(pressed[pl.ds(second, 1), :])
        merged = []
        sums = None
        for g in range(groups):
            at = rows_item * k + 8 * g
            fields = [wide_fields[f, at : at + 8, :] for f in range(9)]
            dx, dy, dz, square, u = close_u(fields, rows)
            u3 = (u * u) * u
            damp = u3 * (square * (1.0 / (square + 0.25 * softening)))
            if kind == "second":
                damp = damp * fields[7]
                pull = u3 * fields[8]
                values = [damp * (fields[4 + c] - rows[3 + c]) for c in range(3)]
                values += [pull * d for d in (dx, dy, dz)]
            else:
                damp = damp * (fields[7] * rows[7])
                pull = u3 * (fields[8] * rows[6] + fields[3] * press)
                values = [
                    pull * d - damp * (fields[4 + c] - rows[3 + c]) for c, d in enumerate((dx, dy, dz))
                ]
            if kind in ("local", "first"):
                merged.append(
                    merge_lanes([jnp.sum(v, axis=1, keepdims=True) for v in values], first, lane)
                )
            if kind != "first":
                sums = values if sums is None else [s + v for s, v in zip(sums, values)]
        outs.append((merged, merge_rows(sums, sub, range(1, 7)) if sums else None))
    return outs


def run_force(columns, spread, fields, source, pressed, acc_first, acc_second, kind, items, cap):
    run_items(
        columns,
        spread,
        fields,
        9,
        items,
        0,
        items[cap - 1],
        functools.partial(force_body, source, pressed, kind),
        functools.partial(add_sums, acc_first, acc_second),
    )


def far_send_kernel(
    blocks,
    faces,
    per_peer,
    send,
    items,
    table,
    density,
    low,
    high,
    far,
    push,
    columns,
    own_source,
    pressed,
    out_low,
    out_high,
    out_far,
    stage,
    last,
    source,
    spread,
    wide_fields,
    acc_second,
):
    others = source.shape[0] // 8
    source[0 : faces * 8, :] = low[...]
    source[faces * 8 : 2 * faces * 8, :] = high[...]
    source[2 * faces * 8 :, :] = far[...]
    own_source[...] = table[...]
    press = force_fields(own_source, density[...], blocks, pressed)
    last[...] = jnp.zeros(last.shape, jnp.float32)
    for p, piece in enumerate(split3(press)):
        last[pl.ds(p, blocks, stride=8), :] = piece
    make_columns(blocks, own_source, last, columns, stage)
    make_spread(spread)
    clear(acc_second, 4)
    run_force(columns, spread, wide_fields, source, None, None, acc_second, "second", items, items.shape[0] // 2)
    for c in range(3):
        acc_second[pl.ds(4 + c, others, stride=8), :] = push[c] - plane(acc_second, others, 4 + c)
    acc_second[pl.ds(0, faces, stride=8), :] = density[0:faces, :]
    acc_second[pl.ds(8 * faces, faces, stride=8), :] = density[blocks - faces :, :]

    def pick(t, carry):
        for k in range(per_peer):
            at = 8 * (2 * faces + t * per_peer + k)
            acc_second[pl.ds(at, 1), :] = density[pl.ds(send[0, t, k], 1), :]
        return carry

    lax.fori_loop(0, send.shape[1], pick, 0, unroll=4)
    out_low[...] = acc_second[0 : 8 * faces, :]
    out_high[...] = acc_second[8 * faces : 16 * faces, :]
    out_far[...] = acc_second[16 * faces :, :]


def own_force_kernel(
    blocks,
    self_items,
    both_items,
    columns,
    source,
    pressed,
    own,
    spread,
    wide_fields,
    acc_first,
    acc_second,
    turned,
):
    make_spread(spread)
    clear(acc_first, 1)
    clear(acc_second, 4)
    force = functools.partial(
        run_force, columns, spread, wide_fields, source, pressed, acc_first, acc_second
    )
    force("self", self_items, self_items.shape[0])
    force("local", both_items, both_items.shape[0] // 2)
    first_rows(acc_first, turned, blocks)
    for c in range(3):
        own[c] = plane(turned, blocks, c) - plane(acc_second, blocks, 1 + c)


def far_force_kernel(
    blocks,
    faces,
    items,
    columns,
    low,
    high,
    far,
    from_below,
    from_above,
    returned,
    own,
    source,
    source_density,
    pressed,
    spread,
    wide_fields,
    acc_first,
    turned,
):
    others = source.shape[0] // 8
    source[0 : faces * 8, :] = low[...]
    source[faces * 8 : 2 * faces * 8, :] = high[...]
    source[2 * faces * 8 :, :] = far[...]
    source_density[0:faces, :] = plane(from_below, faces, 0)
    source_density[faces : 2 * faces, :] = plane(from_above, faces, 0)
    source_density[2 * faces :, :] = plane(returned, others - 2 * faces, 0)
    force_fields(source, source_density[...], others, pressed)
    make_spread(spread)
    clear(acc_first, 1)
    run_force(columns, spread, wide_fields, source, pressed, acc_first, None, "first", items, items.shape[0] // 2)
    first_rows(acc_first, turned, blocks)
    for c in range(3):
        own[c] = plane(turned, blocks, c)


def final_kernel(
    blocks,
    faces,
    per_peer,
    send,
    table,
    density,
    slopes,
    local_sum,
    far_sum,
    own_force,
    far_force,
    from_above,
    from_below,
    returned,
    out,
    total,
):
    total[...] = jnp.zeros(total.shape, jnp.float32)
    total[8 * (blocks - faces) :, :] += from_above[...]
    total[0 : 8 * faces, :] += from_below[...]

    def give(t, carry):
        for k in range(per_peer):
            at = pl.multiple_of(send[0, t, k] * 8, 8)
            source = pl.multiple_of((t * per_peer + k) * 8, 8)
            total[pl.ds(at, 8), :] += returned[pl.ds(source, 8), :]
        return carry

    lax.fori_loop(0, send.shape[1], give, 0, unroll=2)
    fluid = fluid_mask(blocks, table)
    mass = plane(table, blocks, 6)
    over_mass = 1.0 / jnp.where(mass > 0.0, mass, 1.0)
    over_rho = 1.0 / jnp.where(fluid, density[...], 1.0)
    press = jnp.where(fluid, 10.0 * (density[...] - 1.0) * over_rho * over_rho, 0.0)
    for c in range(3):
        force = (own_force[c] + far_force[c]) * over_mass
        force = force + local_sum[1 + c] + far_sum[1 + c]
        force = force + plane(total, blocks, 1 + c) * over_rho + plane(total, blocks, 4 + c)
        out[c] = jnp.where(fluid, kernel_norm * (force - press * slopes[c]), 0.0)


def f32(*shape):
    return jax.ShapeDtypeStruct(shape, jnp.float32)


def i32(*shape):
    return jax.ShapeDtypeStruct(shape, jnp.int32)


def to_above(shard):
    count = lax.axis_size("slab")
    return lax.ppermute(shard, "slab", [(i, i + 1) for i in range(count - 1)])


def to_below(shard):
    count = lax.axis_size("slab")
    return lax.ppermute(shard, "slab", [(i + 1, i) for i in range(count - 1)])


def swap_tiles(rows, tiles):
    parts = rows.reshape(tiles, rows.shape[0] // tiles, lanes)
    return lax.all_to_all(parts, "tile", split_axis=0, concat_axis=0, tiled=True).reshape(rows.shape)


def on_device(
    positions,
    velocities,
    masses,
    wall_areas,
    normals,
    wall_flags,
    counts,
    send_list,
    local_pairs,
    remote_pairs,
    remote_live,
):
    blocks = positions.shape[1]
    faces = blocks // 4
    tiles = lax.axis_size("tile")
    per_peer = send_list.shape[2]
    offered = send_list.shape[1] * per_peer
    others = 2 * faces + offered
    n_local = local_pairs.shape[0]
    n_remote = remote_pairs.shape[0]
    per = lanes // rows_item
    spare = 3 * batch * density_halves
    self_cap = per * blocks + spare
    own_cap = per * n_local + spare
    far_cap = per * n_remote + spare
    pair_cap = n_remote + 2 * pair_pad
    columns_shape = jax.ShapeDtypeStruct((blocks + 1, lanes, lanes), bf16)
    stage = vmem((blocks * 32, lanes), jnp.float32)

    def fields(number, halves):
        return [vmem((lanes, 128 * number), bf16), vmem((halves, number, lanes, lanes), jnp.float32)]

    acc_first = vmem((blocks // 16 + 1, lanes, lanes), jnp.float32)
    turned = vmem((blocks * 8, lanes), jnp.float32)

    def tiles_of(number):
        return vmem((number * 8, lanes), jnp.float32)

    def cost(flops):
        return pl.CostEstimate(flops=flops, bytes_accessed=400_000, transcendentals=0)

    table, picked, head, tail = pl.pallas_call(
        functools.partial(pack_kernel, blocks, faces, per_peer),
        out_shape=(f32(blocks * 8, lanes), f32(offered * 8, lanes), f32(faces * 8, lanes), f32(faces * 8, lanes)),
        in_specs=[spec(smem)] + [spec(vmem)] * 7,
        out_specs=[spec(vmem)] * 4,
        compiler_params=params(grant_mib),
        name="pack",
    )(
        send_list,
        positions,
        velocities,
        masses,
        wall_areas,
        normals,
        wall_flags[None, :],
        counts[None, :],
    )
    low = to_above(tail)
    high = to_below(head)
    far = swap_tiles(picked, tiles)

    columns, self_sum, self_items, own_items, far_pairs = pl.pallas_call(
        functools.partial(self_density_kernel, blocks),
        out_shape=(
            columns_shape,
            f32(blocks, lanes),
            i32(self_cap),
            i32(2 * own_cap),
            i32(2 * pair_cap),
        ),
        in_specs=[spec(smem)] * 5 + [spec(vmem)],
        out_specs=[spec(vmem)] * 2 + [spec(smem)] * 3,
        scratch_shapes=[stage] + fields(8, density_halves) + [tiles_of(blocks)],
        compiler_params=params(grant_mib),
        cost_estimate=cost(40_000_000),
        name="self_density",
    )(counts, wall_flags, remote_live, local_pairs.T, remote_pairs.T, table)

    far_sum, back_low, back_high, back_far, push, far_items = pl.pallas_call(
        functools.partial(far_density_kernel, blocks, faces),
        out_shape=(
            f32(4, blocks, lanes),
            f32(faces * 4, lanes),
            f32(faces * 4, lanes),
            f32(offered * 4, lanes),
            f32(3, others, lanes),
            i32(2 * far_cap),
        ),
        in_specs=[spec(smem)] + [spec(vmem)] * 4,
        out_specs=[spec(vmem)] * 5 + [spec(smem)],
        scratch_shapes=fields(8, density_halves)
        + [acc_first, tiles_of(others), turned]
        + [
            tiles_of(others),
            vmem((others, lanes), jnp.float32),
            smem((others, lanes), jnp.float32),
            smem((far_cap,), jnp.int32),
            pltpu.SemaphoreType.DMA,
        ],
        compiler_params=params(grant_mib),
        cost_estimate=cost(100_000_000),
        name="far_density",
    )(far_pairs, columns, low, high, far)

    from_above = to_below(back_low)
    from_below = to_above(back_high)
    returned = swap_tiles(back_far, tiles)

    local_sum = pl.pallas_call(
        functools.partial(local_density_kernel, blocks),
        out_shape=f32(4, blocks, lanes),
        in_specs=[spec(smem)] + [spec(vmem)] * 2,
        out_specs=spec(vmem),
        scratch_shapes=fields(8, density_halves) + [acc_first, tiles_of(blocks), turned],
        compiler_params=params(grant_mib),
        cost_estimate=cost(40_000_000),
        name="local_density",
    )(own_items, table, columns)

    density, slopes = pl.pallas_call(
        functools.partial(density_kernel, blocks, faces, per_peer),
        out_shape=(f32(blocks, lanes), f32(3, blocks, lanes)),
        in_specs=[spec(smem)] + [spec(vmem)] * 7,
        out_specs=[spec(vmem)] * 2,
        scratch_shapes=[tiles_of(blocks)],
        compiler_params=params(grant_mib),
        name="density",
    )(send_list, table, self_sum, local_sum, far_sum, from_above, from_below, returned)

    force_columns, force_table, pressed, out_low, out_high, out_far = pl.pallas_call(
        functools.partial(far_send_kernel, blocks, faces, per_peer),
        out_shape=(
            columns_shape,
            f32(blocks * 8, lanes),
            f32(blocks, lanes),
            f32(faces * 8, lanes),
            f32(faces * 8, lanes),
            f32(offered * 8, lanes),
        ),
        in_specs=[spec(smem)] * 2 + [spec(vmem)] * 6,
        out_specs=[spec(vmem)] * 6,
        scratch_shapes=[stage, tiles_of(blocks), tiles_of(others)] + fields(10, force_halves) + [tiles_of(others)],
        compiler_params=params(grant_mib),
        cost_estimate=cost(100_000_000),
        name="far_send",
    )(send_list, far_items, table, density, low, high, far, push)

    force_above = to_below(out_low)
    force_below = to_above(out_high)
    force_far = swap_tiles(out_far, tiles)

    own_force = pl.pallas_call(
        functools.partial(own_force_kernel, blocks),
        out_shape=f32(3, blocks, lanes),
        in_specs=[spec(smem)] * 2 + [spec(vmem)] * 3,
        out_specs=spec(vmem),
        scratch_shapes=fields(10, force_halves) + [acc_first, tiles_of(blocks), turned],
        compiler_params=params(grant_mib),
        cost_estimate=cost(80_000_000),
        name="own_force",
    )(self_items, own_items, force_columns, force_table, pressed)

    far_force = pl.pallas_call(
        functools.partial(far_force_kernel, blocks, faces),
        out_shape=f32(3, blocks, lanes),
        in_specs=[spec(smem)] + [spec(vmem)] * 7,
        out_specs=spec(vmem),
        scratch_shapes=[
            tiles_of(others),
            vmem((others, lanes), jnp.float32),
            vmem((others, lanes), jnp.float32),
        ]
        + fields(10, force_halves)
        + [acc_first, turned],
        compiler_params=params(grant_mib),
        cost_estimate=cost(100_000_000),
        name="far_force",
    )(far_items, force_columns, low, high, far, force_below, force_above, force_far)

    acceleration = pl.pallas_call(
        functools.partial(final_kernel, blocks, faces, per_peer),
        out_shape=f32(3, blocks, lanes),
        in_specs=[spec(smem)] + [spec(vmem)] * 10,
        out_specs=spec(vmem),
        scratch_shapes=[tiles_of(blocks)],
        compiler_params=params(grant_mib),
        name="total",
    )(
        send_list,
        table,
        density,
        slopes,
        local_sum,
        far_sum,
        own_force,
        far_force,
        force_above,
        force_below,
        force_far,
    )
    return (density, acceleration)


def solution(mesh):
    placed = (
        P(None, ("slab", "tile"), None),
        P(None, ("slab", "tile"), None),
        P(("slab", "tile"), None),
        P(("slab", "tile"), None),
        P(None, ("slab", "tile"), None),
        P(("slab", "tile")),
        P(("slab", "tile")),
        P(("slab", "tile"), None, None),
        P(("slab", "tile"), None),
        P(("slab", "tile"), None),
        P(("slab", "tile")),
    )
    return jax.shard_map(
        on_device,
        mesh=mesh,
        in_specs=placed,
        out_specs=(P(("slab", "tile"), None), P(None, ("slab", "tile"), None)),
        check_vma=False,
    )
```

```python
import functools
import math

import jax
import jax.numpy as jnp
from jax import lax
from jax.experimental import pallas as pl
from jax.experimental.pallas import tpu as pltpu
from jax.sharding import PartitionSpec as P

kernel_norm = 21.0 / (16.0 * math.pi)
softening = 0.01
tiny = 1e-30
lanes = 128
rows_item = 32
groups = rows_item // 8
batch = lanes // rows_item
density_halves = 4
force_halves = 2
pair_pad = 8
grant_mib = 64
bf16 = jnp.bfloat16
vmem = pltpu.VMEM
smem = pltpu.SMEM


def spec(space):
    return pl.BlockSpec(memory_space=space)


def params(mib):
    return pltpu.CompilerParams(vmem_limit_bytes=mib * 1024 * 1024)


def column_of(row):
    number = row.shape[1]
    same = lax.broadcasted_iota(jnp.int32, (number, number), 0) == lax.broadcasted_iota(
        jnp.int32, (number, number), 1
    )
    return jnp.sum(jnp.where(same, row, 0.0), axis=1, keepdims=True)


def pack_kernel(
    blocks, faces, per_peer, send, pos, vel, mass, area, normal, flags_row, counts_row, table, picked, head, tail
):
    slot = lax.broadcasted_iota(jnp.int32, (blocks, lanes), 1).astype(jnp.float32)
    alive = slot < column_of(counts_row[...].astype(jnp.float32))
    wall_value = column_of(flags_row[...].astype(jnp.float32)) + jnp.zeros((blocks, lanes), jnp.float32)
    wall = wall_value > 0.5
    nx, ny, nz = normal[0], normal[1], normal[2]
    length = jnp.sqrt(nx * nx + ny * ny + nz * nz)
    weight = jnp.where(alive, jnp.where(wall, area[...], mass[...]), 0.0)
    wall_scale = weight / length
    parts = (nx, ny, nz)
    for c in range(3):
        table[pl.ds(c, blocks, stride=8), :] = 0.5 * pos[c]
        table[pl.ds(3 + c, blocks, stride=8), :] = jnp.where(wall, wall_scale * parts[c], vel[c])
    table[pl.ds(6, blocks, stride=8), :] = weight
    table[pl.ds(7, blocks, stride=8), :] = wall_value
    head[...] = table[0 : faces * 8, :]
    tail[...] = table[(blocks - faces) * 8 : blocks * 8, :]

    def pick(t, carry):
        for k in range(per_peer):
            source = pl.multiple_of(send[0, k, t] * 8, 8)
            at = pl.multiple_of((t * per_peer + k) * 8, 8)
            picked[pl.ds(at, 8), :] = table[pl.ds(source, 8), :]
        return carry

    lax.fori_loop(0, picked.shape[0] // (8 * per_peer), pick, 0, unroll=2)


def rounded(x):
    return x.astype(bf16).astype(jnp.float32)


def split3(x):
    high = rounded(x)
    rest = x - high
    middle = rounded(rest)
    return high, middle, rest - middle


def make_spread(spread):
    shape = (lanes, spread.shape[1])
    k = lax.broadcasted_iota(jnp.int32, shape, 0) & 31
    tile = lax.broadcasted_iota(jnp.int32, shape, 1) >> 7
    want = jnp.where(tile == 3, 6, jnp.where(tile > 3, tile - 1, tile))
    want = jnp.where(tile == 7, 7, want)
    hit = jnp.logical_and(jnp.logical_and(k < 24, (k & 7) == want), tile < 8)
    hit = jnp.logical_or(hit, jnp.logical_and(jnp.logical_and(k >= 24, k < 27), tile == 8))
    spread[0:lanes, :] = jnp.where(hit, 1.0, 0.0).astype(bf16)
    lane = lax.broadcasted_iota(jnp.int32, (rows_item, lanes), 1) >> 5
    for j in range(4):
        at = lanes + rows_item * j
        spread[at : at + rows_item, 0:lanes] = jnp.where(lane == j, 1.0, 0.0).astype(bf16)


def make_columns(blocks, table, last, columns, stage):
    for b in range(blocks):
        for p, piece in enumerate(split3(table[8 * b : 8 * b + 8, :])):
            stage[32 * b + 8 * p : 32 * b + 8 * p + 8, :] = piece
        if last is None:
            stage[32 * b + 24 : 32 * b + 32, :] = jnp.zeros((8, lanes), jnp.float32)
        else:
            stage[32 * b + 24 : 32 * b + 32, :] = last[8 * b : 8 * b + 8, :]

    def some(g, carry):
        turned = stage[pl.ds(pl.multiple_of(g * lanes, lanes), lanes), :].T
        columns[g] = turned.astype(bf16)
        return carry

    lax.fori_loop(0, blocks // 4, some, 0, unroll=2)
    columns[blocks // 4] = jnp.zeros((lanes, lanes), bf16)


def put_items(items, at, code):
    for k in range(lanes // rows_item):
        items[at + k] = code | (k << 16)


def close_items(items, count, blocks):
    for k in range(2 * batch * density_halves):
        items[count + k] = jnp.int32(blocks)


def chunks(count):
    return (count + (rows_item - 1)) >> 5


def decode(code):
    first = code & 255
    second = (code >> 8) & 255
    row = pl.multiple_of((code >> 16) * rows_item, rows_item)
    return first, second, row


def wide(row):
    return jnp.broadcast_to(row, (8, lanes))


def spread_fields(columns, spread, wide_fields, tiles, decoded):
    parts = []
    for first, second, row in decoded:
        mask = spread[pl.ds(pl.multiple_of(lanes + (first & 3) * rows_item, rows_item), rows_item), 0:lanes]
        parts.append(columns[first >> 2, pl.ds(row, rows_item), :] * mask)
    left = jnp.concatenate(parts, axis=0)
    for t in range((tiles + 1) // 2):
        both = jnp.dot(left, spread[0:lanes, 256 * t : 256 * t + 256], preferred_element_type=jnp.float32)
        wide_fields[2 * t] = both[:, 0:lanes]
        wide_fields[2 * t + 1] = both[:, lanes : 2 * lanes]


def close_u(fields, rows):
    dx = fields[0] - rows[0]
    dy = fields[1] - rows[1]
    dz = fields[2] - rows[2]
    square = dx * dx + dy * dy + dz * dz
    safe = jnp.maximum(square, tiny)
    q = safe * lax.rsqrt(safe)
    u = jnp.maximum(1.0 - q, 0.0)
    return dx, dy, dz, square, u


def kernel_shape(u):
    u2 = u * u
    return (u2 * u2) * (5.0 - 4.0 * u)


def run_items(columns, spread, wide_fields, tiles, items, start, count, body, finish):
    halves = wide_fields.shape[0]
    size = batch * halves

    def parts(it):
        for h in range(halves):
            yield h, [decode(items[start + (it * halves + h) * batch + k]) for k in range(batch)]

    def prepare(it):
        for h, decoded in parts(it):
            spread_fields(columns, spread, wide_fields.at[h], tiles, decoded)

    def step(it, carry):
        done = [(decoded, body(wide_fields.at[h], decoded)) for h, decoded in parts(it)]
        prepare(it + 1)
        for decoded, outs in done:
            finish(decoded, outs)
        return carry

    prepare(0)
    lax.fori_loop(0, (count + size - 1) >> (size.bit_length() - 1), step, 0)


def merge_lanes(values, first, lane):
    base = (first & 15) * 8
    total = jnp.zeros((8, lanes), jnp.float32)
    for c, value in enumerate(values):
        total = jnp.where(lane == base + c, value, total)
    return total


def merge_rows(values, sub, places):
    total = jnp.zeros((8, lanes), jnp.float32)
    for c, value in zip(places, values):
        total = jnp.where(sub == c, jnp.sum(value, axis=0, keepdims=True), total)
    return total


def add_sums(acc_first, acc_second, decoded, outs):
    for (first, second, row), (merged, tile) in zip(decoded, outs):
        if merged:
            slab = first >> 4
            for g in range(groups):
                acc_first[slab, pl.ds(row + 8 * g, 8), :] += merged[g]
        if tile is not None:
            at = pl.multiple_of(second * 8, 8)
            acc_second[pl.ds(at, 8), :] += tile


def density_body(source, kind, wide_fields, decoded):
    lane = lax.broadcasted_iota(jnp.int32, (8, lanes), 1)
    sub = lax.broadcasted_iota(jnp.int32, (8, lanes), 0)
    places = {"self": (0,), "local": (0,), "both": (0, 1, 2, 3), "second": (0, 4, 5, 6)}
    outs = []
    for k, (first, second, row) in enumerate(decoded):
        base = pl.multiple_of(second * 8, 8)
        rows = [wide(source[pl.ds(base + c, 1), :]) for c in range(3)]
        given = []
        if kind in ("both", "local", "first"):
            given = [wide(source[pl.ds(base + 6, 1), :])]
            if kind == "first":
                given += [wide(source[pl.ds(base + 3 + c, 1), :]) for c in range(3)]
        merged = []
        sums = None
        for g in range(groups):
            at = rows_item * k + 8 * g
            number = {"first": 3, "second": 7}.get(kind, 4)
            fields = [wide_fields[f, at : at + 8, :] for f in range(number)]
            dx, dy, dz, square, u = close_u(fields, rows)
            w = kernel_shape(u)
            if given:
                values = [jnp.sum(w * other, axis=1, keepdims=True) for other in given]
                merged.append(merge_lanes(values, first, lane))
            if kind != "first":
                back = [w * field for field in fields[3:]]
                if kind == "both":
                    slope = ((u * u) * u) * fields[3]
                    back += [slope * d for d in (dx, dy, dz)]
                sums = back if sums is None else [s + b for s, b in zip(sums, back)]
        outs.append((merged, merge_rows(sums, sub, places[kind]) if sums else None))
    return outs


def clear(ref, pieces):
    size = ref.shape[0] // pieces

    def some(k, carry):
        at = pl.multiple_of(k * size, size)
        ref[pl.ds(at, size)] = jnp.zeros((size,) + tuple(ref.shape[1:]), jnp.float32)
        return carry

    lax.fori_loop(0, pieces, some, 0)


def plane(ref, number, c):
    return ref[pl.ds(c, number, stride=8), :]


def first_rows(acc_first, turned, blocks):
    for s in range(blocks // 16):
        turned[s * lanes : (s + 1) * lanes, :] = acc_first[s].T


def run_density(columns, spread, fields, source, acc_first, acc_second, kind, items, start, count):
    run_items(
        columns,
        spread,
        fields,
        7 if kind == "second" else 4,
        items,
        start,
        count,
        functools.partial(density_body, source, kind),
        functools.partial(add_sums, acc_first, acc_second),
    )


def self_density_kernel(
    blocks,
    counts,
    flags,
    live,
    local_pairs,
    remote_pairs,
    table,
    columns_out,
    own,
    items,
    local_items,
    far_pairs,
    stage,
    spread,
    wide_fields,
    acc_second,
    columns,
    sem,
):
    make_columns(blocks, table, None, columns, stage)
    columns_copy = pltpu.make_async_copy(columns, columns_out, sem)
    columns_copy.start()
    make_spread(spread)
    clear(acc_second, 4)
    zero = jnp.int32(0)

    def self_step(b, n):
        put_items(items, n, b | (b << 8))
        return n + chunks(counts[b]) * (1 - flags[b])

    count = lax.fori_loop(0, blocks, self_step, zero, unroll=8)
    close_items(items, count, blocks)
    items[items.shape[0] - 1] = count
    run_density(columns, spread, wide_fields, table, None, acc_second, "self", items, 0, count)
    own[...] = plane(acc_second, blocks, 0)
    cap = local_items.shape[0] // 2

    def local_step(p, state):
        n_both, n_wall = state
        a = local_pairs[0, p]
        b = local_pairs[1, p]
        wall_b = flags[b]
        kinds = flags[a] + wall_b
        swap = jnp.where(kinds == 1, wall_b, (counts[b] < counts[a]).astype(jnp.int32)) > 0
        first = jnp.where(swap, b, a)
        second = jnp.where(swap, a, b)
        number = chunks(counts[first])
        put_items(local_items, jnp.where(kinds == 0, n_both, n_wall), first | (second << 8))
        return n_both + jnp.where(kinds == 0, number, 0), n_wall + jnp.where(kinds == 1, number, 0)

    n_both, n_wall = lax.fori_loop(0, local_pairs.shape[1], local_step, (zero, zero + cap), unroll=8)
    close_items(local_items, n_both, blocks)
    close_items(local_items, n_wall, blocks)
    local_items[cap - 1] = n_both
    local_items[2 * cap - 1] = n_wall - cap
    half = far_pairs.shape[0] // 2

    def remote_step(p, state):
        n_fluid, n_wall = state
        a = remote_pairs[0, p]
        j = remote_pairs[1, p]
        b = jnp.where(j < blocks, j, j - blocks)
        wall = flags[a]
        code = a | (b << 8) | (chunks(counts[a]) << 16)
        far_pairs[jnp.where(wall > 0, n_wall, n_fluid)] = code
        return n_fluid + 1 - wall, n_wall + wall

    n_fluid, n_wall = lax.fori_loop(0, live[0], remote_step, (zero, zero + half))
    far_pairs[half - 1] = n_fluid
    far_pairs[2 * half - 1] = n_wall - half
    for k in range(pair_pad):
        far_pairs[n_fluid + k] = zero
        far_pairs[n_wall + k] = zero
    columns_copy.wait()


def local_density_kernel(
    blocks,
    items,
    table,
    columns_in,
    own,
    spread,
    wide_fields,
    acc_first,
    acc_second,
    turned,
    columns,
    sem,
):
    columns_copy = pltpu.make_async_copy(columns_in, columns, sem)
    columns_copy.start()
    make_spread(spread)
    clear(acc_first, 1)
    clear(acc_second, 4)
    density = functools.partial(run_density, columns, spread, wide_fields, table, acc_first, acc_second)
    columns_copy.wait()
    cap = items.shape[0] // 2
    density("local", items, 0, items[cap - 1])
    density("second", items, cap, items[2 * cap - 1])
    first_rows(acc_first, turned, blocks)
    own[0] = plane(turned, blocks, 0) + plane(acc_second, blocks, 0)
    for c in range(1, 4):
        own[c] = plane(acc_second, blocks, 3 + c)


def rows_out(tiles, out, start, number):
    for k in range(number):
        out[4 * k : 4 * k + 4, :] = tiles[8 * (start + k) : 8 * (start + k) + 4, :]


def far_density_kernel(
    blocks,
    faces,
    far_pairs,
    columns_in,
    low,
    high,
    far,
    own,
    back_low,
    back_high,
    back_far,
    push,
    items,
    spread,
    wide_fields,
    acc_first,
    acc_second,
    turned,
    source,
    wall_rows,
    wall_flag,
    wall_items,
    columns,
    sem,
    sems,
):
    others = source.shape[0] // 8
    copies = fetch_source(faces, low, high, far, source, sems)
    columns_copy = pltpu.make_async_copy(columns_in, columns, sems.at[3])
    columns_copy.start()
    make_spread(spread)
    for copy in copies:
        copy.wait()
    wall_rows[...] = plane(source, others, 7)
    flag_copy = pltpu.make_async_copy(wall_rows, wall_flag, sem)
    flag_copy.start()
    clear(acc_first, 1)
    clear(acc_second, 4)
    flag_copy.wait()
    zero = jnp.int32(0)
    half = far_pairs.shape[0] // 2
    cap = items.shape[0] // 2

    def fluid_second(code):
        return wall_flag[(code >> 8) & 255, 0] < 0.5

    def wall_step(q, n):
        for k in range(pair_pad):
            code = far_pairs[half + q * pair_pad + k]
            put_items(wall_items, n, code & 65535)
            n = n + jnp.where(fluid_second(code), code >> 16, 0)
        return n

    def fluid_step(q, state):
        n_both, n_first = state
        for k in range(pair_pad):
            code = far_pairs[q * pair_pad + k]
            number = code >> 16
            fluid = fluid_second(code)
            put_items(items, jnp.where(fluid, n_both, n_first), code & 65535)
            n_both = n_both + jnp.where(fluid, number, 0)
            n_first = n_first + jnp.where(fluid, 0, number)
        return n_both, n_first

    def passes(pairs):
        return (pairs + (pair_pad - 1)) >> 3

    n_both, n_first = lax.fori_loop(0, passes(far_pairs[half - 1]), fluid_step, (zero, zero + cap))
    close_items(items, n_both, blocks)
    close_items(items, n_first, blocks)
    items[cap - 1] = n_both
    n_second = lax.fori_loop(0, passes(far_pairs[2 * half - 1]), wall_step, zero)
    close_items(wall_items, n_second, blocks)
    columns_copy.wait()
    density = functools.partial(run_density, columns, spread, wide_fields, source, acc_first, acc_second)
    density("second", wall_items, 0, n_second)
    density("both", items, 0, n_both)
    density("first", items, cap, n_first - cap)
    first_rows(acc_first, turned, blocks)
    for c in range(4):
        own[c] = plane(turned, blocks, c)
    rows_out(acc_second, back_low, 0, faces)
    rows_out(acc_second, back_high, faces, faces)
    rows_out(acc_second, back_far, 2 * faces, others - 2 * faces)
    for c in range(3):
        push[c] = plane(acc_second, others, 4 + c)


def fetch(pairs, sems):
    copies = [pltpu.make_async_copy(a, b, sems.at[k]) for k, (a, b) in enumerate(pairs)]
    for copy in copies:
        copy.start()
    return copies


def fetch_source(faces, low, high, far, source, sems):
    return fetch(
        (
            (low, source.at[0 : faces * 8]),
            (high, source.at[faces * 8 : 2 * faces * 8]),
            (far, source.at[2 * faces * 8 :]),
        ),
        sems,
    )


def fluid_mask(blocks, table):
    return jnp.logical_and(plane(table, blocks, 6) > 0.0, plane(table, blocks, 7) < 0.5)


def density_kernel(
    blocks,
    faces,
    per_peer,
    send,
    table,
    self_sum,
    local_sum,
    far_sum,
    from_above,
    from_below,
    returned,
    density,
    slopes,
    total,
):
    total[pl.ds(0, blocks, stride=8), :] = self_sum[...] + local_sum[0] + far_sum[0]
    for c in range(1, 8):
        total[pl.ds(c, blocks, stride=8), :] = jnp.zeros((blocks, lanes), jnp.float32)
    for k in range(faces):
        at = 8 * (blocks - faces + k)
        total[at : at + 4, :] += from_above[4 * k : 4 * k + 4, :]
        total[8 * k : 8 * k + 4, :] += from_below[4 * k : 4 * k + 4, :]

    def give(t, carry):
        for k in range(per_peer):
            at = pl.multiple_of(send[0, k, t] * 8, 8)
            source = pl.multiple_of((t * per_peer + k) * 4, 4)
            total[pl.ds(at, 4), :] += returned[pl.ds(source, 4), :]
        return carry

    lax.fori_loop(0, send.shape[2], give, 0, unroll=2)
    density[...] = jnp.where(fluid_mask(blocks, table), kernel_norm * plane(total, blocks, 0), 0.0)
    for c in range(3):
        slopes[c] = plane(total, blocks, 1 + c)


def force_fields(source, density, number, pressed):
    mass = plane(source, number, 6)
    rho = jnp.where(mass > 0.0, density, 1.0)
    inverse = 1.0 / jnp.where(rho > 0.0, rho, 1.0)
    scaled = mass * inverse
    source[pl.ds(7, number, stride=8), :] = scaled
    press = 10.0 * (rho - 1.0) * inverse * scaled
    pressed[...] = press
    return press


def force_body(source, pressed, kind, wide_fields, decoded):
    lane = lax.broadcasted_iota(jnp.int32, (8, lanes), 1)
    sub = lax.broadcasted_iota(jnp.int32, (8, lanes), 0)
    outs = []
    for k, (first, second, row) in enumerate(decoded):
        base = pl.multiple_of(second * 8, 8)
        rows = [wide(source[pl.ds(base + c, 1), :]) for c in range(6 if kind == "second" else 8)]
        if kind != "second":
            press = wide(pressed[pl.ds(second, 1), :])
        merged = []
        sums = None
        for g in range(groups):
            at = rows_item * k + 8 * g
            fields = [wide_fields[f, at : at + 8, :] for f in range(9)]
            dx, dy, dz, square, u = close_u(fields, rows)
            u3 = (u * u) * u
            damp = u3 * (square * (1.0 / (square + 0.25 * softening)))
            if kind == "second":
                damp = damp * fields[7]
                pull = u3 * fields[8]
                values = [damp * (fields[4 + c] - rows[3 + c]) for c in range(3)]
                values += [pull * d for d in (dx, dy, dz)]
            else:
                damp = damp * (fields[7] * rows[7])
                pull = u3 * (fields[8] * rows[6] + fields[3] * press)
                values = [
                    pull * d - damp * (fields[4 + c] - rows[3 + c]) for c, d in enumerate((dx, dy, dz))
                ]
            if kind in ("local", "first"):
                merged.append(
                    merge_lanes([jnp.sum(v, axis=1, keepdims=True) for v in values], first, lane)
                )
            if kind != "first":
                sums = values if sums is None else [s + v for s, v in zip(sums, values)]
        outs.append((merged, merge_rows(sums, sub, range(1, 7)) if sums else None))
    return outs


def run_force(columns, spread, fields, source, pressed, acc_first, acc_second, kind, items, cap):
    run_items(
        columns,
        spread,
        fields,
        9,
        items,
        0,
        items[cap - 1],
        functools.partial(force_body, source, pressed, kind),
        functools.partial(add_sums, acc_first, acc_second),
    )


def far_send_kernel(
    blocks,
    faces,
    per_peer,
    send,
    items,
    table,
    density,
    low,
    high,
    far,
    push,
    columns_out,
    own_source,
    pressed,
    out_low,
    out_high,
    out_far,
    stage,
    last,
    source,
    spread,
    wide_fields,
    acc_second,
    columns,
    sems,
):
    others = source.shape[0] // 8
    copies = fetch_source(faces, low, high, far, source, sems)
    own_source[...] = table[...]
    press = force_fields(own_source, density[...], blocks, pressed)
    last[...] = jnp.zeros(last.shape, jnp.float32)
    for p, piece in enumerate(split3(press)):
        last[pl.ds(p, blocks, stride=8), :] = piece
    make_columns(blocks, own_source, last, columns, stage)
    columns_copy = pltpu.make_async_copy(columns, columns_out, sems.at[3])
    columns_copy.start()
    make_spread(spread)
    clear(acc_second, 4)
    for copy in copies:
        copy.wait()
    run_force(columns, spread, wide_fields, source, None, None, acc_second, "second", items, items.shape[0] // 2)
    for c in range(3):
        acc_second[pl.ds(4 + c, others, stride=8), :] = push[c] - plane(acc_second, others, 4 + c)
    acc_second[pl.ds(0, faces, stride=8), :] = density[0:faces, :]
    acc_second[pl.ds(8 * faces, faces, stride=8), :] = density[blocks - faces :, :]

    def pick(t, carry):
        for k in range(per_peer):
            at = 8 * (2 * faces + t * per_peer + k)
            acc_second[pl.ds(at, 1), :] = density[pl.ds(send[0, k, t], 1), :]
        return carry

    lax.fori_loop(0, send.shape[2], pick, 0, unroll=4)
    out_low[...] = acc_second[0 : 8 * faces, :]
    out_high[...] = acc_second[8 * faces : 16 * faces, :]
    out_far[...] = acc_second[16 * faces :, :]
    columns_copy.wait()


def own_force_kernel(
    blocks,
    self_items,
    both_items,
    columns_in,
    source,
    pressed,
    own,
    spread,
    wide_fields,
    acc_first,
    acc_second,
    turned,
    columns,
    sem,
):
    columns_copy = pltpu.make_async_copy(columns_in, columns, sem)
    columns_copy.start()
    make_spread(spread)
    clear(acc_first, 1)
    clear(acc_second, 4)
    columns_copy.wait()
    force = functools.partial(
        run_force, columns, spread, wide_fields, source, pressed, acc_first, acc_second
    )
    force("self", self_items, self_items.shape[0])
    force("local", both_items, both_items.shape[0] // 2)
    first_rows(acc_first, turned, blocks)
    for c in range(3):
        own[c] = plane(turned, blocks, c) - plane(acc_second, blocks, 1 + c)


def far_force_kernel(
    blocks,
    faces,
    items,
    columns_in,
    low,
    high,
    far,
    from_below,
    from_above,
    returned,
    own,
    source,
    source_density,
    pressed,
    spread,
    wide_fields,
    acc_first,
    turned,
    columns,
    sems,
):
    others = source.shape[0] // 8
    copies = fetch_source(faces, low, high, far, source, sems)
    columns_copy = pltpu.make_async_copy(columns_in, columns, sems.at[3])
    columns_copy.start()
    source_density[0:faces, :] = plane(from_below, faces, 0)
    source_density[faces : 2 * faces, :] = plane(from_above, faces, 0)
    source_density[2 * faces :, :] = plane(returned, others - 2 * faces, 0)
    make_spread(spread)
    clear(acc_first, 1)
    for copy in copies:
        copy.wait()
    force_fields(source, source_density[...], others, pressed)
    columns_copy.wait()
    run_force(columns, spread, wide_fields, source, pressed, acc_first, None, "first", items, items.shape[0] // 2)
    first_rows(acc_first, turned, blocks)
    for c in range(3):
        own[c] = plane(turned, blocks, c)


def final_kernel(
    blocks,
    faces,
    per_peer,
    send,
    table,
    density,
    slopes,
    local_sum,
    far_sum,
    own_force,
    far_force,
    from_above,
    from_below,
    returned,
    out,
    total,
):
    total[...] = jnp.zeros(total.shape, jnp.float32)
    total[8 * (blocks - faces) :, :] += from_above[...]
    total[0 : 8 * faces, :] += from_below[...]

    def give(t, carry):
        for k in range(per_peer):
            at = pl.multiple_of(send[0, k, t] * 8, 8)
            source = pl.multiple_of((t * per_peer + k) * 8, 8)
            total[pl.ds(at, 8), :] += returned[pl.ds(source, 8), :]
        return carry

    lax.fori_loop(0, send.shape[2], give, 0, unroll=2)
    fluid = fluid_mask(blocks, table)
    mass = plane(table, blocks, 6)
    over_mass = 1.0 / jnp.where(mass > 0.0, mass, 1.0)
    over_rho = 1.0 / jnp.where(fluid, density[...], 1.0)
    press = jnp.where(fluid, 10.0 * (density[...] - 1.0) * over_rho * over_rho, 0.0)
    for c in range(3):
        force = (own_force[c] + far_force[c]) * over_mass
        force = force + local_sum[1 + c] + far_sum[1 + c]
        force = force + plane(total, blocks, 1 + c) * over_rho + plane(total, blocks, 4 + c)
        out[c] = jnp.where(fluid, kernel_norm * (force - press * slopes[c]), 0.0)


def f32(*shape):
    return jax.ShapeDtypeStruct(shape, jnp.float32)


def i32(*shape):
    return jax.ShapeDtypeStruct(shape, jnp.int32)


def to_above(shard):
    count = lax.axis_size("slab")
    return lax.ppermute(shard, "slab", [(i, i + 1) for i in range(count - 1)])


def to_below(shard):
    count = lax.axis_size("slab")
    return lax.ppermute(shard, "slab", [(i + 1, i) for i in range(count - 1)])


def swap_tiles(rows, tiles):
    parts = rows.reshape(tiles, rows.shape[0] // tiles, lanes)
    return lax.all_to_all(parts, "tile", split_axis=0, concat_axis=0, tiled=True).reshape(rows.shape)


def on_device(
    positions,
    velocities,
    masses,
    wall_areas,
    normals,
    wall_flags,
    counts,
    send_list,
    local_pairs,
    remote_pairs,
    remote_live,
):
    blocks = positions.shape[1]
    faces = blocks // 4
    tiles = lax.axis_size("tile")
    per_peer = send_list.shape[2]
    offered = send_list.shape[1] * per_peer
    send = jnp.swapaxes(send_list, 1, 2)
    others = 2 * faces + offered
    n_local = local_pairs.shape[0]
    n_remote = remote_pairs.shape[0]
    per = lanes // rows_item
    spare = 3 * batch * density_halves
    self_cap = per * blocks + spare
    own_cap = per * n_local + spare
    far_cap = per * n_remote + spare
    pair_cap = n_remote + 2 * pair_pad
    columns_shape = jax.ShapeDtypeStruct((blocks // 4 + 1, lanes, lanes), bf16)
    columns_scratch = vmem((blocks // 4 + 1, lanes, lanes), bf16)
    stage = vmem((blocks * 32, lanes), jnp.float32)

    def fields(number, halves):
        return [vmem((lanes + 4 * rows_item, 128 * number), bf16), vmem((halves, number, lanes, lanes), jnp.float32)]

    acc_first = vmem((blocks // 16 + 1, lanes, lanes), jnp.float32)
    turned = vmem((blocks * 8, lanes), jnp.float32)

    def tiles_of(number):
        return vmem((number * 8, lanes), jnp.float32)

    def cost(flops):
        return pl.CostEstimate(flops=flops, bytes_accessed=400_000, transcendentals=0)

    table, picked, head, tail = pl.pallas_call(
        functools.partial(pack_kernel, blocks, faces, per_peer),
        out_shape=(f32(blocks * 8, lanes), f32(offered * 8, lanes), f32(faces * 8, lanes), f32(faces * 8, lanes)),
        in_specs=[spec(smem)] + [spec(vmem)] * 7,
        out_specs=[spec(vmem)] * 4,
        compiler_params=params(grant_mib),
        name="pack",
    )(
        send,
        positions,
        velocities,
        masses,
        wall_areas,
        normals,
        wall_flags[None, :],
        counts[None, :],
    )
    low = to_above(tail)
    high = to_below(head)
    far = swap_tiles(picked, tiles)

    columns, self_sum, self_items, own_items, far_pairs = pl.pallas_call(
        functools.partial(self_density_kernel, blocks),
        out_shape=(
            columns_shape,
            f32(blocks, lanes),
            i32(self_cap),
            i32(2 * own_cap),
            i32(2 * pair_cap),
        ),
        in_specs=[spec(smem)] * 5 + [spec(vmem)],
        out_specs=[spec(pl.ANY), spec(vmem)] + [spec(smem)] * 3,
        scratch_shapes=[stage]
        + fields(8, density_halves)
        + [tiles_of(blocks), columns_scratch, pltpu.SemaphoreType.DMA],
        compiler_params=params(grant_mib),
        cost_estimate=cost(40_000_000),
        name="self_density",
    )(counts, wall_flags, remote_live, local_pairs.T, remote_pairs.T, table)

    far_sum, back_low, back_high, back_far, push, far_items = pl.pallas_call(
        functools.partial(far_density_kernel, blocks, faces),
        out_shape=(
            f32(4, blocks, lanes),
            f32(faces * 4, lanes),
            f32(faces * 4, lanes),
            f32(offered * 4, lanes),
            f32(3, others, lanes),
            i32(2 * far_cap),
        ),
        in_specs=[spec(smem)] + [spec(pl.ANY)] * 4,
        out_specs=[spec(vmem)] * 5 + [spec(smem)],
        scratch_shapes=fields(8, density_halves)
        + [acc_first, tiles_of(others), turned]
        + [
            tiles_of(others),
            vmem((others, lanes), jnp.float32),
            smem((others, lanes), jnp.float32),
            smem((far_cap,), jnp.int32),
            columns_scratch,
            pltpu.SemaphoreType.DMA,
            pltpu.SemaphoreType.DMA((4,)),
        ],
        compiler_params=params(grant_mib),
        cost_estimate=cost(100_000_000),
        name="far_density",
    )(far_pairs, columns, low, high, far)

    from_above = to_below(back_low)
    from_below = to_above(back_high)
    returned = swap_tiles(back_far, tiles)

    local_sum = pl.pallas_call(
        functools.partial(local_density_kernel, blocks),
        out_shape=f32(4, blocks, lanes),
        in_specs=[spec(smem), spec(vmem), spec(pl.ANY)],
        out_specs=spec(vmem),
        scratch_shapes=fields(8, density_halves)
        + [acc_first, tiles_of(blocks), turned, columns_scratch, pltpu.SemaphoreType.DMA],
        compiler_params=params(grant_mib),
        cost_estimate=cost(40_000_000),
        name="local_density",
    )(own_items, table, columns)

    density, slopes = pl.pallas_call(
        functools.partial(density_kernel, blocks, faces, per_peer),
        out_shape=(f32(blocks, lanes), f32(3, blocks, lanes)),
        in_specs=[spec(smem)] + [spec(vmem)] * 7,
        out_specs=[spec(vmem)] * 2,
        scratch_shapes=[tiles_of(blocks)],
        compiler_params=params(grant_mib),
        name="density",
    )(send, table, self_sum, local_sum, far_sum, from_above, from_below, returned)

    force_columns, force_table, pressed, out_low, out_high, out_far = pl.pallas_call(
        functools.partial(far_send_kernel, blocks, faces, per_peer),
        out_shape=(
            columns_shape,
            f32(blocks * 8, lanes),
            f32(blocks, lanes),
            f32(faces * 8, lanes),
            f32(faces * 8, lanes),
            f32(offered * 8, lanes),
        ),
        in_specs=[spec(smem)] * 2 + [spec(vmem)] * 2 + [spec(pl.ANY)] * 3 + [spec(vmem)],
        out_specs=[spec(pl.ANY)] + [spec(vmem)] * 5,
        scratch_shapes=[stage, tiles_of(blocks), tiles_of(others)] + fields(10, force_halves) + [tiles_of(others), columns_scratch, pltpu.SemaphoreType.DMA((4,))],
        compiler_params=params(grant_mib),
        cost_estimate=cost(100_000_000),
        name="far_send",
    )(send, far_items, table, density, low, high, far, push)

    force_above = to_below(out_low)
    force_below = to_above(out_high)
    force_far = swap_tiles(out_far, tiles)

    own_force = pl.pallas_call(
        functools.partial(own_force_kernel, blocks),
        out_shape=f32(3, blocks, lanes),
        in_specs=[spec(smem)] * 2 + [spec(pl.ANY)] + [spec(vmem)] * 2,
        out_specs=spec(vmem),
        scratch_shapes=fields(10, force_halves)
        + [acc_first, tiles_of(blocks), turned, columns_scratch, pltpu.SemaphoreType.DMA],
        compiler_params=params(grant_mib),
        cost_estimate=cost(80_000_000),
        name="own_force",
    )(self_items, own_items, force_columns, force_table, pressed)

    far_force = pl.pallas_call(
        functools.partial(far_force_kernel, blocks, faces),
        out_shape=f32(3, blocks, lanes),
        in_specs=[spec(smem)] + [spec(pl.ANY)] * 4 + [spec(vmem)] * 3,
        out_specs=spec(vmem),
        scratch_shapes=[
            tiles_of(others),
            vmem((others, lanes), jnp.float32),
            vmem((others, lanes), jnp.float32),
        ]
        + fields(10, force_halves)
        + [acc_first, turned, columns_scratch, pltpu.SemaphoreType.DMA((4,))],
        compiler_params=params(grant_mib),
        cost_estimate=cost(100_000_000),
        name="far_force",
    )(far_items, force_columns, low, high, far, force_below, force_above, force_far)

    acceleration = pl.pallas_call(
        functools.partial(final_kernel, blocks, faces, per_peer),
        out_shape=f32(3, blocks, lanes),
        in_specs=[spec(smem)] + [spec(vmem)] * 10,
        out_specs=spec(vmem),
        scratch_shapes=[tiles_of(blocks)],
        compiler_params=params(grant_mib),
        name="total",
    )(
        send,
        table,
        density,
        slopes,
        local_sum,
        far_sum,
        own_force,
        far_force,
        force_above,
        force_below,
        force_far,
    )
    return (density, acceleration)


def solution(mesh):
    placed = (
        P(None, ("slab", "tile"), None),
        P(None, ("slab", "tile"), None),
        P(("slab", "tile"), None),
        P(("slab", "tile"), None),
        P(None, ("slab", "tile"), None),
        P(("slab", "tile")),
        P(("slab", "tile")),
        P(("slab", "tile"), None, None),
        P(("slab", "tile"), None),
        P(("slab", "tile"), None),
        P(("slab", "tile")),
    )
    return jax.shard_map(
        on_device,
        mesh=mesh,
        in_specs=placed,
        out_specs=(P(("slab", "tile"), None), P(None, ("slab", "tile"), None)),
        check_vma=False,
    )
```

```python
import functools
import math

import jax
import jax.numpy as jnp
from jax import lax
from jax.experimental import pallas as pl
from jax.experimental.pallas import tpu as pltpu
from jax.sharding import PartitionSpec as P

kernel_norm = 21.0 / (16.0 * math.pi)
softening = 0.01
tiny = 1e-30
lanes = 128
rows_item = 32
groups = rows_item // 8
batch = lanes // rows_item
density_halves = 4
force_halves = 4
pair_pad = 8
grant_mib = 64
density_order = (0, 1, 2, 6, 3, 4, 5)
force_order = (0, 1, 2, 3, 4, 5, 7, 8, 6)
bf16 = jnp.bfloat16
vmem = pltpu.VMEM
smem = pltpu.SMEM


def spec(space):
    return pl.BlockSpec(memory_space=space)


def params(mib):
    return pltpu.CompilerParams(vmem_limit_bytes=mib * 1024 * 1024)


def column_of(row):
    number = row.shape[1]
    same = lax.broadcasted_iota(jnp.int32, (number, number), 0) == lax.broadcasted_iota(
        jnp.int32, (number, number), 1
    )
    return jnp.sum(jnp.where(same, row, 0.0), axis=1, keepdims=True)


def pack_kernel(
    blocks, faces, per_peer, send, pos, vel, mass, area, normal, flags_row, counts_row, table, picked, head, tail
):
    slot = lax.broadcasted_iota(jnp.int32, (blocks, lanes), 1).astype(jnp.float32)
    alive = slot < column_of(counts_row[...].astype(jnp.float32))
    wall_value = column_of(flags_row[...].astype(jnp.float32)) + jnp.zeros((blocks, lanes), jnp.float32)
    wall = wall_value > 0.5
    nx, ny, nz = normal[0], normal[1], normal[2]
    length = jnp.sqrt(nx * nx + ny * ny + nz * nz)
    weight = jnp.where(alive, jnp.where(wall, area[...], mass[...]), 0.0)
    wall_scale = weight / length
    parts = (nx, ny, nz)
    for c in range(3):
        table[pl.ds(c, blocks, stride=8), :] = 0.5 * pos[c]
        table[pl.ds(3 + c, blocks, stride=8), :] = jnp.where(wall, wall_scale * parts[c], vel[c])
    table[pl.ds(6, blocks, stride=8), :] = weight
    table[pl.ds(7, blocks, stride=8), :] = wall_value
    head[...] = table[0 : faces * 8, :]
    tail[...] = table[(blocks - faces) * 8 : blocks * 8, :]

    def pick(t, carry):
        for k in range(per_peer):
            source = pl.multiple_of(send[0, k, t] * 8, 8)
            at = pl.multiple_of((t * per_peer + k) * 8, 8)
            picked[pl.ds(at, 8), :] = table[pl.ds(source, 8), :]
        return carry

    lax.fori_loop(0, picked.shape[0] // (8 * per_peer), pick, 0, unroll=2)


def rounded(x):
    return x.astype(bf16).astype(jnp.float32)


def split3(x):
    high = rounded(x)
    rest = x - high
    middle = rounded(rest)
    return high, middle, rest - middle


def make_spread(spread, order):
    shape = (lanes, spread.shape[1])
    k = lax.broadcasted_iota(jnp.int32, shape, 0) & 31
    tile = lax.broadcasted_iota(jnp.int32, shape, 1) >> 7
    want = jnp.full(shape, -1, jnp.int32)
    for t, field in enumerate(order):
        want = jnp.where(tile == t, field, want)
    hit = jnp.logical_and(k < 24, (k & 7) == want)
    hit = jnp.logical_or(hit, jnp.logical_and(jnp.logical_and(k >= 24, k < 27), want == 8))
    spread[0:lanes, :] = jnp.where(hit, 1.0, 0.0).astype(bf16)
    lane = lax.broadcasted_iota(jnp.int32, (rows_item, lanes), 1) >> 5
    for j in range(4):
        at = lanes + rows_item * j
        spread[at : at + rows_item, 0:lanes] = jnp.where(lane == j, 1.0, 0.0).astype(bf16)


def make_columns(blocks, table, last, columns, stage):
    for b in range(blocks):
        for p, piece in enumerate(split3(table[8 * b : 8 * b + 8, :])):
            stage[32 * b + 8 * p : 32 * b + 8 * p + 8, :] = piece
        if last is None:
            stage[32 * b + 24 : 32 * b + 32, :] = jnp.zeros((8, lanes), jnp.float32)
        else:
            stage[32 * b + 24 : 32 * b + 32, :] = last[8 * b : 8 * b + 8, :]

    def some(g, carry):
        turned = stage[pl.ds(pl.multiple_of(g * lanes, lanes), lanes), :].T
        columns[g] = turned.astype(bf16)
        return carry

    lax.fori_loop(0, blocks // 4, some, 0, unroll=2)
    columns[blocks // 4] = jnp.zeros((lanes, lanes), bf16)


def put_items(items, at, code):
    for k in range(lanes // rows_item):
        items[at + k] = code | (k << 16)


def close_items(items, count, blocks):
    for k in range(2 * batch * density_halves):
        items[count + k] = jnp.int32(blocks)


def chunks(count):
    return (count + (rows_item - 1)) >> 5


def decode(code):
    first = code & 255
    second = (code >> 8) & 255
    row = pl.multiple_of((code >> 16) * rows_item, rows_item)
    return first, second, row


def wide(row):
    return jnp.broadcast_to(row, (8, lanes))


def spread_fields(columns, spread, wide_fields, tiles, decoded):
    parts = []
    for first, second, row in decoded:
        mask = spread[pl.ds(pl.multiple_of(lanes + (first & 3) * rows_item, rows_item), rows_item), 0:lanes]
        parts.append(columns[first >> 2, pl.ds(row, rows_item), :] * mask)
    left = jnp.concatenate(parts, axis=0)
    for t in range((tiles + 1) // 2):
        both = jnp.dot(left, spread[0:lanes, 256 * t : 256 * t + 256], preferred_element_type=jnp.float32)
        wide_fields[2 * t] = both[:, 0:lanes]
        wide_fields[2 * t + 1] = both[:, lanes : 2 * lanes]


def close_u(fields, rows):
    dx = fields[0] - rows[0]
    dy = fields[1] - rows[1]
    dz = fields[2] - rows[2]
    square = dx * dx + dy * dy + dz * dz
    safe = jnp.maximum(square, tiny)
    q = safe * lax.rsqrt(safe)
    u = jnp.maximum(1.0 - q, 0.0)
    return dx, dy, dz, square, u


def kernel_shape(u):
    u2 = u * u
    return (u2 * u2) * (5.0 - 4.0 * u)


def run_items(columns, spread, wide_fields, tiles, items, start, count, body, finish, alternate=False):
    halves = wide_fields.shape[0]
    size = batch * halves

    def decoded_of(it, h):
        return [decode(items[start + (it * halves + h) * batch + k]) for k in range(batch)]

    def prepare(it, hs):
        for h in hs:
            spread_fields(columns, spread, wide_fields.at[h], tiles, decoded_of(it, h))

    def work(it, hs):
        done = []
        for h in hs:
            decoded = decoded_of(it, h)
            done.append((decoded, body(wide_fields.at[h], decoded)))
        return done

    group = halves // 2 if alternate else halves
    front, rear = range(group), range(group, halves)

    def step(it, carry):
        prepare(it, rear)
        done = work(it, front)
        prepare(it + 1, front)
        done += work(it, rear)
        for decoded, outs in done:
            finish(decoded, outs)
        return carry

    prepare(0, front)
    lax.fori_loop(0, (count + size - 1) >> (size.bit_length() - 1), step, 0)


def merge_lanes(values, first, lane):
    base = (first & 15) * 8
    total = jnp.zeros((8, lanes), jnp.float32)
    for c, value in enumerate(values):
        total = jnp.where(lane == base + c, value, total)
    return total


def merge_rows(values, sub, places):
    total = jnp.zeros((8, lanes), jnp.float32)
    for c, value in zip(places, values):
        total = jnp.where(sub == c, jnp.sum(value, axis=0, keepdims=True), total)
    return total


def add_sums(acc_first, acc_second, decoded, outs):
    for (first, second, row), (merged, tile) in zip(decoded, outs):
        if merged:
            slab = first >> 4
            for g in range(groups):
                acc_first[slab, pl.ds(row + 8 * g, 8), :] += merged[g]
        if tile is not None:
            at = pl.multiple_of(second * 8, 8)
            acc_second[pl.ds(at, 8), :] += tile


def density_body(source, kind, wide_fields, decoded):
    lane = lax.broadcasted_iota(jnp.int32, (8, lanes), 1)
    sub = lax.broadcasted_iota(jnp.int32, (8, lanes), 0)
    places = {"self": (0,), "local": (0,), "both": (0, 1, 2, 3), "second": (0, 4, 5, 6)}
    outs = []
    for k, (first, second, row) in enumerate(decoded):
        base = pl.multiple_of(second * 8, 8)
        rows = [wide(source[pl.ds(base + c, 1), :]) for c in range(3)]
        given = []
        if kind in ("both", "local", "first"):
            given = [wide(source[pl.ds(base + 6, 1), :])]
            if kind == "first":
                given += [wide(source[pl.ds(base + 3 + c, 1), :]) for c in range(3)]
        merged = []
        sums = None
        for g in range(groups):
            at = rows_item * k + 8 * g
            number = {"first": 3, "second": 7}.get(kind, 4)
            fields = [wide_fields[f, at : at + 8, :] for f in range(number)]
            dx, dy, dz, square, u = close_u(fields, rows)
            w = kernel_shape(u)
            if given:
                values = [jnp.sum(w * other, axis=1, keepdims=True) for other in given]
                merged.append(merge_lanes(values, first, lane))
            if kind != "first":
                back = [w * field for field in fields[3:]]
                if kind == "both":
                    slope = ((u * u) * u) * fields[3]
                    back += [slope * d for d in (dx, dy, dz)]
                sums = back if sums is None else [s + b for s, b in zip(sums, back)]
        outs.append((merged, merge_rows(sums, sub, places[kind]) if sums else None))
    return outs


def clear(ref, pieces):
    size = ref.shape[0] // pieces

    def some(k, carry):
        at = pl.multiple_of(k * size, size)
        ref[pl.ds(at, size)] = jnp.zeros((size,) + tuple(ref.shape[1:]), jnp.float32)
        return carry

    lax.fori_loop(0, pieces, some, 0)


def plane(ref, number, c):
    return ref[pl.ds(c, number, stride=8), :]


def first_rows(acc_first, turned, blocks):
    for s in range(blocks // 16):
        turned[s * lanes : (s + 1) * lanes, :] = acc_first[s].T


def run_density(columns, spread, fields, source, acc_first, acc_second, kind, items, start, count):
    run_items(
        columns,
        spread,
        fields,
        7 if kind == "second" else 4,
        items,
        start,
        count,
        functools.partial(density_body, source, kind),
        functools.partial(add_sums, acc_first, acc_second),
    )


def self_density_kernel(
    blocks,
    counts,
    flags,
    live,
    local_pairs,
    remote_pairs,
    table,
    columns_out,
    own,
    items,
    local_items,
    far_pairs,
    stage,
    spread,
    wide_fields,
    acc_second,
    columns,
    sem,
):
    make_columns(blocks, table, None, columns, stage)
    columns_copy = pltpu.make_async_copy(columns, columns_out, sem)
    columns_copy.start()
    make_spread(spread, density_order)
    clear(acc_second, 4)
    zero = jnp.int32(0)

    def self_step(b, n):
        put_items(items, n, b | (b << 8))
        return n + chunks(counts[b]) * (1 - flags[b])

    count = lax.fori_loop(0, blocks, self_step, zero, unroll=8)
    close_items(items, count, blocks)
    items[items.shape[0] - 1] = count
    run_density(columns, spread, wide_fields, table, None, acc_second, "self", items, 0, count)
    own[...] = plane(acc_second, blocks, 0)
    cap = local_items.shape[0] // 2

    def local_step(p, state):
        n_both, n_wall = state
        a = local_pairs[0, p]
        b = local_pairs[1, p]
        wall_b = flags[b]
        kinds = flags[a] + wall_b
        swap = jnp.where(kinds == 1, wall_b, (counts[b] < counts[a]).astype(jnp.int32)) > 0
        first = jnp.where(swap, b, a)
        second = jnp.where(swap, a, b)
        number = chunks(counts[first])
        put_items(local_items, jnp.where(kinds == 0, n_both, n_wall), first | (second << 8))
        return n_both + jnp.where(kinds == 0, number, 0), n_wall + jnp.where(kinds == 1, number, 0)

    n_both, n_wall = lax.fori_loop(0, local_pairs.shape[1], local_step, (zero, zero + cap), unroll=8)
    close_items(local_items, n_both, blocks)
    close_items(local_items, n_wall, blocks)
    local_items[cap - 1] = n_both
    local_items[2 * cap - 1] = n_wall - cap
    half = far_pairs.shape[0] // 2

    def remote_step(p, state):
        n_fluid, n_wall = state
        a = remote_pairs[0, p]
        j = remote_pairs[1, p]
        b = jnp.where(j < blocks, j, j - blocks)
        wall = flags[a]
        code = a | (b << 8) | (chunks(counts[a]) << 16)
        far_pairs[jnp.where(wall > 0, n_wall, n_fluid)] = code
        return n_fluid + 1 - wall, n_wall + wall

    n_fluid, n_wall = lax.fori_loop(0, live[0], remote_step, (zero, zero + half))
    far_pairs[half - 1] = n_fluid
    far_pairs[2 * half - 1] = n_wall - half
    for k in range(pair_pad):
        far_pairs[n_fluid + k] = zero
        far_pairs[n_wall + k] = zero
    columns_copy.wait()


def local_density_kernel(
    blocks,
    items,
    table,
    columns_in,
    own,
    spread,
    wide_fields,
    acc_first,
    acc_second,
    turned,
    columns,
    sem,
):
    columns_copy = pltpu.make_async_copy(columns_in, columns, sem)
    columns_copy.start()
    make_spread(spread, density_order)
    clear(acc_first, 1)
    clear(acc_second, 4)
    density = functools.partial(run_density, columns, spread, wide_fields, table, acc_first, acc_second)
    columns_copy.wait()
    cap = items.shape[0] // 2
    density("local", items, 0, items[cap - 1])
    density("second", items, cap, items[2 * cap - 1])
    first_rows(acc_first, turned, blocks)
    own[0] = plane(turned, blocks, 0) + plane(acc_second, blocks, 0)
    for c in range(1, 4):
        own[c] = plane(acc_second, blocks, 3 + c)


def rows_out(tiles, out, start, number):
    for k in range(number):
        out[4 * k : 4 * k + 4, :] = tiles[8 * (start + k) : 8 * (start + k) + 4, :]


def far_density_kernel(
    blocks,
    faces,
    far_pairs,
    columns_in,
    low,
    high,
    far,
    own,
    back_low,
    back_high,
    back_far,
    push,
    items,
    spread,
    wide_fields,
    acc_first,
    acc_second,
    turned,
    source,
    wall_rows,
    wall_flag,
    wall_items,
    columns,
    sem,
    sems,
):
    others = source.shape[0] // 8
    copies = fetch_source(faces, low, high, far, source, sems)
    columns_copy = pltpu.make_async_copy(columns_in, columns, sems.at[3])
    columns_copy.start()
    make_spread(spread, density_order)
    for copy in copies:
        copy.wait()
    wall_rows[...] = plane(source, others, 7)
    flag_copy = pltpu.make_async_copy(wall_rows, wall_flag, sem)
    flag_copy.start()
    clear(acc_first, 1)
    clear(acc_second, 4)
    flag_copy.wait()
    zero = jnp.int32(0)
    half = far_pairs.shape[0] // 2
    cap = items.shape[0] // 2

    def fluid_second(code):
        return wall_flag[(code >> 8) & 255, 0] < 0.5

    def wall_step(q, n):
        for k in range(pair_pad):
            code = far_pairs[half + q * pair_pad + k]
            put_items(wall_items, n, code & 65535)
            n = n + jnp.where(fluid_second(code), code >> 16, 0)
        return n

    def fluid_step(q, state):
        n_both, n_first = state
        for k in range(pair_pad):
            code = far_pairs[q * pair_pad + k]
            number = code >> 16
            fluid = fluid_second(code)
            put_items(items, jnp.where(fluid, n_both, n_first), code & 65535)
            n_both = n_both + jnp.where(fluid, number, 0)
            n_first = n_first + jnp.where(fluid, 0, number)
        return n_both, n_first

    def passes(pairs):
        return (pairs + (pair_pad - 1)) >> 3

    n_both, n_first = lax.fori_loop(0, passes(far_pairs[half - 1]), fluid_step, (zero, zero + cap))
    close_items(items, n_both, blocks)
    close_items(items, n_first, blocks)
    items[cap - 1] = n_both
    n_second = lax.fori_loop(0, passes(far_pairs[2 * half - 1]), wall_step, zero)
    close_items(wall_items, n_second, blocks)
    columns_copy.wait()
    density = functools.partial(run_density, columns, spread, wide_fields, source, acc_first, acc_second)
    density("second", wall_items, 0, n_second)
    density("both", items, 0, n_both)
    density("first", items, cap, n_first - cap)
    first_rows(acc_first, turned, blocks)
    for c in range(4):
        own[c] = plane(turned, blocks, c)
    rows_out(acc_second, back_low, 0, faces)
    rows_out(acc_second, back_high, faces, faces)
    rows_out(acc_second, back_far, 2 * faces, others - 2 * faces)
    for c in range(3):
        push[c] = plane(acc_second, others, 4 + c)


def fetch(pairs, sems):
    copies = [pltpu.make_async_copy(a, b, sems.at[k]) for k, (a, b) in enumerate(pairs)]
    for copy in copies:
        copy.start()
    return copies


def fetch_source(faces, low, high, far, source, sems):
    return fetch(
        (
            (low, source.at[0 : faces * 8]),
            (high, source.at[faces * 8 : 2 * faces * 8]),
            (far, source.at[2 * faces * 8 :]),
        ),
        sems,
    )


def fluid_mask(blocks, table):
    return jnp.logical_and(plane(table, blocks, 6) > 0.0, plane(table, blocks, 7) < 0.5)


def density_kernel(
    blocks,
    faces,
    per_peer,
    send,
    table,
    self_sum,
    local_sum,
    far_sum,
    from_above,
    from_below,
    returned,
    density,
    slopes,
    total,
):
    total[pl.ds(0, blocks, stride=8), :] = self_sum[...] + local_sum[0] + far_sum[0]
    for c in range(1, 8):
        total[pl.ds(c, blocks, stride=8), :] = jnp.zeros((blocks, lanes), jnp.float32)
    for k in range(faces):
        at = 8 * (blocks - faces + k)
        total[at : at + 4, :] += from_above[4 * k : 4 * k + 4, :]
        total[8 * k : 8 * k + 4, :] += from_below[4 * k : 4 * k + 4, :]

    def give(t, carry):
        for k in range(per_peer):
            at = pl.multiple_of(send[0, k, t] * 8, 8)
            source = pl.multiple_of((t * per_peer + k) * 4, 4)
            total[pl.ds(at, 4), :] += returned[pl.ds(source, 4), :]
        return carry

    lax.fori_loop(0, send.shape[2], give, 0, unroll=2)
    density[...] = jnp.where(fluid_mask(blocks, table), kernel_norm * plane(total, blocks, 0), 0.0)
    for c in range(3):
        slopes[c] = plane(total, blocks, 1 + c)


def force_fields(source, density, number, pressed):
    mass = plane(source, number, 6)
    rho = jnp.where(mass > 0.0, density, 1.0)
    inverse = 1.0 / jnp.where(rho > 0.0, rho, 1.0)
    press = 10.0 * (rho - 1.0) * inverse * inverse
    pressed[...] = press * mass
    return inverse, press, mass * inverse


def force_body(source, pressed, kind, wide_fields, decoded):
    lane = lax.broadcasted_iota(jnp.int32, (8, lanes), 1)
    sub = lax.broadcasted_iota(jnp.int32, (8, lanes), 0)
    outs = []
    for k, (first, second, row) in enumerate(decoded):
        base = pl.multiple_of(second * 8, 8)
        rows = [wide(source[pl.ds(base + c, 1), :]) for c in range(6 if kind == "second" else 8)]
        if kind != "second":
            press = wide(pressed[pl.ds(second, 1), :])
        merged = []
        sums = None
        for g in range(groups):
            at = rows_item * k + 8 * g
            fields = [wide_fields[f, at : at + 8, :] for f in range(8 if kind == "first" else 9)]
            dx, dy, dz, square, u = close_u(fields, rows)
            u3 = (u * u) * u
            if kind != "first":
                u3 = u3 * fields[8]
            damp = (u3 * (square * (1.0 / (square + 0.25 * softening)))) * (
                fields[6] if kind == "second" else fields[6] * rows[7]
            )
            pull = u3 * (fields[7] if kind == "second" else fields[7] * rows[6] + press)
            pushed = [pull * d for d in (dx, dy, dz)]
            damped = [damp * (fields[3 + c] - rows[3 + c]) for c in range(3)]
            if kind == "second":
                values = damped + pushed
            else:
                values = [a - b for a, b in zip(pushed, damped)]
            if kind in ("local", "first"):
                merged.append(
                    merge_lanes([jnp.sum(v, axis=1, keepdims=True) for v in values], first, lane)
                )
            if kind != "first":
                sums = values if sums is None else [s + v for s, v in zip(sums, values)]
        outs.append((merged, merge_rows(sums, sub, range(1, 7)) if sums else None))
    return outs


def run_force(columns, spread, fields, source, pressed, acc_first, acc_second, kind, items, cap):
    run_items(
        columns,
        spread,
        fields,
        8 if kind == "first" else 9,
        items,
        0,
        items[cap - 1],
        functools.partial(force_body, source, pressed, kind),
        functools.partial(add_sums, acc_first, acc_second),
        kind != "self",
    )


def far_send_kernel(
    blocks,
    faces,
    per_peer,
    send,
    items,
    table,
    density,
    low,
    high,
    far,
    push,
    columns_out,
    own_source,
    pressed,
    out_low,
    out_high,
    out_far,
    stage,
    last,
    source,
    spread,
    wide_fields,
    acc_second,
    columns,
    sems,
):
    others = source.shape[0] // 8
    copies = fetch_source(faces, low, high, far, source, sems)
    own_source[...] = table[...]
    inverse, press, scaled = force_fields(own_source, density[...], blocks, pressed)
    own_source[pl.ds(7, blocks, stride=8), :] = inverse
    last[...] = jnp.zeros(last.shape, jnp.float32)
    for p, piece in enumerate(split3(press)):
        last[pl.ds(p, blocks, stride=8), :] = piece
    make_columns(blocks, own_source, last, columns, stage)
    own_source[pl.ds(7, blocks, stride=8), :] = scaled
    columns_copy = pltpu.make_async_copy(columns, columns_out, sems.at[3])
    columns_copy.start()
    make_spread(spread, force_order)
    clear(acc_second, 4)
    for copy in copies:
        copy.wait()
    run_force(columns, spread, wide_fields, source, None, None, acc_second, "second", items, items.shape[0] // 2)
    for c in range(3):
        acc_second[pl.ds(4 + c, others, stride=8), :] = push[c] - plane(acc_second, others, 4 + c)
    acc_second[pl.ds(0, faces, stride=8), :] = density[0:faces, :]
    acc_second[pl.ds(8 * faces, faces, stride=8), :] = density[blocks - faces :, :]

    def pick(t, carry):
        for k in range(per_peer):
            at = 8 * (2 * faces + t * per_peer + k)
            acc_second[pl.ds(at, 1), :] = density[pl.ds(send[0, k, t], 1), :]
        return carry

    lax.fori_loop(0, send.shape[2], pick, 0, unroll=4)
    out_low[...] = acc_second[0 : 8 * faces, :]
    out_high[...] = acc_second[8 * faces : 16 * faces, :]
    out_far[...] = acc_second[16 * faces :, :]
    columns_copy.wait()


def own_force_kernel(
    blocks,
    self_items,
    both_items,
    columns_in,
    source,
    pressed,
    own,
    spread,
    wide_fields,
    acc_first,
    acc_second,
    turned,
    columns,
    sem,
):
    columns_copy = pltpu.make_async_copy(columns_in, columns, sem)
    columns_copy.start()
    make_spread(spread, force_order)
    clear(acc_first, 1)
    clear(acc_second, 4)
    columns_copy.wait()
    force = functools.partial(
        run_force, columns, spread, wide_fields, source, pressed, acc_first, acc_second
    )
    force("self", self_items, self_items.shape[0])
    force("local", both_items, both_items.shape[0] // 2)
    first_rows(acc_first, turned, blocks)
    for c in range(3):
        own[c] = plane(turned, blocks, c) - plane(acc_second, blocks, 1 + c)


def far_force_kernel(
    blocks,
    faces,
    items,
    columns_in,
    low,
    high,
    far,
    from_below,
    from_above,
    returned,
    own,
    source,
    source_density,
    pressed,
    spread,
    wide_fields,
    acc_first,
    turned,
    columns,
    sems,
):
    others = source.shape[0] // 8
    copies = fetch_source(faces, low, high, far, source, sems)
    columns_copy = pltpu.make_async_copy(columns_in, columns, sems.at[3])
    columns_copy.start()
    source_density[0:faces, :] = plane(from_below, faces, 0)
    source_density[faces : 2 * faces, :] = plane(from_above, faces, 0)
    source_density[2 * faces :, :] = plane(returned, others - 2 * faces, 0)
    make_spread(spread, force_order)
    clear(acc_first, 1)
    for copy in copies:
        copy.wait()
    scaled = force_fields(source, source_density[...], others, pressed)[2]
    source[pl.ds(7, others, stride=8), :] = scaled
    columns_copy.wait()
    run_force(columns, spread, wide_fields, source, pressed, acc_first, None, "first", items, items.shape[0] // 2)
    first_rows(acc_first, turned, blocks)
    for c in range(3):
        own[c] = plane(turned, blocks, c)


def final_kernel(
    blocks,
    faces,
    per_peer,
    send,
    table,
    density,
    slopes,
    local_sum,
    far_sum,
    own_force,
    far_force,
    from_above,
    from_below,
    returned,
    out,
    total,
):
    total[...] = jnp.zeros(total.shape, jnp.float32)
    total[8 * (blocks - faces) :, :] += from_above[...]
    total[0 : 8 * faces, :] += from_below[...]

    def give(t, carry):
        for k in range(per_peer):
            at = pl.multiple_of(send[0, k, t] * 8, 8)
            source = pl.multiple_of((t * per_peer + k) * 8, 8)
            total[pl.ds(at, 8), :] += returned[pl.ds(source, 8), :]
        return carry

    lax.fori_loop(0, send.shape[2], give, 0, unroll=2)
    fluid = fluid_mask(blocks, table)
    mass = plane(table, blocks, 6)
    over_mass = 1.0 / jnp.where(mass > 0.0, mass, 1.0)
    over_rho = 1.0 / jnp.where(fluid, density[...], 1.0)
    press = jnp.where(fluid, 10.0 * (density[...] - 1.0) * over_rho * over_rho, 0.0)
    for c in range(3):
        force = own_force[c] * over_mass + far_force[c]
        force = force + local_sum[1 + c] + far_sum[1 + c]
        force = force + plane(total, blocks, 1 + c) * over_rho + plane(total, blocks, 4 + c)
        out[c] = jnp.where(fluid, kernel_norm * (force - press * slopes[c]), 0.0)


def f32(*shape):
    return jax.ShapeDtypeStruct(shape, jnp.float32)


def i32(*shape):
    return jax.ShapeDtypeStruct(shape, jnp.int32)


def to_above(shard):
    count = lax.axis_size("slab")
    return lax.ppermute(shard, "slab", [(i, i + 1) for i in range(count - 1)])


def to_below(shard):
    count = lax.axis_size("slab")
    return lax.ppermute(shard, "slab", [(i + 1, i) for i in range(count - 1)])


def swap_tiles(rows, tiles):
    parts = rows.reshape(tiles, rows.shape[0] // tiles, lanes)
    return lax.all_to_all(parts, "tile", split_axis=0, concat_axis=0, tiled=True).reshape(rows.shape)


def on_device(
    positions,
    velocities,
    masses,
    wall_areas,
    normals,
    wall_flags,
    counts,
    send_list,
    local_pairs,
    remote_pairs,
    remote_live,
):
    blocks = positions.shape[1]
    faces = blocks // 4
    tiles = lax.axis_size("tile")
    per_peer = send_list.shape[2]
    offered = send_list.shape[1] * per_peer
    send = jnp.swapaxes(send_list, 1, 2)
    others = 2 * faces + offered
    n_local = local_pairs.shape[0]
    n_remote = remote_pairs.shape[0]
    per = lanes // rows_item
    spare = 3 * batch * density_halves
    self_cap = per * blocks + spare
    own_cap = per * n_local + spare
    far_cap = per * n_remote + spare
    pair_cap = n_remote + 2 * pair_pad
    columns_shape = jax.ShapeDtypeStruct((blocks // 4 + 1, lanes, lanes), bf16)
    columns_scratch = vmem((blocks // 4 + 1, lanes, lanes), bf16)
    stage = vmem((blocks * 32, lanes), jnp.float32)

    def fields(number, halves):
        return [vmem((lanes + 4 * rows_item, 128 * number), bf16), vmem((halves, number, lanes, lanes), jnp.float32)]

    acc_first = vmem((blocks // 16 + 1, lanes, lanes), jnp.float32)
    turned = vmem((blocks * 8, lanes), jnp.float32)

    def tiles_of(number):
        return vmem((number * 8, lanes), jnp.float32)

    def cost(flops):
        return pl.CostEstimate(flops=flops, bytes_accessed=400_000, transcendentals=0)

    table, picked, head, tail = pl.pallas_call(
        functools.partial(pack_kernel, blocks, faces, per_peer),
        out_shape=(f32(blocks * 8, lanes), f32(offered * 8, lanes), f32(faces * 8, lanes), f32(faces * 8, lanes)),
        in_specs=[spec(smem)] + [spec(vmem)] * 7,
        out_specs=[spec(vmem)] * 4,
        compiler_params=params(grant_mib),
        name="pack",
    )(
        send,
        positions,
        velocities,
        masses,
        wall_areas,
        normals,
        wall_flags[None, :],
        counts[None, :],
    )
    low = to_above(tail)
    high = to_below(head)
    far = swap_tiles(picked, tiles)

    columns, self_sum, self_items, own_items, far_pairs = pl.pallas_call(
        functools.partial(self_density_kernel, blocks),
        out_shape=(
            columns_shape,
            f32(blocks, lanes),
            i32(self_cap),
            i32(2 * own_cap),
            i32(2 * pair_cap),
        ),
        in_specs=[spec(smem)] * 5 + [spec(vmem)],
        out_specs=[spec(pl.ANY), spec(vmem)] + [spec(smem)] * 3,
        scratch_shapes=[stage]
        + fields(8, density_halves)
        + [tiles_of(blocks), columns_scratch, pltpu.SemaphoreType.DMA],
        compiler_params=params(grant_mib),
        cost_estimate=cost(40_000_000),
        name="self_density",
    )(counts, wall_flags, remote_live, local_pairs.T, remote_pairs.T, table)

    far_sum, back_low, back_high, back_far, push, far_items = pl.pallas_call(
        functools.partial(far_density_kernel, blocks, faces),
        out_shape=(
            f32(4, blocks, lanes),
            f32(faces * 4, lanes),
            f32(faces * 4, lanes),
            f32(offered * 4, lanes),
            f32(3, others, lanes),
            i32(2 * far_cap),
        ),
        in_specs=[spec(smem)] + [spec(pl.ANY)] * 4,
        out_specs=[spec(vmem)] * 5 + [spec(smem)],
        scratch_shapes=fields(8, density_halves)
        + [acc_first, tiles_of(others), turned]
        + [
            tiles_of(others),
            vmem((others, lanes), jnp.float32),
            smem((others, lanes), jnp.float32),
            smem((far_cap,), jnp.int32),
            columns_scratch,
            pltpu.SemaphoreType.DMA,
            pltpu.SemaphoreType.DMA((4,)),
        ],
        compiler_params=params(grant_mib),
        cost_estimate=cost(100_000_000),
        name="far_density",
    )(far_pairs, columns, low, high, far)

    from_above = to_below(back_low)
    from_below = to_above(back_high)
    returned = swap_tiles(back_far, tiles)

    local_sum = pl.pallas_call(
        functools.partial(local_density_kernel, blocks),
        out_shape=f32(4, blocks, lanes),
        in_specs=[spec(smem), spec(vmem), spec(pl.ANY)],
        out_specs=spec(vmem),
        scratch_shapes=fields(8, density_halves)
        + [acc_first, tiles_of(blocks), turned, columns_scratch, pltpu.SemaphoreType.DMA],
        compiler_params=params(grant_mib),
        cost_estimate=cost(40_000_000),
        name="local_density",
    )(own_items, table, columns)

    density, slopes = pl.pallas_call(
        functools.partial(density_kernel, blocks, faces, per_peer),
        out_shape=(f32(blocks, lanes), f32(3, blocks, lanes)),
        in_specs=[spec(smem)] + [spec(vmem)] * 7,
        out_specs=[spec(vmem)] * 2,
        scratch_shapes=[tiles_of(blocks)],
        compiler_params=params(grant_mib),
        name="density",
    )(send, table, self_sum, local_sum, far_sum, from_above, from_below, returned)

    force_columns, force_table, pressed, out_low, out_high, out_far = pl.pallas_call(
        functools.partial(far_send_kernel, blocks, faces, per_peer),
        out_shape=(
            columns_shape,
            f32(blocks * 8, lanes),
            f32(blocks, lanes),
            f32(faces * 8, lanes),
            f32(faces * 8, lanes),
            f32(offered * 8, lanes),
        ),
        in_specs=[spec(smem)] * 2 + [spec(vmem)] * 2 + [spec(pl.ANY)] * 3 + [spec(vmem)],
        out_specs=[spec(pl.ANY)] + [spec(vmem)] * 5,
        scratch_shapes=[stage, tiles_of(blocks), tiles_of(others)] + fields(10, force_halves) + [tiles_of(others), columns_scratch, pltpu.SemaphoreType.DMA((4,))],
        compiler_params=params(grant_mib),
        cost_estimate=cost(100_000_000),
        name="far_send",
    )(send, far_items, table, density, low, high, far, push)

    force_above = to_below(out_low)
    force_below = to_above(out_high)
    force_far = swap_tiles(out_far, tiles)

    own_force = pl.pallas_call(
        functools.partial(own_force_kernel, blocks),
        out_shape=f32(3, blocks, lanes),
        in_specs=[spec(smem)] * 2 + [spec(pl.ANY)] + [spec(vmem)] * 2,
        out_specs=spec(vmem),
        scratch_shapes=fields(10, force_halves)
        + [acc_first, tiles_of(blocks), turned, columns_scratch, pltpu.SemaphoreType.DMA],
        compiler_params=params(grant_mib),
        cost_estimate=cost(80_000_000),
        name="own_force",
    )(self_items, own_items, force_columns, force_table, pressed)

    far_force = pl.pallas_call(
        functools.partial(far_force_kernel, blocks, faces),
        out_shape=f32(3, blocks, lanes),
        in_specs=[spec(smem)] + [spec(pl.ANY)] * 4 + [spec(vmem)] * 3,
        out_specs=spec(vmem),
        scratch_shapes=[
            tiles_of(others),
            vmem((others, lanes), jnp.float32),
            vmem((others, lanes), jnp.float32),
        ]
        + fields(10, force_halves)
        + [acc_first, turned, columns_scratch, pltpu.SemaphoreType.DMA((4,))],
        compiler_params=params(grant_mib),
        cost_estimate=cost(100_000_000),
        name="far_force",
    )(far_items, force_columns, low, high, far, force_below, force_above, force_far)

    acceleration = pl.pallas_call(
        functools.partial(final_kernel, blocks, faces, per_peer),
        out_shape=f32(3, blocks, lanes),
        in_specs=[spec(smem)] + [spec(vmem)] * 10,
        out_specs=spec(vmem),
        scratch_shapes=[tiles_of(blocks)],
        compiler_params=params(grant_mib),
        name="total",
    )(
        send,
        table,
        density,
        slopes,
        local_sum,
        far_sum,
        own_force,
        far_force,
        force_above,
        force_below,
        force_far,
    )
    return (density, acceleration)


def solution(mesh):
    placed = (
        P(None, ("slab", "tile"), None),
        P(None, ("slab", "tile"), None),
        P(("slab", "tile"), None),
        P(("slab", "tile"), None),
        P(None, ("slab", "tile"), None),
        P(("slab", "tile")),
        P(("slab", "tile")),
        P(("slab", "tile"), None, None),
        P(("slab", "tile"), None),
        P(("slab", "tile"), None),
        P(("slab", "tile")),
    )
    return jax.shard_map(
        on_device,
        mesh=mesh,
        in_specs=placed,
        out_specs=(P(("slab", "tile"), None), P(None, ("slab", "tile"), None)),
        check_vma=False,
    )
```

```python
import functools
import math

import jax
import jax.numpy as jnp
from jax import lax
from jax.experimental import pallas as pl
from jax.experimental.pallas import tpu as pltpu
from jax.sharding import PartitionSpec as P

kernel_norm = 21.0 / (16.0 * math.pi)
softening = 0.01
tiny = 1e-30
lanes = 128
rows_item = 32
groups = rows_item // 8
batch = lanes // rows_item
density_halves = 4
force_halves = 4
pair_pad = 8
grant_mib = 64
density_order = (0, 1, 2, 6, 3, 4, 5)
force_order = (0, 1, 2, 3, 4, 5, 7, 8, 6)
bf16 = jnp.bfloat16
vmem = pltpu.VMEM
smem = pltpu.SMEM


def spec(space):
    return pl.BlockSpec(memory_space=space)


def params(mib):
    return pltpu.CompilerParams(vmem_limit_bytes=mib * 1024 * 1024)


def column_of(row):
    number = row.shape[1]
    same = lax.broadcasted_iota(jnp.int32, (number, number), 0) == lax.broadcasted_iota(
        jnp.int32, (number, number), 1
    )
    return jnp.sum(jnp.where(same, row, 0.0), axis=1, keepdims=True)


def pack_kernel(
    blocks, faces, per_peer, send, pos, vel, mass, area, normal, flags_row, counts_row, table, picked, head, tail
):
    slot = lax.broadcasted_iota(jnp.int32, (blocks, lanes), 1).astype(jnp.float32)
    alive = slot < column_of(counts_row[...].astype(jnp.float32))
    wall_value = column_of(flags_row[...].astype(jnp.float32)) + jnp.zeros((blocks, lanes), jnp.float32)
    wall = wall_value > 0.5
    nx, ny, nz = normal[0], normal[1], normal[2]
    length = jnp.sqrt(nx * nx + ny * ny + nz * nz)
    weight = jnp.where(alive, jnp.where(wall, area[...], mass[...]), 0.0)
    wall_scale = weight / length
    parts = (nx, ny, nz)
    for c in range(3):
        table[pl.ds(c, blocks, stride=8), :] = 0.5 * pos[c]
        table[pl.ds(3 + c, blocks, stride=8), :] = jnp.where(wall, wall_scale * parts[c], vel[c])
    table[pl.ds(6, blocks, stride=8), :] = weight
    table[pl.ds(7, blocks, stride=8), :] = wall_value
    head[...] = table[0 : faces * 8, :]
    tail[...] = table[(blocks - faces) * 8 : blocks * 8, :]

    def pick(t, carry):
        for k in range(per_peer):
            source = pl.multiple_of(send[0, k, t] * 8, 8)
            at = pl.multiple_of((t * per_peer + k) * 8, 8)
            picked[pl.ds(at, 8), :] = table[pl.ds(source, 8), :]
        return carry

    lax.fori_loop(0, picked.shape[0] // (8 * per_peer), pick, 0, unroll=2)


def rounded(x):
    return x.astype(bf16).astype(jnp.float32)


def split3(x):
    high = rounded(x)
    rest = x - high
    middle = rounded(rest)
    return high, middle, rest - middle


def make_spread(spread, order):
    shape = (lanes, spread.shape[1])
    k = lax.broadcasted_iota(jnp.int32, shape, 0) & 31
    tile = lax.broadcasted_iota(jnp.int32, shape, 1) >> 7
    want = jnp.full(shape, -1, jnp.int32)
    for t, field in enumerate(order):
        want = jnp.where(tile == t, field, want)
    hit = jnp.logical_and(k < 24, (k & 7) == want)
    hit = jnp.logical_or(hit, jnp.logical_and(jnp.logical_and(k >= 24, k < 27), want == 8))
    spread[0:lanes, :] = jnp.where(hit, 1.0, 0.0).astype(bf16)
    lane = lax.broadcasted_iota(jnp.int32, (rows_item, lanes), 1) >> 5
    for j in range(4):
        at = lanes + rows_item * j
        spread[at : at + rows_item, 0:lanes] = jnp.where(lane == j, 1.0, 0.0).astype(bf16)


def make_columns(blocks, table, last, columns, stage):
    for b in range(blocks):
        for p, piece in enumerate(split3(table[8 * b : 8 * b + 8, :])):
            stage[32 * b + 8 * p : 32 * b + 8 * p + 8, :] = piece
        if last is None:
            stage[32 * b + 24 : 32 * b + 32, :] = jnp.zeros((8, lanes), jnp.float32)
        else:
            stage[32 * b + 24 : 32 * b + 32, :] = last[8 * b : 8 * b + 8, :]

    def some(g, carry):
        turned = stage[pl.ds(pl.multiple_of(g * lanes, lanes), lanes), :].T
        columns[g] = turned.astype(bf16)
        return carry

    lax.fori_loop(0, blocks // 4, some, 0, unroll=2)
    columns[blocks // 4] = jnp.zeros((lanes, lanes), bf16)


def put_items(items, at, code):
    for k in range(lanes // rows_item):
        items[at + k] = code | (k << 16)


def close_items(items, count, blocks):
    for k in range(2 * batch * density_halves):
        items[count + k] = jnp.int32(blocks)


def chunks(count):
    return (count + (rows_item - 1)) >> 5


def decode(code):
    first = code & 255
    second = (code >> 8) & 255
    row = pl.multiple_of((code >> 16) * rows_item, rows_item)
    return first, second, row


def wide(row):
    return jnp.broadcast_to(row, (8, lanes))


def spread_fields(columns, spread, wide_fields, tiles, decoded):
    parts = []
    for first, second, row in decoded:
        mask = spread[pl.ds(pl.multiple_of(lanes + (first & 3) * rows_item, rows_item), rows_item), 0:lanes]
        parts.append(columns[first >> 2, pl.ds(row, rows_item), :] * mask)
    left = jnp.concatenate(parts, axis=0)
    for t in range((tiles + 1) // 2):
        both = jnp.dot(left, spread[0:lanes, 256 * t : 256 * t + 256], preferred_element_type=jnp.float32)
        wide_fields[2 * t] = both[:, 0:lanes]
        wide_fields[2 * t + 1] = both[:, lanes : 2 * lanes]


def close_u(fields, rows):
    dx = fields[0] - rows[0]
    dy = fields[1] - rows[1]
    dz = fields[2] - rows[2]
    square = dx * dx + dy * dy + dz * dz
    safe = jnp.maximum(square, tiny)
    q = safe * lax.rsqrt(safe)
    u = jnp.maximum(1.0 - q, 0.0)
    return dx, dy, dz, square, u


def kernel_shape(u):
    u2 = u * u
    return (u2 * u2) * (5.0 - 4.0 * u)


def run_items(columns, spread, wide_fields, tiles, items, start, count, body, finish, alternate=False):
    halves = wide_fields.shape[0]
    size = batch * halves

    def decoded_of(it, h):
        return [decode(items[start + (it * halves + h) * batch + k]) for k in range(batch)]

    def prepare(it, hs):
        for h in hs:
            spread_fields(columns, spread, wide_fields.at[h], tiles, decoded_of(it, h))

    def work(it, hs):
        done = []
        for h in hs:
            decoded = decoded_of(it, h)
            done.append((decoded, body(wide_fields.at[h], decoded)))
        return done

    group = halves // 2 if alternate else halves
    front, rear = range(group), range(group, halves)

    def step(it, carry):
        prepare(it, rear)
        done = work(it, front)
        prepare(it + 1, front)
        done += work(it, rear)
        for decoded, outs in done:
            finish(decoded, outs)
        return carry

    prepare(0, front)
    lax.fori_loop(0, (count + size - 1) >> (size.bit_length() - 1), step, 0)


def merge_lanes(values, first, lane):
    base = (first & 15) * 8
    total = jnp.zeros((8, lanes), jnp.float32)
    for c, value in enumerate(values):
        total = jnp.where(lane == base + c, value, total)
    return total


def merge_rows(values, sub, places):
    total = jnp.zeros((8, lanes), jnp.float32)
    for c, value in zip(places, values):
        total = jnp.where(sub == c, jnp.sum(value, axis=0, keepdims=True), total)
    return total


def add_sums(acc_first, acc_second, decoded, outs):
    for (first, second, row), (merged, tile) in zip(decoded, outs):
        if merged:
            slab = first >> 4
            for g in range(groups):
                acc_first[slab, pl.ds(row + 8 * g, 8), :] += merged[g]
        if tile is not None:
            at = pl.multiple_of(second * 8, 8)
            acc_second[pl.ds(at, 8), :] += tile


def density_body(source, kind, wide_fields, decoded):
    lane = lax.broadcasted_iota(jnp.int32, (8, lanes), 1)
    sub = lax.broadcasted_iota(jnp.int32, (8, lanes), 0)
    places = {"self": (0,), "local": (0,), "both": (0, 1, 2, 3), "second": (0, 4, 5, 6)}
    outs = []
    for k, (first, second, row) in enumerate(decoded):
        base = pl.multiple_of(second * 8, 8)
        rows = [wide(source[pl.ds(base + c, 1), :]) for c in range(3)]
        given = []
        if kind in ("both", "local", "first"):
            given = [wide(source[pl.ds(base + 6, 1), :])]
            if kind == "first":
                given += [wide(source[pl.ds(base + 3 + c, 1), :]) for c in range(3)]
        merged = []
        sums = None
        for g in range(groups):
            at = rows_item * k + 8 * g
            number = {"first": 3, "second": 7}.get(kind, 4)
            fields = [wide_fields[f, at : at + 8, :] for f in range(number)]
            dx, dy, dz, square, u = close_u(fields, rows)
            w = kernel_shape(u)
            if given:
                values = [jnp.sum(w * other, axis=1, keepdims=True) for other in given]
                merged.append(merge_lanes(values, first, lane))
            if kind != "first":
                back = [w * field for field in fields[3:]]
                if kind == "both":
                    slope = ((u * u) * u) * fields[3]
                    back += [slope * d for d in (dx, dy, dz)]
                sums = back if sums is None else [s + b for s, b in zip(sums, back)]
        outs.append((merged, merge_rows(sums, sub, places[kind]) if sums else None))
    return outs


def clear(ref, pieces):
    size = ref.shape[0] // pieces

    def some(k, carry):
        at = pl.multiple_of(k * size, size)
        ref[pl.ds(at, size)] = jnp.zeros((size,) + tuple(ref.shape[1:]), jnp.float32)
        return carry

    lax.fori_loop(0, pieces, some, 0)


def plane(ref, number, c):
    return ref[pl.ds(c, number, stride=8), :]


def first_rows(acc_first, turned, blocks):
    for s in range(blocks // 16):
        turned[s * lanes : (s + 1) * lanes, :] = acc_first[s].T


def run_density(columns, spread, fields, source, acc_first, acc_second, kind, items, start, count):
    run_items(
        columns,
        spread,
        fields,
        7 if kind == "second" else 4,
        items,
        start,
        count,
        functools.partial(density_body, source, kind),
        functools.partial(add_sums, acc_first, acc_second),
    )


def self_density_kernel(
    blocks,
    counts,
    flags,
    live,
    local_pairs,
    remote_pairs,
    table,
    columns_out,
    own,
    items,
    local_items,
    far_pairs,
    stage,
    spread,
    wide_fields,
    acc_second,
    columns,
    sem,
):
    make_columns(blocks, table, None, columns, stage)
    columns_copy = pltpu.make_async_copy(columns, columns_out, sem)
    columns_copy.start()
    make_spread(spread, density_order)
    clear(acc_second, 4)
    zero = jnp.int32(0)

    def self_step(b, n):
        put_items(items, n, b | (b << 8))
        return n + chunks(counts[b]) * (1 - flags[b])

    count = lax.fori_loop(0, blocks, self_step, zero, unroll=8)
    close_items(items, count, blocks)
    items[items.shape[0] - 1] = count
    run_density(columns, spread, wide_fields, table, None, acc_second, "self", items, 0, count)
    own[...] = plane(acc_second, blocks, 0)
    cap = local_items.shape[0] // 2

    def local_step(p, state):
        n_both, n_wall = state
        a = local_pairs[0, p]
        b = local_pairs[1, p]
        wall_b = flags[b]
        kinds = flags[a] + wall_b
        swap = jnp.where(kinds == 1, wall_b, (counts[b] < counts[a]).astype(jnp.int32)) > 0
        first = jnp.where(swap, b, a)
        second = jnp.where(swap, a, b)
        number = chunks(counts[first])
        put_items(local_items, jnp.where(kinds == 0, n_both, n_wall), first | (second << 8))
        return n_both + jnp.where(kinds == 0, number, 0), n_wall + jnp.where(kinds == 1, number, 0)

    n_both, n_wall = lax.fori_loop(0, local_pairs.shape[1], local_step, (zero, zero + cap), unroll=8)
    close_items(local_items, n_both, blocks)
    close_items(local_items, n_wall, blocks)
    local_items[cap - 1] = n_both
    local_items[2 * cap - 1] = n_wall - cap
    half = far_pairs.shape[0] // 2

    def remote_step(p, state):
        n_fluid, n_wall = state
        a = remote_pairs[0, p]
        j = remote_pairs[1, p]
        b = jnp.where(j < blocks, j, j - blocks)
        wall = flags[a]
        code = a | (b << 8) | (chunks(counts[a]) << 16)
        far_pairs[jnp.where(wall > 0, n_wall, n_fluid)] = code
        return n_fluid + 1 - wall, n_wall + wall

    n_fluid, n_wall = lax.fori_loop(0, live[0], remote_step, (zero, zero + half))
    far_pairs[half - 1] = n_fluid
    far_pairs[2 * half - 1] = n_wall - half
    for k in range(pair_pad):
        far_pairs[n_fluid + k] = zero
        far_pairs[n_wall + k] = zero
    columns_copy.wait()


def local_density_kernel(
    blocks,
    items,
    table,
    columns_in,
    own,
    spread,
    wide_fields,
    acc_first,
    acc_second,
    turned,
    columns,
    sem,
):
    columns_copy = pltpu.make_async_copy(columns_in, columns, sem)
    columns_copy.start()
    make_spread(spread, density_order)
    clear(acc_first, 1)
    clear(acc_second, 4)
    density = functools.partial(run_density, columns, spread, wide_fields, table, acc_first, acc_second)
    columns_copy.wait()
    cap = items.shape[0] // 2
    density("local", items, 0, items[cap - 1])
    density("second", items, cap, items[2 * cap - 1])
    first_rows(acc_first, turned, blocks)
    own[0] = plane(turned, blocks, 0) + plane(acc_second, blocks, 0)
    for c in range(1, 4):
        own[c] = plane(acc_second, blocks, 3 + c)


def rows_out(tiles, out, start, number):
    for k in range(number):
        out[4 * k : 4 * k + 4, :] = tiles[8 * (start + k) : 8 * (start + k) + 4, :]


def far_density_kernel(
    blocks,
    faces,
    far_pairs,
    columns_in,
    low,
    high,
    far,
    own,
    back_low,
    back_high,
    back_far,
    push,
    items,
    spread,
    wide_fields,
    acc_first,
    acc_second,
    turned,
    source,
    wall_rows,
    wall_flag,
    wall_items,
    columns,
    sem,
    sems,
):
    others = source.shape[0] // 8
    copies = fetch_source(faces, low, high, far, source, sems)
    columns_copy = pltpu.make_async_copy(columns_in, columns, sems.at[3])
    columns_copy.start()
    make_spread(spread, density_order)
    for copy in copies:
        copy.wait()
    wall_rows[...] = plane(source, others, 7)
    flag_copy = pltpu.make_async_copy(wall_rows, wall_flag, sem)
    flag_copy.start()
    clear(acc_first, 1)
    clear(acc_second, 4)
    flag_copy.wait()
    zero = jnp.int32(0)
    half = far_pairs.shape[0] // 2
    cap = items.shape[0] // 2

    def fluid_second(code):
        return wall_flag[(code >> 8) & 255, 0] < 0.5

    def wall_step(q, n):
        for k in range(pair_pad):
            code = far_pairs[half + q * pair_pad + k]
            put_items(wall_items, n, code & 65535)
            n = n + jnp.where(fluid_second(code), code >> 16, 0)
        return n

    def fluid_step(q, state):
        n_both, n_first = state
        for k in range(pair_pad):
            code = far_pairs[q * pair_pad + k]
            number = code >> 16
            fluid = fluid_second(code)
            put_items(items, jnp.where(fluid, n_both, n_first), code & 65535)
            n_both = n_both + jnp.where(fluid, number, 0)
            n_first = n_first + jnp.where(fluid, 0, number)
        return n_both, n_first

    def passes(pairs):
        return (pairs + (pair_pad - 1)) >> 3

    n_both, n_first = lax.fori_loop(0, passes(far_pairs[half - 1]), fluid_step, (zero, zero + cap))
    close_items(items, n_both, blocks)
    close_items(items, n_first, blocks)
    items[cap - 1] = n_both
    n_second = lax.fori_loop(0, passes(far_pairs[2 * half - 1]), wall_step, zero)
    close_items(wall_items, n_second, blocks)
    columns_copy.wait()
    density = functools.partial(run_density, columns, spread, wide_fields, source, acc_first, acc_second)
    density("second", wall_items, 0, n_second)
    density("both", items, 0, n_both)
    density("first", items, cap, n_first - cap)
    first_rows(acc_first, turned, blocks)
    for c in range(4):
        own[c] = plane(turned, blocks, c)
    rows_out(acc_second, back_low, 0, faces)
    rows_out(acc_second, back_high, faces, faces)
    rows_out(acc_second, back_far, 2 * faces, others - 2 * faces)
    for c in range(3):
        push[c] = plane(acc_second, others, 4 + c)


def fetch(pairs, sems):
    copies = [pltpu.make_async_copy(a, b, sems.at[k]) for k, (a, b) in enumerate(pairs)]
    for copy in copies:
        copy.start()
    return copies


def fetch_source(faces, low, high, far, source, sems):
    return fetch(
        (
            (low, source.at[0 : faces * 8]),
            (high, source.at[faces * 8 : 2 * faces * 8]),
            (far, source.at[2 * faces * 8 :]),
        ),
        sems,
    )


def fluid_mask(blocks, table):
    return jnp.logical_and(plane(table, blocks, 6) > 0.0, plane(table, blocks, 7) < 0.5)


def own_density(
    blocks,
    faces,
    per_peer,
    send,
    table,
    self_sum,
    local_sum,
    far_sum,
    from_above,
    from_below,
    returned,
    density,
    slopes,
    total,
):
    total[pl.ds(0, blocks, stride=8), :] = self_sum[...] + local_sum[0] + far_sum[0]
    for c in range(1, 8):
        total[pl.ds(c, blocks, stride=8), :] = jnp.zeros((blocks, lanes), jnp.float32)
    for k in range(faces):
        at = 8 * (blocks - faces + k)
        total[at : at + 4, :] += from_above[4 * k : 4 * k + 4, :]
        total[8 * k : 8 * k + 4, :] += from_below[4 * k : 4 * k + 4, :]

    def give(t, carry):
        for k in range(per_peer):
            at = pl.multiple_of(send[0, k, t] * 8, 8)
            source = pl.multiple_of((t * per_peer + k) * 4, 4)
            total[pl.ds(at, 4), :] += returned[pl.ds(source, 4), :]
        return carry

    lax.fori_loop(0, send.shape[2], give, 0, unroll=2)
    density[...] = jnp.where(fluid_mask(blocks, table), kernel_norm * plane(total, blocks, 0), 0.0)
    for c in range(3):
        slopes[c] = plane(total, blocks, 1 + c)


def force_fields(source, density, number, pressed):
    mass = plane(source, number, 6)
    rho = jnp.where(mass > 0.0, density, 1.0)
    inverse = 1.0 / jnp.where(rho > 0.0, rho, 1.0)
    press = 10.0 * (rho - 1.0) * inverse * inverse
    pressed[...] = press * mass
    return inverse, press, mass * inverse


def force_body(source, pressed, kind, wide_fields, decoded):
    lane = lax.broadcasted_iota(jnp.int32, (8, lanes), 1)
    sub = lax.broadcasted_iota(jnp.int32, (8, lanes), 0)
    outs = []
    for k, (first, second, row) in enumerate(decoded):
        base = pl.multiple_of(second * 8, 8)
        rows = [wide(source[pl.ds(base + c, 1), :]) for c in range(6 if kind == "second" else 8)]
        if kind != "second":
            press = wide(pressed[pl.ds(second, 1), :])
        merged = []
        sums = None
        for g in range(groups):
            at = rows_item * k + 8 * g
            fields = [wide_fields[f, at : at + 8, :] for f in range(8 if kind == "first" else 9)]
            dx, dy, dz, square, u = close_u(fields, rows)
            u3 = (u * u) * u
            if kind != "first":
                u3 = u3 * fields[8]
            damp = (u3 * (square * (1.0 / (square + 0.25 * softening)))) * (
                fields[6] if kind == "second" else fields[6] * rows[7]
            )
            pull = u3 * (fields[7] if kind == "second" else fields[7] * rows[6] + press)
            pushed = [pull * d for d in (dx, dy, dz)]
            damped = [damp * (fields[3 + c] - rows[3 + c]) for c in range(3)]
            if kind == "second":
                values = damped + pushed
            else:
                values = [a - b for a, b in zip(pushed, damped)]
            if kind in ("local", "first"):
                merged.append(
                    merge_lanes([jnp.sum(v, axis=1, keepdims=True) for v in values], first, lane)
                )
            if kind != "first":
                sums = values if sums is None else [s + v for s, v in zip(sums, values)]
        outs.append((merged, merge_rows(sums, sub, range(1, 7)) if sums else None))
    return outs


def run_force(columns, spread, fields, source, pressed, acc_first, acc_second, kind, items, cap):
    run_items(
        columns,
        spread,
        fields,
        8 if kind == "first" else 9,
        items,
        0,
        items[cap - 1],
        functools.partial(force_body, source, pressed, kind),
        functools.partial(add_sums, acc_first, acc_second),
        kind != "self",
    )


def far_send_kernel(
    blocks,
    faces,
    per_peer,
    send,
    items,
    table,
    self_sum,
    local_sum,
    far_sum,
    from_above,
    from_below,
    returned,
    low,
    high,
    far,
    push,
    density,
    slopes,
    columns_out,
    own_source,
    pressed,
    out_low,
    out_high,
    out_far,
    stage,
    last,
    source,
    spread,
    wide_fields,
    acc_second,
    columns,
    sems,
):
    others = source.shape[0] // 8
    copies = fetch_source(faces, low, high, far, source, sems)
    own_density(
        blocks,
        faces,
        per_peer,
        send,
        table,
        self_sum,
        local_sum,
        far_sum,
        from_above,
        from_below,
        returned,
        density,
        slopes,
        own_source,
    )
    own_source[...] = table[...]
    inverse, press, scaled = force_fields(own_source, density[...], blocks, pressed)
    own_source[pl.ds(7, blocks, stride=8), :] = inverse
    last[...] = jnp.zeros(last.shape, jnp.float32)
    for p, piece in enumerate(split3(press)):
        last[pl.ds(p, blocks, stride=8), :] = piece
    make_columns(blocks, own_source, last, columns, stage)
    own_source[pl.ds(7, blocks, stride=8), :] = scaled
    columns_copy = pltpu.make_async_copy(columns, columns_out, sems.at[3])
    columns_copy.start()
    make_spread(spread, force_order)
    clear(acc_second, 4)
    for copy in copies:
        copy.wait()
    run_force(columns, spread, wide_fields, source, None, None, acc_second, "second", items, items.shape[0] // 2)
    for c in range(3):
        acc_second[pl.ds(4 + c, others, stride=8), :] = push[c] - plane(acc_second, others, 4 + c)
    acc_second[pl.ds(0, faces, stride=8), :] = density[0:faces, :]
    acc_second[pl.ds(8 * faces, faces, stride=8), :] = density[blocks - faces :, :]

    def pick(t, carry):
        for k in range(per_peer):
            at = 8 * (2 * faces + t * per_peer + k)
            acc_second[pl.ds(at, 1), :] = density[pl.ds(send[0, k, t], 1), :]
        return carry

    lax.fori_loop(0, send.shape[2], pick, 0, unroll=4)
    out_low[...] = acc_second[0 : 8 * faces, :]
    out_high[...] = acc_second[8 * faces : 16 * faces, :]
    out_far[...] = acc_second[16 * faces :, :]
    columns_copy.wait()


def own_force_kernel(
    blocks,
    self_items,
    both_items,
    columns_in,
    source,
    pressed,
    own,
    spread,
    wide_fields,
    acc_first,
    acc_second,
    turned,
    columns,
    sem,
):
    columns_copy = pltpu.make_async_copy(columns_in, columns, sem)
    columns_copy.start()
    make_spread(spread, force_order)
    clear(acc_first, 1)
    clear(acc_second, 4)
    columns_copy.wait()
    force = functools.partial(
        run_force, columns, spread, wide_fields, source, pressed, acc_first, acc_second
    )
    force("self", self_items, self_items.shape[0])
    force("local", both_items, both_items.shape[0] // 2)
    first_rows(acc_first, turned, blocks)
    for c in range(3):
        own[c] = plane(turned, blocks, c) - plane(acc_second, blocks, 1 + c)


def far_force_kernel(
    blocks,
    faces,
    per_peer,
    items,
    columns_in,
    low,
    high,
    far,
    from_below,
    from_above,
    returned,
    send,
    table,
    density,
    slopes,
    local_sum,
    far_sum,
    own_force,
    out,
    own,
    total,
    source,
    source_density,
    pressed,
    spread,
    wide_fields,
    acc_first,
    turned,
    columns,
    sems,
):
    others = source.shape[0] // 8
    copies = fetch_source(faces, low, high, far, source, sems)
    columns_copy = pltpu.make_async_copy(columns_in, columns, sems.at[3])
    columns_copy.start()
    source_density[0:faces, :] = plane(from_below, faces, 0)
    source_density[faces : 2 * faces, :] = plane(from_above, faces, 0)
    source_density[2 * faces :, :] = plane(returned, others - 2 * faces, 0)
    make_spread(spread, force_order)
    clear(acc_first, 1)
    for copy in copies:
        copy.wait()
    scaled = force_fields(source, source_density[...], others, pressed)[2]
    source[pl.ds(7, others, stride=8), :] = scaled
    columns_copy.wait()
    run_force(columns, spread, wide_fields, source, pressed, acc_first, None, "first", items, items.shape[0] // 2)
    first_rows(acc_first, turned, blocks)
    for c in range(3):
        own[c] = plane(turned, blocks, c)
    final_sum(
        blocks,
        faces,
        per_peer,
        send,
        table,
        density,
        slopes,
        local_sum,
        far_sum,
        own_force,
        own,
        from_above,
        from_below,
        returned,
        out,
        total,
    )


def final_sum(
    blocks,
    faces,
    per_peer,
    send,
    table,
    density,
    slopes,
    local_sum,
    far_sum,
    own_force,
    far_force,
    from_above,
    from_below,
    returned,
    out,
    total,
):
    total[...] = jnp.zeros(total.shape, jnp.float32)
    total[8 * (blocks - faces) :, :] += from_above[...]
    total[0 : 8 * faces, :] += from_below[...]

    def give(t, carry):
        for k in range(per_peer):
            at = pl.multiple_of(send[0, k, t] * 8, 8)
            source = pl.multiple_of((t * per_peer + k) * 8, 8)
            total[pl.ds(at, 8), :] += returned[pl.ds(source, 8), :]
        return carry

    lax.fori_loop(0, send.shape[2], give, 0, unroll=2)
    fluid = fluid_mask(blocks, table)
    mass = plane(table, blocks, 6)
    over_mass = 1.0 / jnp.where(mass > 0.0, mass, 1.0)
    over_rho = 1.0 / jnp.where(fluid, density[...], 1.0)
    press = jnp.where(fluid, 10.0 * (density[...] - 1.0) * over_rho * over_rho, 0.0)
    for c in range(3):
        force = own_force[c] * over_mass + far_force[c]
        force = force + local_sum[1 + c] + far_sum[1 + c]
        force = force + plane(total, blocks, 1 + c) * over_rho + plane(total, blocks, 4 + c)
        out[c] = jnp.where(fluid, kernel_norm * (force - press * slopes[c]), 0.0)


def f32(*shape):
    return jax.ShapeDtypeStruct(shape, jnp.float32)


def i32(*shape):
    return jax.ShapeDtypeStruct(shape, jnp.int32)


def to_above(shard):
    count = lax.axis_size("slab")
    return lax.ppermute(shard, "slab", [(i, i + 1) for i in range(count - 1)])


def to_below(shard):
    count = lax.axis_size("slab")
    return lax.ppermute(shard, "slab", [(i + 1, i) for i in range(count - 1)])


def swap_tiles(rows, tiles):
    parts = rows.reshape(tiles, rows.shape[0] // tiles, lanes)
    return lax.all_to_all(parts, "tile", split_axis=0, concat_axis=0, tiled=True).reshape(rows.shape)


def on_device(
    positions,
    velocities,
    masses,
    wall_areas,
    normals,
    wall_flags,
    counts,
    send_list,
    local_pairs,
    remote_pairs,
    remote_live,
):
    blocks = positions.shape[1]
    faces = blocks // 4
    tiles = lax.axis_size("tile")
    per_peer = send_list.shape[2]
    offered = send_list.shape[1] * per_peer
    send = jnp.swapaxes(send_list, 1, 2)
    others = 2 * faces + offered
    n_local = local_pairs.shape[0]
    n_remote = remote_pairs.shape[0]
    per = lanes // rows_item
    spare = 3 * batch * density_halves
    self_cap = per * blocks + spare
    own_cap = per * n_local + spare
    far_cap = per * n_remote + spare
    pair_cap = n_remote + 2 * pair_pad
    columns_shape = jax.ShapeDtypeStruct((blocks // 4 + 1, lanes, lanes), bf16)
    columns_scratch = vmem((blocks // 4 + 1, lanes, lanes), bf16)
    stage = vmem((blocks * 32, lanes), jnp.float32)

    def fields(number, halves):
        return [vmem((lanes + 4 * rows_item, 128 * number), bf16), vmem((halves, number, lanes, lanes), jnp.float32)]

    acc_first = vmem((blocks // 16 + 1, lanes, lanes), jnp.float32)
    turned = vmem((blocks * 8, lanes), jnp.float32)

    def tiles_of(number):
        return vmem((number * 8, lanes), jnp.float32)

    def cost(flops):
        return pl.CostEstimate(flops=flops, bytes_accessed=400_000, transcendentals=0)

    table, picked, head, tail = pl.pallas_call(
        functools.partial(pack_kernel, blocks, faces, per_peer),
        out_shape=(f32(blocks * 8, lanes), f32(offered * 8, lanes), f32(faces * 8, lanes), f32(faces * 8, lanes)),
        in_specs=[spec(smem)] + [spec(vmem)] * 7,
        out_specs=[spec(vmem)] * 4,
        compiler_params=params(grant_mib),
        name="pack",
    )(
        send,
        positions,
        velocities,
        masses,
        wall_areas,
        normals,
        wall_flags[None, :],
        counts[None, :],
    )
    low = to_above(tail)
    high = to_below(head)
    far = swap_tiles(picked, tiles)

    columns, self_sum, self_items, own_items, far_pairs = pl.pallas_call(
        functools.partial(self_density_kernel, blocks),
        out_shape=(
            columns_shape,
            f32(blocks, lanes),
            i32(self_cap),
            i32(2 * own_cap),
            i32(2 * pair_cap),
        ),
        in_specs=[spec(smem)] * 5 + [spec(vmem)],
        out_specs=[spec(pl.ANY), spec(vmem)] + [spec(smem)] * 3,
        scratch_shapes=[stage]
        + fields(8, density_halves)
        + [tiles_of(blocks), columns_scratch, pltpu.SemaphoreType.DMA],
        compiler_params=params(grant_mib),
        cost_estimate=cost(40_000_000),
        name="self_density",
    )(counts, wall_flags, remote_live, local_pairs.T, remote_pairs.T, table)

    far_sum, back_low, back_high, back_far, push, far_items = pl.pallas_call(
        functools.partial(far_density_kernel, blocks, faces),
        out_shape=(
            f32(4, blocks, lanes),
            f32(faces * 4, lanes),
            f32(faces * 4, lanes),
            f32(offered * 4, lanes),
            f32(3, others, lanes),
            i32(2 * far_cap),
        ),
        in_specs=[spec(smem)] + [spec(pl.ANY)] * 4,
        out_specs=[spec(vmem)] * 5 + [spec(smem)],
        scratch_shapes=fields(8, density_halves)
        + [acc_first, tiles_of(others), turned]
        + [
            tiles_of(others),
            vmem((others, lanes), jnp.float32),
            smem((others, lanes), jnp.float32),
            smem((far_cap,), jnp.int32),
            columns_scratch,
            pltpu.SemaphoreType.DMA,
            pltpu.SemaphoreType.DMA((4,)),
        ],
        compiler_params=params(grant_mib),
        cost_estimate=cost(100_000_000),
        name="far_density",
    )(far_pairs, columns, low, high, far)

    from_above = to_below(back_low)
    from_below = to_above(back_high)
    returned = swap_tiles(back_far, tiles)

    local_sum = pl.pallas_call(
        functools.partial(local_density_kernel, blocks),
        out_shape=f32(4, blocks, lanes),
        in_specs=[spec(smem), spec(vmem), spec(pl.ANY)],
        out_specs=spec(vmem),
        scratch_shapes=fields(8, density_halves)
        + [acc_first, tiles_of(blocks), turned, columns_scratch, pltpu.SemaphoreType.DMA],
        compiler_params=params(grant_mib),
        cost_estimate=cost(40_000_000),
        name="local_density",
    )(own_items, table, columns)

    density, slopes, force_columns, force_table, pressed, out_low, out_high, out_far = pl.pallas_call(
        functools.partial(far_send_kernel, blocks, faces, per_peer),
        out_shape=(
            f32(blocks, lanes),
            f32(3, blocks, lanes),
            columns_shape,
            f32(blocks * 8, lanes),
            f32(blocks, lanes),
            f32(faces * 8, lanes),
            f32(faces * 8, lanes),
            f32(offered * 8, lanes),
        ),
        in_specs=[spec(smem)] * 2 + [spec(vmem)] * 7 + [spec(pl.ANY)] * 3 + [spec(vmem)],
        out_specs=[spec(vmem)] * 2 + [spec(pl.ANY)] + [spec(vmem)] * 5,
        scratch_shapes=[stage, tiles_of(blocks), tiles_of(others)] + fields(10, force_halves) + [tiles_of(others), columns_scratch, pltpu.SemaphoreType.DMA((4,))],
        compiler_params=params(grant_mib),
        cost_estimate=cost(100_000_000),
        name="far_send",
    )(
        send,
        far_items,
        table,
        self_sum,
        local_sum,
        far_sum,
        from_above,
        from_below,
        returned,
        low,
        high,
        far,
        push,
    )

    force_above = to_below(out_low)
    force_below = to_above(out_high)
    force_far = swap_tiles(out_far, tiles)

    own_force = pl.pallas_call(
        functools.partial(own_force_kernel, blocks),
        out_shape=f32(3, blocks, lanes),
        in_specs=[spec(smem)] * 2 + [spec(pl.ANY)] + [spec(vmem)] * 2,
        out_specs=spec(vmem),
        scratch_shapes=fields(10, force_halves)
        + [acc_first, tiles_of(blocks), turned, columns_scratch, pltpu.SemaphoreType.DMA],
        compiler_params=params(grant_mib),
        cost_estimate=cost(80_000_000),
        name="own_force",
    )(self_items, own_items, force_columns, force_table, pressed)

    acceleration = pl.pallas_call(
        functools.partial(far_force_kernel, blocks, faces, per_peer),
        out_shape=f32(3, blocks, lanes),
        in_specs=[spec(smem)] + [spec(pl.ANY)] * 4 + [spec(vmem)] * 3 + [spec(smem)] + [spec(vmem)] * 6,
        out_specs=spec(vmem),
        scratch_shapes=[
            vmem((3, blocks, lanes), jnp.float32),
            tiles_of(blocks),
            tiles_of(others),
            vmem((others, lanes), jnp.float32),
            vmem((others, lanes), jnp.float32),
        ]
        + fields(10, force_halves)
        + [acc_first, turned, columns_scratch, pltpu.SemaphoreType.DMA((4,))],
        compiler_params=params(grant_mib),
        cost_estimate=cost(100_000_000),
        name="far_force",
    )(
        far_items,
        force_columns,
        low,
        high,
        far,
        force_below,
        force_above,
        force_far,
        send,
        table,
        density,
        slopes,
        local_sum,
        far_sum,
        own_force,
    )

    return (density, acceleration)


def solution(mesh):
    placed = (
        P(None, ("slab", "tile"), None),
        P(None, ("slab", "tile"), None),
        P(("slab", "tile"), None),
        P(("slab", "tile"), None),
        P(None, ("slab", "tile"), None),
        P(("slab", "tile")),
        P(("slab", "tile")),
        P(("slab", "tile"), None, None),
        P(("slab", "tile"), None),
        P(("slab", "tile"), None),
        P(("slab", "tile")),
    )
    return jax.shard_map(
        on_device,
        mesh=mesh,
        in_specs=placed,
        out_specs=(P(("slab", "tile"), None), P(None, ("slab", "tile"), None)),
        check_vma=False,
    )
```

```python
import functools
import math

import jax
import jax.numpy as jnp
from jax import lax
from jax.experimental import pallas as pl
from jax.experimental.pallas import tpu as pltpu
from jax.sharding import PartitionSpec as P

kernel_norm = 21.0 / (16.0 * math.pi)
softening = 0.01
tiny = 1e-30
lanes = 128
rows_item = 32
groups = rows_item // 8
batch = lanes // rows_item
density_halves = 4
force_halves = 4
pair_pad = 8
grant_mib = 64
density_order = (0, 1, 2, 6, 3, 4, 5)
force_order = (0, 1, 2, 3, 4, 5, 7, 8, 6)
bf16 = jnp.bfloat16
vmem = pltpu.VMEM
smem = pltpu.SMEM


def spec(space):
    return pl.BlockSpec(memory_space=space)


def params(mib):
    return pltpu.CompilerParams(vmem_limit_bytes=mib * 1024 * 1024)


def column_of(row):
    number = row.shape[1]
    same = lax.broadcasted_iota(jnp.int32, (number, number), 0) == lax.broadcasted_iota(
        jnp.int32, (number, number), 1
    )
    return jnp.sum(jnp.where(same, row, 0.0), axis=1, keepdims=True)


def pack_kernel(
    blocks, faces, per_peer, send, pos, vel, mass, area, normal, flags_row, counts_row, table, picked, head, tail
):
    slot = lax.broadcasted_iota(jnp.int32, (blocks, lanes), 1).astype(jnp.float32)
    alive = slot < column_of(counts_row[...].astype(jnp.float32))
    wall_value = column_of(flags_row[...].astype(jnp.float32)) + jnp.zeros((blocks, lanes), jnp.float32)
    wall = wall_value > 0.5
    nx, ny, nz = normal[0], normal[1], normal[2]
    length = jnp.sqrt(nx * nx + ny * ny + nz * nz)
    weight = jnp.where(alive, jnp.where(wall, area[...], mass[...]), 0.0)
    wall_scale = weight / length
    parts = (nx, ny, nz)
    for c in range(3):
        table[pl.ds(c, blocks, stride=8), :] = 0.5 * pos[c]
        table[pl.ds(3 + c, blocks, stride=8), :] = jnp.where(wall, wall_scale * parts[c], vel[c])
    table[pl.ds(6, blocks, stride=8), :] = weight
    table[pl.ds(7, blocks, stride=8), :] = wall_value
    head[...] = table[0 : faces * 8, :]
    tail[...] = table[(blocks - faces) * 8 : blocks * 8, :]

    def pick(t, carry):
        for k in range(per_peer):
            source = pl.multiple_of(send[0, k, t] * 8, 8)
            at = pl.multiple_of((t * per_peer + k) * 8, 8)
            picked[pl.ds(at, 8), :] = table[pl.ds(source, 8), :]
        return carry

    lax.fori_loop(0, picked.shape[0] // (8 * per_peer), pick, 0, unroll=2)


def rounded(x):
    return x.astype(bf16).astype(jnp.float32)


def split3(x):
    high = rounded(x)
    rest = x - high
    middle = rounded(rest)
    return high, middle, rest - middle


def make_spread(spread, order):
    shape = (lanes, spread.shape[1])
    k = lax.broadcasted_iota(jnp.int32, shape, 0) & 31
    tile = lax.broadcasted_iota(jnp.int32, shape, 1) >> 7
    want = jnp.full(shape, -1, jnp.int32)
    for t, field in enumerate(order):
        want = jnp.where(tile == t, field, want)
    hit = jnp.logical_and(k < 24, (k & 7) == want)
    hit = jnp.logical_or(hit, jnp.logical_and(jnp.logical_and(k >= 24, k < 27), want == 8))
    spread[0:lanes, :] = jnp.where(hit, 1.0, 0.0).astype(bf16)
    lane = lax.broadcasted_iota(jnp.int32, (rows_item, lanes), 1) >> 5
    for j in range(4):
        at = lanes + rows_item * j
        spread[at : at + rows_item, 0:lanes] = jnp.where(lane == j, 1.0, 0.0).astype(bf16)


def make_columns(blocks, table, last, columns, stage):
    for b in range(blocks):
        for p, piece in enumerate(split3(table[8 * b : 8 * b + 8, :])):
            stage[32 * b + 8 * p : 32 * b + 8 * p + 8, :] = piece
        if last is None:
            stage[32 * b + 24 : 32 * b + 32, :] = jnp.zeros((8, lanes), jnp.float32)
        else:
            stage[32 * b + 24 : 32 * b + 32, :] = last[8 * b : 8 * b + 8, :]

    def some(g, carry):
        turned = stage[pl.ds(pl.multiple_of(g * lanes, lanes), lanes), :].T
        columns[g] = turned.astype(bf16)
        return carry

    lax.fori_loop(0, blocks // 4, some, 0, unroll=2)
    columns[blocks // 4] = jnp.zeros((lanes, lanes), bf16)


def put_items(items, at, code):
    for k in range(lanes // rows_item):
        items[at + k] = code | (k << 16)


def close_items(items, count, blocks):
    for k in range(2 * batch * density_halves):
        items[count + k] = jnp.int32(blocks)


def chunks(count):
    return (count + (rows_item - 1)) >> 5


def decode(code):
    first = code & 255
    second = (code >> 8) & 255
    row = pl.multiple_of((code >> 16) * rows_item, rows_item)
    return first, second, row


def wide(row):
    return jnp.broadcast_to(row, (8, lanes))


def spread_fields(columns, spread, wide_fields, tiles, decoded):
    parts = []
    for first, second, row in decoded:
        mask = spread[pl.ds(pl.multiple_of(lanes + (first & 3) * rows_item, rows_item), rows_item), 0:lanes]
        parts.append(columns[first >> 2, pl.ds(row, rows_item), :] * mask)
    left = jnp.concatenate(parts, axis=0)
    for t in range((tiles + 1) // 2):
        both = jnp.dot(left, spread[0:lanes, 256 * t : 256 * t + 256], preferred_element_type=jnp.float32)
        wide_fields[2 * t] = both[:, 0:lanes]
        wide_fields[2 * t + 1] = both[:, lanes : 2 * lanes]


def close_u(fields, rows):
    dx = fields[0] - rows[0]
    dy = fields[1] - rows[1]
    dz = fields[2] - rows[2]
    square = dx * dx + dy * dy + dz * dz
    safe = jnp.maximum(square, tiny)
    q = safe * lax.rsqrt(safe)
    u = jnp.maximum(1.0 - q, 0.0)
    return dx, dy, dz, square, u


def kernel_shape(u):
    u2 = u * u
    return (u2 * u2) * (5.0 - 4.0 * u)


def run_items(columns, spread, wide_fields, tiles, items, start, count, body, finish, alternate=False):
    halves = wide_fields.shape[0]
    size = batch * halves

    def decoded_of(it, h):
        return [decode(items[start + (it * halves + h) * batch + k]) for k in range(batch)]

    def prepare(it, hs):
        for h in hs:
            spread_fields(columns, spread, wide_fields.at[h], tiles, decoded_of(it, h))

    def work(it, hs):
        done = []
        for h in hs:
            decoded = decoded_of(it, h)
            done.append((decoded, body(wide_fields.at[h], decoded)))
        return done

    group = halves // 2 if alternate else halves
    front, rear = range(group), range(group, halves)

    def step(it, carry):
        prepare(it, rear)
        done = work(it, front)
        prepare(it + 1, front)
        done += work(it, rear)
        for decoded, outs in done:
            finish(decoded, outs)
        return carry

    prepare(0, front)
    lax.fori_loop(0, (count + size - 1) >> (size.bit_length() - 1), step, 0)


def merge_lanes(values, first, lane):
    base = (first & 15) * 8
    total = jnp.zeros((8, lanes), jnp.float32)
    for c, value in enumerate(values):
        total = jnp.where(lane == base + c, value, total)
    return total


def merge_rows(values, sub, places):
    total = jnp.zeros((8, lanes), jnp.float32)
    for c, value in zip(places, values):
        total = jnp.where(sub == c, jnp.sum(value, axis=0, keepdims=True), total)
    return total


def add_sums(acc_first, acc_second, decoded, outs):
    for (first, second, row), (merged, tile) in zip(decoded, outs):
        if merged:
            slab = first >> 4
            for g in range(groups):
                acc_first[slab, pl.ds(row + 8 * g, 8), :] += merged[g]
        if tile is not None:
            at = pl.multiple_of(second * 8, 8)
            acc_second[pl.ds(at, 8), :] += tile


def density_body(source, kind, wide_fields, decoded):
    lane = lax.broadcasted_iota(jnp.int32, (8, lanes), 1)
    sub = lax.broadcasted_iota(jnp.int32, (8, lanes), 0)
    places = {"self": (0,), "local": (0,), "both": (0, 1, 2, 3), "second": (0, 4, 5, 6)}
    outs = []
    for k, (first, second, row) in enumerate(decoded):
        base = pl.multiple_of(second * 8, 8)
        rows = [wide(source[pl.ds(base + c, 1), :]) for c in range(3)]
        given = []
        if kind in ("both", "local", "first"):
            given = [wide(source[pl.ds(base + 6, 1), :])]
            if kind == "first":
                given += [wide(source[pl.ds(base + 3 + c, 1), :]) for c in range(3)]
        merged = []
        sums = None
        for g in range(groups):
            at = rows_item * k + 8 * g
            number = {"first": 3, "second": 7}.get(kind, 4)
            fields = [wide_fields[f, at : at + 8, :] for f in range(number)]
            dx, dy, dz, square, u = close_u(fields, rows)
            w = kernel_shape(u)
            if given:
                values = [jnp.sum(w * other, axis=1, keepdims=True) for other in given]
                merged.append(merge_lanes(values, first, lane))
            if kind != "first":
                back = [w * field for field in fields[3:]]
                if kind == "both":
                    slope = ((u * u) * u) * fields[3]
                    back += [slope * d for d in (dx, dy, dz)]
                sums = back if sums is None else [s + b for s, b in zip(sums, back)]
        outs.append((merged, merge_rows(sums, sub, places[kind]) if sums else None))
    return outs


def clear(ref, pieces):
    size = ref.shape[0] // pieces

    def some(k, carry):
        at = pl.multiple_of(k * size, size)
        ref[pl.ds(at, size)] = jnp.zeros((size,) + tuple(ref.shape[1:]), jnp.float32)
        return carry

    lax.fori_loop(0, pieces, some, 0)


def plane(ref, number, c):
    return ref[pl.ds(c, number, stride=8), :]


def first_rows(acc_first, turned, blocks):
    for s in range(blocks // 16):
        turned[s * lanes : (s + 1) * lanes, :] = acc_first[s].T


def run_density(columns, spread, fields, source, acc_first, acc_second, kind, items, start, count):
    run_items(
        columns,
        spread,
        fields,
        7 if kind == "second" else 4,
        items,
        start,
        count,
        functools.partial(density_body, source, kind),
        functools.partial(add_sums, acc_first, acc_second),
    )


def self_density_kernel(
    blocks,
    counts,
    flags,
    live,
    local_pairs,
    remote_pairs,
    table,
    columns_out,
    own,
    items,
    local_items,
    far_pairs,
    stage,
    spread,
    wide_fields,
    acc_second,
    columns,
    sem,
):
    make_columns(blocks, table, None, columns, stage)
    columns_copy = pltpu.make_async_copy(columns, columns_out, sem)
    columns_copy.start()
    make_spread(spread, density_order)
    clear(acc_second, 4)
    zero = jnp.int32(0)

    def self_step(b, n):
        put_items(items, n, b | (b << 8))
        return n + chunks(counts[b]) * (1 - flags[b])

    count = lax.fori_loop(0, blocks, self_step, zero, unroll=8)
    close_items(items, count, blocks)
    items[items.shape[0] - 1] = count
    run_density(columns, spread, wide_fields, table, None, acc_second, "self", items, 0, count)
    own[...] = plane(acc_second, blocks, 0)
    cap = local_items.shape[0] // 2

    def local_step(p, state):
        n_both, n_wall = state
        a = local_pairs[0, p]
        b = local_pairs[1, p]
        wall_b = flags[b]
        kinds = flags[a] + wall_b
        swap = jnp.where(kinds == 1, wall_b, (counts[b] < counts[a]).astype(jnp.int32)) > 0
        first = jnp.where(swap, b, a)
        second = jnp.where(swap, a, b)
        number = chunks(counts[first])
        put_items(local_items, jnp.where(kinds == 0, n_both, n_wall), first | (second << 8))
        return n_both + jnp.where(kinds == 0, number, 0), n_wall + jnp.where(kinds == 1, number, 0)

    n_both, n_wall = lax.fori_loop(0, local_pairs.shape[1], local_step, (zero, zero + cap), unroll=8)
    close_items(local_items, n_both, blocks)
    close_items(local_items, n_wall, blocks)
    local_items[cap - 1] = n_both
    local_items[2 * cap - 1] = n_wall - cap
    half = far_pairs.shape[0] // 2

    def remote_step(p, state):
        n_fluid, n_wall = state
        a = remote_pairs[0, p]
        j = remote_pairs[1, p]
        b = jnp.where(j < blocks, j, j - blocks)
        wall = flags[a]
        code = a | (b << 8) | (chunks(counts[a]) << 16)
        far_pairs[jnp.where(wall > 0, n_wall, n_fluid)] = code
        return n_fluid + 1 - wall, n_wall + wall

    n_fluid, n_wall = lax.fori_loop(0, live[0], remote_step, (zero, zero + half))
    far_pairs[half - 1] = n_fluid
    far_pairs[2 * half - 1] = n_wall - half
    for k in range(pair_pad):
        far_pairs[n_fluid + k] = zero
        far_pairs[n_wall + k] = zero
    columns_copy.wait()


def local_density_kernel(
    blocks,
    items,
    table,
    columns_in,
    own,
    spread,
    wide_fields,
    acc_first,
    acc_second,
    turned,
    columns,
    sem,
):
    columns_copy = pltpu.make_async_copy(columns_in, columns, sem)
    columns_copy.start()
    make_spread(spread, density_order)
    clear(acc_first, 1)
    clear(acc_second, 4)
    density = functools.partial(run_density, columns, spread, wide_fields, table, acc_first, acc_second)
    columns_copy.wait()
    cap = items.shape[0] // 2
    density("local", items, 0, items[cap - 1])
    density("second", items, cap, items[2 * cap - 1])
    first_rows(acc_first, turned, blocks)
    own[0] = plane(turned, blocks, 0) + plane(acc_second, blocks, 0)
    for c in range(1, 4):
        own[c] = plane(acc_second, blocks, 3 + c)


def rows_out(tiles, out, start, number):
    for k in range(number):
        out[4 * k : 4 * k + 4, :] = tiles[8 * (start + k) : 8 * (start + k) + 4, :]


def far_density_kernel(
    blocks,
    faces,
    far_pairs,
    columns_in,
    low,
    high,
    far,
    own,
    back_low,
    back_high,
    back_far,
    push,
    items,
    spread,
    wide_fields,
    acc_first,
    acc_second,
    turned,
    source,
    wall_rows,
    wall_flag,
    wall_items,
    columns,
    sem,
    sems,
):
    others = source.shape[0] // 8
    copies = fetch_source(faces, low, high, far, source, sems)
    columns_copy = pltpu.make_async_copy(columns_in, columns, sems.at[3])
    columns_copy.start()
    make_spread(spread, density_order)
    for copy in copies:
        copy.wait()
    wall_rows[...] = plane(source, others, 7)
    flag_copy = pltpu.make_async_copy(wall_rows, wall_flag, sem)
    flag_copy.start()
    clear(acc_first, 1)
    clear(acc_second, 4)
    flag_copy.wait()
    zero = jnp.int32(0)
    half = far_pairs.shape[0] // 2
    cap = items.shape[0] // 2

    def fluid_second(code):
        return wall_flag[(code >> 8) & 255, 0] < 0.5

    def wall_step(q, n):
        for k in range(pair_pad):
            code = far_pairs[half + q * pair_pad + k]
            put_items(wall_items, n, code & 65535)
            n = n + jnp.where(fluid_second(code), code >> 16, 0)
        return n

    def fluid_step(q, state):
        n_both, n_first = state
        for k in range(pair_pad):
            code = far_pairs[q * pair_pad + k]
            number = code >> 16
            fluid = fluid_second(code)
            put_items(items, jnp.where(fluid, n_both, n_first), code & 65535)
            n_both = n_both + jnp.where(fluid, number, 0)
            n_first = n_first + jnp.where(fluid, 0, number)
        return n_both, n_first

    def passes(pairs):
        return (pairs + (pair_pad - 1)) >> 3

    n_both, n_first = lax.fori_loop(0, passes(far_pairs[half - 1]), fluid_step, (zero, zero + cap))
    close_items(items, n_both, blocks)
    close_items(items, n_first, blocks)
    items[cap - 1] = n_both
    n_second = lax.fori_loop(0, passes(far_pairs[2 * half - 1]), wall_step, zero)
    close_items(wall_items, n_second, blocks)
    columns_copy.wait()
    density = functools.partial(run_density, columns, spread, wide_fields, source, acc_first, acc_second)
    density("second", wall_items, 0, n_second)
    density("both", items, 0, n_both)
    density("first", items, cap, n_first - cap)
    first_rows(acc_first, turned, blocks)
    for c in range(4):
        own[c] = plane(turned, blocks, c)
    rows_out(acc_second, back_low, 0, faces)
    rows_out(acc_second, back_high, faces, faces)
    rows_out(acc_second, back_far, 2 * faces, others - 2 * faces)
    for c in range(3):
        push[c] = plane(acc_second, others, 4 + c)


def fetch(pairs, sems):
    copies = [pltpu.make_async_copy(a, b, sems.at[k]) for k, (a, b) in enumerate(pairs)]
    for copy in copies:
        copy.start()
    return copies


def fetch_source(faces, low, high, far, source, sems):
    return fetch(
        (
            (low, source.at[0 : faces * 8]),
            (high, source.at[faces * 8 : 2 * faces * 8]),
            (far, source.at[2 * faces * 8 :]),
        ),
        sems,
    )


def fluid_mask(blocks, table):
    return jnp.logical_and(plane(table, blocks, 6) > 0.0, plane(table, blocks, 7) < 0.5)


def own_density(
    blocks,
    faces,
    per_peer,
    send,
    table,
    self_sum,
    local_sum,
    far_sum,
    from_above,
    from_below,
    returned,
    density,
    slopes,
    total,
):
    total[pl.ds(0, blocks, stride=8), :] = self_sum[...] + local_sum[0] + far_sum[0]
    for c in range(1, 8):
        total[pl.ds(c, blocks, stride=8), :] = jnp.zeros((blocks, lanes), jnp.float32)
    for k in range(faces):
        at = 8 * (blocks - faces + k)
        total[at : at + 4, :] += from_above[4 * k : 4 * k + 4, :]
        total[8 * k : 8 * k + 4, :] += from_below[4 * k : 4 * k + 4, :]

    def give(t, carry):
        for k in range(per_peer):
            at = pl.multiple_of(send[0, k, t] * 8, 8)
            source = pl.multiple_of((t * per_peer + k) * 4, 4)
            total[pl.ds(at, 4), :] += returned[pl.ds(source, 4), :]
        return carry

    lax.fori_loop(0, send.shape[2], give, 0, unroll=2)
    density[...] = jnp.where(fluid_mask(blocks, table), kernel_norm * plane(total, blocks, 0), 0.0)
    for c in range(3):
        slopes[c] = plane(total, blocks, 1 + c)


def force_fields(source, density, number, pressed):
    mass = plane(source, number, 6)
    rho = jnp.where(mass > 0.0, density, 1.0)
    inverse = 1.0 / jnp.where(rho > 0.0, rho, 1.0)
    press = 10.0 * (rho - 1.0) * inverse * inverse
    pressed[...] = press * mass
    return inverse, press, mass * inverse


def force_body(source, pressed, kind, wide_fields, decoded):
    lane = lax.broadcasted_iota(jnp.int32, (8, lanes), 1)
    sub = lax.broadcasted_iota(jnp.int32, (8, lanes), 0)
    outs = []
    for k, (first, second, row) in enumerate(decoded):
        base = pl.multiple_of(second * 8, 8)
        rows = [wide(source[pl.ds(base + c, 1), :]) for c in range(6 if kind == "second" else 8)]
        if kind != "second":
            press = wide(pressed[pl.ds(second, 1), :])
        merged = []
        sums = None
        for g in range(groups):
            at = rows_item * k + 8 * g
            fields = [wide_fields[f, at : at + 8, :] for f in range(8 if kind == "first" else 9)]
            dx, dy, dz, square, u = close_u(fields, rows)
            u3 = (u * u) * u
            if kind != "first":
                u3 = u3 * fields[8]
            damp = (u3 * (square * (1.0 / (square + 0.25 * softening)))) * (
                fields[6] if kind == "second" else fields[6] * rows[7]
            )
            pull = u3 * (fields[7] if kind == "second" else fields[7] * rows[6] + press)
            pushed = [pull * d for d in (dx, dy, dz)]
            damped = [damp * (fields[3 + c] - rows[3 + c]) for c in range(3)]
            if kind == "second":
                values = damped + pushed
            else:
                values = [a - b for a, b in zip(pushed, damped)]
            if kind in ("local", "first"):
                merged.append(
                    merge_lanes([jnp.sum(v, axis=1, keepdims=True) for v in values], first, lane)
                )
            if kind != "first":
                sums = values if sums is None else [s + v for s, v in zip(sums, values)]
        outs.append((merged, merge_rows(sums, sub, range(1, 7)) if sums else None))
    return outs


def run_force(columns, spread, fields, source, pressed, acc_first, acc_second, kind, items, cap):
    run_items(
        columns,
        spread,
        fields,
        8 if kind == "first" else 9,
        items,
        0,
        items[cap - 1],
        functools.partial(force_body, source, pressed, kind),
        functools.partial(add_sums, acc_first, acc_second),
        kind != "self",
    )


def far_send_kernel(
    blocks,
    faces,
    per_peer,
    send,
    items,
    table,
    self_sum,
    local_sum,
    far_sum,
    from_above,
    from_below,
    returned,
    low,
    high,
    far,
    push_in,
    density,
    slopes,
    columns_out,
    own_source,
    pressed,
    out_low,
    out_high,
    out_far,
    stage,
    last,
    source,
    spread,
    wide_fields,
    acc_second,
    columns,
    sems,
    push,
    push_sem,
):
    others = source.shape[0] // 8
    copies = fetch_source(faces, low, high, far, source, sems)
    push_copy = pltpu.make_async_copy(push_in, push, push_sem)
    push_copy.start()
    own_density(
        blocks,
        faces,
        per_peer,
        send,
        table,
        self_sum,
        local_sum,
        far_sum,
        from_above,
        from_below,
        returned,
        density,
        slopes,
        own_source,
    )
    own_source[...] = table[...]
    inverse, press, scaled = force_fields(own_source, density[...], blocks, pressed)
    own_source[pl.ds(7, blocks, stride=8), :] = inverse
    last[...] = jnp.zeros(last.shape, jnp.float32)
    for p, piece in enumerate(split3(press)):
        last[pl.ds(p, blocks, stride=8), :] = piece
    make_columns(blocks, own_source, last, columns, stage)
    own_source[pl.ds(7, blocks, stride=8), :] = scaled
    columns_copy = pltpu.make_async_copy(columns, columns_out, sems.at[3])
    columns_copy.start()
    make_spread(spread, force_order)
    clear(acc_second, 4)
    for copy in copies:
        copy.wait()
    run_force(columns, spread, wide_fields, source, None, None, acc_second, "second", items, items.shape[0] // 2)
    push_copy.wait()
    for c in range(3):
        acc_second[pl.ds(4 + c, others, stride=8), :] = push[c] - plane(acc_second, others, 4 + c)
    acc_second[pl.ds(0, faces, stride=8), :] = density[0:faces, :]
    acc_second[pl.ds(8 * faces, faces, stride=8), :] = density[blocks - faces :, :]

    def pick(t, carry):
        for k in range(per_peer):
            at = 8 * (2 * faces + t * per_peer + k)
            acc_second[pl.ds(at, 1), :] = density[pl.ds(send[0, k, t], 1), :]
        return carry

    lax.fori_loop(0, send.shape[2], pick, 0, unroll=4)
    out_low[...] = acc_second[0 : 8 * faces, :]
    out_high[...] = acc_second[8 * faces : 16 * faces, :]
    out_far[...] = acc_second[16 * faces :, :]
    columns_copy.wait()


def own_force_kernel(
    blocks,
    self_items,
    both_items,
    columns_in,
    source,
    pressed,
    own,
    spread,
    wide_fields,
    acc_first,
    acc_second,
    turned,
    columns,
    sem,
):
    columns_copy = pltpu.make_async_copy(columns_in, columns, sem)
    columns_copy.start()
    make_spread(spread, force_order)
    clear(acc_first, 1)
    clear(acc_second, 4)
    columns_copy.wait()
    force = functools.partial(
        run_force, columns, spread, wide_fields, source, pressed, acc_first, acc_second
    )
    force("self", self_items, self_items.shape[0])
    force("local", both_items, both_items.shape[0] // 2)
    first_rows(acc_first, turned, blocks)
    for c in range(3):
        own[c] = plane(turned, blocks, c) - plane(acc_second, blocks, 1 + c)


def far_force_kernel(
    blocks,
    faces,
    per_peer,
    items,
    columns_in,
    low,
    high,
    far,
    from_below,
    from_above,
    returned,
    send,
    table_in,
    density_in,
    slopes_in,
    local_sum_in,
    far_sum_in,
    own_force_in,
    out,
    own,
    total,
    source,
    source_density,
    pressed,
    spread,
    wide_fields,
    acc_first,
    turned,
    columns,
    sems,
    table,
    density,
    slopes,
    local_sum,
    far_sum,
    own_force,
    late_sems,
):
    others = source.shape[0] // 8
    copies = fetch_source(faces, low, high, far, source, sems)
    columns_copy = pltpu.make_async_copy(columns_in, columns, sems.at[3])
    columns_copy.start()
    late = fetch(
        (
            (table_in, table),
            (density_in, density),
            (slopes_in, slopes),
            (local_sum_in, local_sum),
            (far_sum_in, far_sum),
            (own_force_in, own_force),
        ),
        late_sems,
    )
    source_density[0:faces, :] = plane(from_below, faces, 0)
    source_density[faces : 2 * faces, :] = plane(from_above, faces, 0)
    source_density[2 * faces :, :] = plane(returned, others - 2 * faces, 0)
    make_spread(spread, force_order)
    clear(acc_first, 1)
    for copy in copies:
        copy.wait()
    scaled = force_fields(source, source_density[...], others, pressed)[2]
    source[pl.ds(7, others, stride=8), :] = scaled
    columns_copy.wait()
    run_force(columns, spread, wide_fields, source, pressed, acc_first, None, "first", items, items.shape[0] // 2)
    first_rows(acc_first, turned, blocks)
    for c in range(3):
        own[c] = plane(turned, blocks, c)
    for copy in late:
        copy.wait()
    final_sum(
        blocks,
        faces,
        per_peer,
        send,
        table,
        density,
        slopes,
        local_sum,
        far_sum,
        own_force,
        own,
        from_above,
        from_below,
        returned,
        out,
        total,
    )


def final_sum(
    blocks,
    faces,
    per_peer,
    send,
    table,
    density,
    slopes,
    local_sum,
    far_sum,
    own_force,
    far_force,
    from_above,
    from_below,
    returned,
    out,
    total,
):
    total[...] = jnp.zeros(total.shape, jnp.float32)
    total[8 * (blocks - faces) :, :] += from_above[...]
    total[0 : 8 * faces, :] += from_below[...]

    def give(t, carry):
        for k in range(per_peer):
            at = pl.multiple_of(send[0, k, t] * 8, 8)
            source = pl.multiple_of((t * per_peer + k) * 8, 8)
            total[pl.ds(at, 8), :] += returned[pl.ds(source, 8), :]
        return carry

    lax.fori_loop(0, send.shape[2], give, 0, unroll=2)
    fluid = fluid_mask(blocks, table)
    mass = plane(table, blocks, 6)
    over_mass = 1.0 / jnp.where(mass > 0.0, mass, 1.0)
    over_rho = 1.0 / jnp.where(fluid, density[...], 1.0)
    press = jnp.where(fluid, 10.0 * (density[...] - 1.0) * over_rho * over_rho, 0.0)
    for c in range(3):
        force = own_force[c] * over_mass + far_force[c]
        force = force + local_sum[1 + c] + far_sum[1 + c]
        force = force + plane(total, blocks, 1 + c) * over_rho + plane(total, blocks, 4 + c)
        out[c] = jnp.where(fluid, kernel_norm * (force - press * slopes[c]), 0.0)


def f32(*shape):
    return jax.ShapeDtypeStruct(shape, jnp.float32)


def i32(*shape):
    return jax.ShapeDtypeStruct(shape, jnp.int32)


def to_above(shard):
    count = lax.axis_size("slab")
    return lax.ppermute(shard, "slab", [(i, i + 1) for i in range(count - 1)])


def to_below(shard):
    count = lax.axis_size("slab")
    return lax.ppermute(shard, "slab", [(i + 1, i) for i in range(count - 1)])


def swap_tiles(rows, tiles):
    parts = rows.reshape(tiles, rows.shape[0] // tiles, lanes)
    return lax.all_to_all(parts, "tile", split_axis=0, concat_axis=0, tiled=True).reshape(rows.shape)


def on_device(
    positions,
    velocities,
    masses,
    wall_areas,
    normals,
    wall_flags,
    counts,
    send_list,
    local_pairs,
    remote_pairs,
    remote_live,
):
    blocks = positions.shape[1]
    faces = blocks // 4
    tiles = lax.axis_size("tile")
    per_peer = send_list.shape[2]
    offered = send_list.shape[1] * per_peer
    send = jnp.swapaxes(send_list, 1, 2)
    others = 2 * faces + offered
    n_local = local_pairs.shape[0]
    n_remote = remote_pairs.shape[0]
    per = lanes // rows_item
    spare = 3 * batch * density_halves
    self_cap = per * blocks + spare
    own_cap = per * n_local + spare
    far_cap = per * n_remote + spare
    pair_cap = n_remote + 2 * pair_pad
    columns_shape = jax.ShapeDtypeStruct((blocks // 4 + 1, lanes, lanes), bf16)
    columns_scratch = vmem((blocks // 4 + 1, lanes, lanes), bf16)
    stage = vmem((blocks * 32, lanes), jnp.float32)

    def fields(number, halves):
        return [vmem((lanes + 4 * rows_item, 128 * number), bf16), vmem((halves, number, lanes, lanes), jnp.float32)]

    acc_first = vmem((blocks // 16 + 1, lanes, lanes), jnp.float32)
    turned = vmem((blocks * 8, lanes), jnp.float32)

    def tiles_of(number):
        return vmem((number * 8, lanes), jnp.float32)

    def cost(flops):
        return pl.CostEstimate(flops=flops, bytes_accessed=400_000, transcendentals=0)

    table, picked, head, tail = pl.pallas_call(
        functools.partial(pack_kernel, blocks, faces, per_peer),
        out_shape=(f32(blocks * 8, lanes), f32(offered * 8, lanes), f32(faces * 8, lanes), f32(faces * 8, lanes)),
        in_specs=[spec(smem)] + [spec(vmem)] * 7,
        out_specs=[spec(vmem)] * 4,
        compiler_params=params(grant_mib),
        name="pack",
    )(
        send,
        positions,
        velocities,
        masses,
        wall_areas,
        normals,
        wall_flags[None, :],
        counts[None, :],
    )
    low = to_above(tail)
    high = to_below(head)
    far = swap_tiles(picked, tiles)

    columns, self_sum, self_items, own_items, far_pairs = pl.pallas_call(
        functools.partial(self_density_kernel, blocks),
        out_shape=(
            columns_shape,
            f32(blocks, lanes),
            i32(self_cap),
            i32(2 * own_cap),
            i32(2 * pair_cap),
        ),
        in_specs=[spec(smem)] * 5 + [spec(vmem)],
        out_specs=[spec(pl.ANY), spec(vmem)] + [spec(smem)] * 3,
        scratch_shapes=[stage]
        + fields(8, density_halves)
        + [tiles_of(blocks), columns_scratch, pltpu.SemaphoreType.DMA],
        compiler_params=params(grant_mib),
        cost_estimate=cost(40_000_000),
        name="self_density",
    )(counts, wall_flags, remote_live, local_pairs.T, remote_pairs.T, table)

    far_sum, back_low, back_high, back_far, push, far_items = pl.pallas_call(
        functools.partial(far_density_kernel, blocks, faces),
        out_shape=(
            f32(4, blocks, lanes),
            f32(faces * 4, lanes),
            f32(faces * 4, lanes),
            f32(offered * 4, lanes),
            f32(3, others, lanes),
            i32(2 * far_cap),
        ),
        in_specs=[spec(smem)] + [spec(pl.ANY)] * 4,
        out_specs=[spec(vmem)] * 5 + [spec(smem)],
        scratch_shapes=fields(8, density_halves)
        + [acc_first, tiles_of(others), turned]
        + [
            tiles_of(others),
            vmem((others, lanes), jnp.float32),
            smem((others, lanes), jnp.float32),
            smem((far_cap,), jnp.int32),
            columns_scratch,
            pltpu.SemaphoreType.DMA,
            pltpu.SemaphoreType.DMA((4,)),
        ],
        compiler_params=params(grant_mib),
        cost_estimate=cost(100_000_000),
        name="far_density",
    )(far_pairs, columns, low, high, far)

    from_above = to_below(back_low)
    from_below = to_above(back_high)
    returned = swap_tiles(back_far, tiles)

    local_sum = pl.pallas_call(
        functools.partial(local_density_kernel, blocks),
        out_shape=f32(4, blocks, lanes),
        in_specs=[spec(smem), spec(vmem), spec(pl.ANY)],
        out_specs=spec(vmem),
        scratch_shapes=fields(8, density_halves)
        + [acc_first, tiles_of(blocks), turned, columns_scratch, pltpu.SemaphoreType.DMA],
        compiler_params=params(grant_mib),
        cost_estimate=cost(40_000_000),
        name="local_density",
    )(own_items, table, columns)

    density, slopes, force_columns, force_table, pressed, out_low, out_high, out_far = pl.pallas_call(
        functools.partial(far_send_kernel, blocks, faces, per_peer),
        out_shape=(
            f32(blocks, lanes),
            f32(3, blocks, lanes),
            columns_shape,
            f32(blocks * 8, lanes),
            f32(blocks, lanes),
            f32(faces * 8, lanes),
            f32(faces * 8, lanes),
            f32(offered * 8, lanes),
        ),
        in_specs=[spec(smem)] * 2 + [spec(vmem)] * 7 + [spec(pl.ANY)] * 4,
        out_specs=[spec(vmem)] * 2 + [spec(pl.ANY)] + [spec(vmem)] * 5,
        scratch_shapes=[stage, tiles_of(blocks), tiles_of(others)] + fields(10, force_halves) + [tiles_of(others), columns_scratch, pltpu.SemaphoreType.DMA((4,))]
        + [vmem((3, others, lanes), jnp.float32), pltpu.SemaphoreType.DMA],
        compiler_params=params(grant_mib),
        cost_estimate=cost(100_000_000),
        name="far_send",
    )(
        send,
        far_items,
        table,
        self_sum,
        local_sum,
        far_sum,
        from_above,
        from_below,
        returned,
        low,
        high,
        far,
        push,
    )

    force_above = to_below(out_low)
    force_below = to_above(out_high)
    force_far = swap_tiles(out_far, tiles)

    own_force = pl.pallas_call(
        functools.partial(own_force_kernel, blocks),
        out_shape=f32(3, blocks, lanes),
        in_specs=[spec(smem)] * 2 + [spec(pl.ANY)] + [spec(vmem)] * 2,
        out_specs=spec(vmem),
        scratch_shapes=fields(10, force_halves)
        + [acc_first, tiles_of(blocks), turned, columns_scratch, pltpu.SemaphoreType.DMA],
        compiler_params=params(grant_mib),
        cost_estimate=cost(80_000_000),
        name="own_force",
    )(self_items, own_items, force_columns, force_table, pressed)

    acceleration = pl.pallas_call(
        functools.partial(far_force_kernel, blocks, faces, per_peer),
        out_shape=f32(3, blocks, lanes),
        in_specs=[spec(smem)] + [spec(pl.ANY)] * 4 + [spec(vmem)] * 3 + [spec(smem)] + [spec(pl.ANY)] * 6,
        out_specs=spec(vmem),
        scratch_shapes=[
            vmem((3, blocks, lanes), jnp.float32),
            tiles_of(blocks),
            tiles_of(others),
            vmem((others, lanes), jnp.float32),
            vmem((others, lanes), jnp.float32),
        ]
        + fields(10, force_halves)
        + [acc_first, turned, columns_scratch, pltpu.SemaphoreType.DMA((4,))]
        + [
            tiles_of(blocks),
            vmem((blocks, lanes), jnp.float32),
            vmem((3, blocks, lanes), jnp.float32),
            vmem((4, blocks, lanes), jnp.float32),
            vmem((4, blocks, lanes), jnp.float32),
            vmem((3, blocks, lanes), jnp.float32),
            pltpu.SemaphoreType.DMA((6,)),
        ],
        compiler_params=params(grant_mib),
        cost_estimate=cost(100_000_000),
        name="far_force",
    )(
        far_items,
        force_columns,
        low,
        high,
        far,
        force_below,
        force_above,
        force_far,
        send,
        table,
        density,
        slopes,
        local_sum,
        far_sum,
        own_force,
    )

    return (density, acceleration)


def solution(mesh):
    placed = (
        P(None, ("slab", "tile"), None),
        P(None, ("slab", "tile"), None),
        P(("slab", "tile"), None),
        P(("slab", "tile"), None),
        P(None, ("slab", "tile"), None),
        P(("slab", "tile")),
        P(("slab", "tile")),
        P(("slab", "tile"), None, None),
        P(("slab", "tile"), None),
        P(("slab", "tile"), None),
        P(("slab", "tile")),
    )
    return jax.shard_map(
        on_device,
        mesh=mesh,
        in_specs=placed,
        out_specs=(P(("slab", "tile"), None), P(None, ("slab", "tile"), None)),
        check_vma=False,
    )
```
